512 devices in a mesh: step: 32 (over z, core), seq: 16 (over y, x).
Axes of the slice: x: 4, y: 4, z: 16, core: 2. Of those that a mesh axis runs over, the one named last changes fastest.
Arguments:
- start_latent: float32 [1024, 64], P('seq')
- timesteps: int32 [33], replicated, may hold values from 213 to 949, as said below
- modulation: bfloat16 [32, 3072], P('step'), may hold values from -3 to 3
- w_in: bfloat16 [64, 1536], replicated, may hold values from -0.75 to 0.75
- w_qkv: bfloat16 [1536, 3072], P('step')
- w_o: bfloat16 [1024, 1536], P('step'), may hold values from -0.1875 to 0.1875
- w_out: bfloat16 [1536, 64], replicated, may hold values from -0.15625 to 0.15625
Outputs:
- window_latents: float32 [32, 1024, 64], P('step', 'seq')
- errors: float32 [32], P('step')
The draws below stay inside these ranges and needn't reach their ends.
Inputs may be any that keep to these rules, and one draw needn't show every extreme that they name: timesteps starts at 949 and falls by 6 to 23 from each entry to the next.
All inputs are finite; a program needn't handle non-finite values.
Results may differ from the reference program's by a relative error of at most 0.0017.
Values may be sent and summed in bfloat16 or wider, within the bound.
No kernel may reach another device: no remote copies, remote signals or barrier semaphores. Data moves between devices by JAX's collectives and lax.ppermute only.
A program may use at most 64 MiB of HBM per device.

```python
import math
import jax
import jax.numpy as jnp
from jax import lax

D = 1536
HEADS = 8
HEAD_DIM = 128
C = 64
SWEEPS = 2
INNER = 1024
STEPS = 32
TOKENS = 1024


def draw_start_latent(key, part):
    key = jax.random.fold_in(key, 11)
    key_base, key_spread = jax.random.split(key, 2)
    position = jnp.arange(TOKENS, dtype=jnp.float32) / TOKENS
    spread = jnp.exp(jax.random.uniform(key_spread, (TOKENS, 1), minval=-1.15, maxval=1.15))
    trend = 0.5 + position[:, None]
    base = jax.random.normal(key_base, (TOKENS, C))
    return (base * spread * trend).astype(jnp.float32)


def draw_timesteps(key, part):
    key = jax.random.fold_in(key, 37)
    gaps = jax.random.randint(key, (STEPS,), 6, 24)
    first = jnp.full((1,), 949, jnp.int32)
    later = 949 - jnp.cumsum(gaps)
    return jnp.concatenate([first, later.astype(jnp.int32)]).astype(jnp.int32)


def draw_w_qkv(key, part):
    key = jax.random.fold_in(key, 23)
    key_q, key_k, key_v = jax.random.split(key, 3)
    factor = D ** (-0.5)
    query = jax.random.normal(key_q, (D, INNER)) * factor
    values = jax.random.normal(key_v, (D, INNER)) * factor
    keys = jax.random.normal(key_k, (D, INNER)) * factor
    return jnp.concatenate([query, keys, values], axis=1).astype(jnp.bfloat16)


def level_of(stream_key, extent, cuts, least, high):
    level, own = 1.0, jax.random.fold_in(stream_key, 6)
    for axis_at, shards_of in cuts:
        draws = jnp.exp(jax.random.uniform(jax.random.fold_in(own, axis_at), (shards_of,), jnp.float32, least / len(cuts), high / len(cuts)))
        level = level * jnp.repeat(draws, extent[axis_at] // shards_of).reshape([-1 if axis == axis_at else 1 for axis in range(len(extent))])
    return level


def scatter_about(stream_key, shape, scale, bound, cuts=(), kind=jnp.bfloat16):
    entries = jax.random.normal(stream_key, shape, jnp.float32) * scale
    if len(cuts) > 0:
        entries = level_of(stream_key, shape, cuts, -0.22, 0.18) * entries
    return jnp.clip(entries, min=-bound, max=bound).astype(kind)


def setup_inputs(seed: int = 0) -> dict:
    key_of = jax.random.split(jax.random.key(seed), 8)
    return {
        "start_latent": draw_start_latent(jax.random.fold_in(key_of[7], 71), 0),
        "timesteps": draw_timesteps(jax.random.fold_in(key_of[7], 71), 0),
        "modulation": scatter_about(key_of[2], (STEPS, 2 * D), 0.5, 3.0, ((0, 32),)),
        "w_in": scatter_about(key_of[3], (C, D), C ** -0.5, 0.75),
        "w_qkv": draw_w_qkv(jax.random.fold_in(key_of[7], 71), 0),
        "w_o": scatter_about(key_of[5], (INNER, D), INNER ** -0.5, 0.1875, ((0, 32),)),
        "w_out": scatter_about(key_of[6], (D, C), D ** -0.5, 0.15625),
    }


def alpha_bar(steps_in):
    angle = (steps_in.astype(jnp.float32) / 1000.0 + 0.008) / 1.008 * (math.pi / 2)
    return jnp.cos(angle) ** 2

def layer_norm(values):
    center = values - lax.optimization_barrier(jnp.mean(values, axis=-1, keepdims=True))
    spread = lax.optimization_barrier(jnp.mean(center * center, axis=-1, keepdims=True))
    return center * lax.rsqrt(spread + 1e-06)

def predict(latent, mod_row, w_in, w_qkv, w_o, w_out):
    rows = latent.shape[0]
    embed = jnp.dot(latent.astype(jnp.bfloat16), w_in, preferred_element_type=jnp.float32)
    shift = mod_row[:D].astype(jnp.float32)
    gain = mod_row[D:].astype(jnp.float32)
    hidden = (layer_norm(embed) * (1.0 + gain) + shift).astype(jnp.bfloat16)
    qkv = jnp.dot(hidden, w_qkv, preferred_element_type=jnp.float32).astype(jnp.bfloat16)
    query = qkv[:, :INNER].reshape(rows, HEADS, HEAD_DIM).astype(jnp.float32)
    keys = qkv[:, INNER:2 * INNER].reshape(rows, HEADS, HEAD_DIM).astype(jnp.float32)
    values = qkv[:, 2 * INNER:].reshape(rows, HEADS, HEAD_DIM).astype(jnp.float32)
    scores = jnp.einsum('qhd,khd->hqk', query, keys) / math.sqrt(HEAD_DIM)
    top = lax.optimization_barrier(jnp.max(scores, axis=-1, keepdims=True))
    weights = jnp.exp(scores - top)
    total = lax.optimization_barrier(jnp.sum(weights, axis=-1))
    rounded = weights.astype(jnp.bfloat16).astype(jnp.float32)
    mixed = jnp.einsum('hqk,khd->qhd', rounded, values)
    heads = (mixed / jnp.transpose(total)[:, :, None]).astype(jnp.bfloat16).reshape(rows, INNER)
    attended = jnp.dot(heads, w_o, preferred_element_type=jnp.float32)
    resid = (embed + attended).astype(jnp.bfloat16)
    return jnp.dot(resid, w_out, preferred_element_type=jnp.float32)

def reference(start_latent, timesteps, modulation, w_in, w_qkv, w_o, w_out):
    abar = alpha_bar(timesteps)
    keep = jnp.sqrt(abar[1:] / abar[:-1])
    noise = jnp.sqrt(1.0 - abar[1:]) - keep * jnp.sqrt(1.0 - abar[:-1])
    latents = jnp.broadcast_to(start_latent[None], (STEPS,) + start_latent.shape).astype(jnp.float32)

    def one_step(pair):
        return predict(pair[0], pair[1], w_in, w_qkv, w_o, w_out)
    previous = latents
    for sweep in range(SWEEPS):
        eps = lax.map(one_step, (latents, modulation))
        drift = (keep - 1.0)[:, None, None] * latents + noise[:, None, None] * eps
        term = drift.at[0].add(latents[0])
        prefix = jnp.cumsum(term, axis=0)
        fresh = jnp.concatenate([latents[:1], prefix[:-1]], axis=0)
        previous, latents = (latents, fresh)
    change = latents - previous
    errors = jnp.sqrt(lax.optimization_barrier(jnp.mean(change * change, axis=(1, 2))) + 1e-06)
    return (latents, errors)
```

```python
import math

import jax
import jax.numpy as jnp
from jax import lax
from jax.experimental import pallas as pl
from jax.experimental.pallas import tpu as pltpu
from jax.sharding import Mesh
from jax.sharding import PartitionSpec as P

D = 1536
HEADS = 8
HEAD_DIM = 128
C = 64
INNER = 1024
STEPS = 32
TOKENS = 1024
Z = 16
PEERS = 32
ROWS = 48
FLAT = ("core", "y", "x")
BF = jnp.bfloat16
F32 = jnp.float32
NT = (((1,), (1,)), ((), ()))
SCALE = 1.0 / (math.sqrt(HEAD_DIM) * math.log(2.0))


def place():
    return lax.axis_index("z"), lax.axis_index("core"), lax.axis_index("y") * 4 + lax.axis_index("x")


def lanes(shape):
    return lax.broadcasted_iota(jnp.int32, shape, len(shape) - 1)


def rows(shape):
    return lax.broadcasted_iota(jnp.int32, shape, 0)


def dot(a, b):
    return jnp.dot(a, b, preferred_element_type=F32)


def unpack(packed):
    low = lanes(packed.shape) < C
    return jnp.concatenate([jnp.where(low, packed, 0.0), jnp.where(low, pltpu.roll(packed, C, 1), 0.0)], axis=0)


def pack_high(values):
    half = values.shape[0] // 2
    low = lanes((half, 2 * C)) < C
    return jnp.where(low, pltpu.roll(values[:half], C, 1), values[half:])


def split_of(values, count):
    pieces = []
    for _ in range(count):
        piece = values.astype(BF)
        pieces.append(piece)
        values = values - piece.astype(F32)
    return pieces


def call(kernel, outs, args, scratch=(), smem=()):
    return pl.pallas_call(
        kernel,
        out_shape=outs,
        in_specs=[pl.BlockSpec(memory_space=pltpu.SMEM if at in smem else pltpu.VMEM) for at in range(len(args))],
        out_specs=jax.tree.map(lambda _: pl.BlockSpec(memory_space=pltpu.VMEM), outs),
        scratch_shapes=scratch,
        compiler_params=pltpu.CompilerParams(vmem_limit_bytes=40 * 1024 * 1024),
    )(*args)


def shape(dims, kind):
    return jax.ShapeDtypeStruct(dims, kind)


def send_weights(w_qkv, w_o, w_out, out):
    _, _, seq = place()
    odd = lax.rem(seq, 2) == 1

    def columns(base):
        start = pl.multiple_of(base + (seq // 2) * HEAD_DIM, HEAD_DIM)
        block = w_qkv[:, pl.ds(start, HEAD_DIM)].astype(F32)
        return jnp.where(odd, block[:, C:], block[:, :C])

    head = dot(w_o[...], w_out[...])
    head = jnp.concatenate([head, jnp.zeros((ROWS - head.shape[0], C), F32)], axis=0)
    first = jnp.concatenate([columns(0), columns(INNER)], axis=1).astype(BF)
    second = jnp.concatenate([columns(2 * INNER), head], axis=1).astype(BF)
    for to in range(Z):
        out[to, 0:ROWS, :] = first
        out[to, ROWS : 2 * ROWS, :] = second


def make_tables(own, peer, w_in, w_out, modulation, start, out, table, left, qk, vw):
    _, core, seq = place()
    for z in range(Z):
        for source, parity in ((own, core), (peer, 1 - core)):
            at = pl.ds(pl.multiple_of(z * 2 * ROWS + parity * ROWS, 16), ROWS)
            qk[at, :] = source[z, 0:ROWS, :]
            vw[at, :] = source[z, ROWS : 2 * ROWS, :]
    w = w_in[...].astype(F32)
    centred = w - jnp.mean(w, axis=1, keepdims=True)
    shift = modulation[:, 0:D].astype(F32)
    gain = modulation[:, D : 2 * D].astype(F32)
    left[0:C, :] = (centred * (1.0 + gain)).astype(BF)
    left[C : C + 16, :] = jnp.where(rows((16, D)) == 0, shift, 0.0).astype(BF)
    first = dot(left[...], qk[...])
    value = dot(left[...], vw[...])[:, :C]
    query, key = first[:, :C], first[:, C:]
    mine = own[seq, ROWS : ROWS + 32, C:].astype(F32)
    other = peer[seq, ROWS : ROWS + 32, C:].astype(F32)
    even = core == 0
    head = jnp.concatenate([jnp.where(even, mine, other), jnp.where(even, other, mine)], axis=0)
    best = lax.Precision.HIGHEST
    a = lax.dot_general(query, key, NT, precision=best, preferred_element_type=F32) * SCALE
    b = jnp.dot(value, head, precision=best, preferred_element_type=F32)
    bias = lax.dot_general(key[C : C + 8], query, NT, precision=best, preferred_element_type=F32) * SCALE
    bias = jnp.concatenate([bias, jnp.zeros((8, 128 - bias.shape[1]), F32)], axis=1)[0:1]
    main = jnp.concatenate([a[:, :C], b], axis=1)
    main = jnp.where(rows(main.shape) == C + 1, bias, main).astype(BF)
    x = start[pl.ds(pl.multiple_of(core * 32, 32), 32), :]
    x = jnp.concatenate([x[:16], x[16:]], axis=1).astype(BF)
    for to in range(PEERS):
        out[to, 0:80, :] = main
        out[to, 80:96, :] = x
    gram = lax.dot_general(centred, centred, NT, precision=best, preferred_element_type=F32) / D
    direct = dot(w_in[...], w_out[...])
    pad = jnp.zeros((C, C), F32)
    below = jnp.zeros((C, 2 * C), BF)
    gram = jnp.concatenate([gram, pad], axis=1)
    direct = jnp.concatenate([pad, direct], axis=1)
    for at, piece in enumerate(split_of(gram, 3) + split_of(direct, 2)):
        table[at, 0:C, :] = piece
        table[at, C : 2 * C, :] = below


def normalized(x, table):
    exact = x.astype(BF)
    y = dot(exact, table[0]) + dot(exact, table[1]) + dot(exact, table[2])
    spread = jnp.sum(x * y, axis=1, keepdims=True)
    return jnp.where(lanes(x.shape) == C, 1.0, x * lax.rsqrt(spread + 1e-06))


def attend(steps, heads, table, x, work):
    query_ref, key_ref, weight_ref, mixed_ref, direct_ref = work
    count = x.shape[0]
    span = HEADS * count
    mine = normalized(x, table)
    short = mine.astype(BF)
    lane = lanes((count, 128))
    exact = x.astype(BF)
    direct_ref[...] = dot(exact, table[3]) + dot(exact, table[4])
    results = []
    for step in steps:
        for head in range(HEADS):
            both = heads[step * HEADS + head]
            grown = dot(short, both)
            constant = jnp.sum(mine * both[C : C + 16].astype(F32)[1:2], axis=1, keepdims=True)
            grown = jnp.where(lane < C, grown, jnp.where(lane == C, constant, 0.0)).astype(BF)
            query_ref[step, head * count : (head + 1) * count, :] = grown
        scores = lax.dot_general(query_ref[step], key_ref[...], NT, preferred_element_type=F32)
        weight_ref[step] = jnp.exp2(scores - jnp.max(scores, axis=1, keepdims=True)).astype(BF)
        mixed = dot(weight_ref[step], key_ref[...])
        mixed_ref[step] = (mixed / mixed[:, C : C + 1]).astype(BF)
        eps = jnp.zeros((count, 128), F32)
        for head in range(HEADS):
            eps = eps + dot(mixed_ref[step, head * count : (head + 1) * count, :], heads[step * HEADS + head])
        results.append(pack_high(eps + direct_ref[...]))
    return results


def work_space():
    return (
        pltpu.VMEM((2, HEADS * 32, 128), BF),
        pltpu.VMEM((TOKENS, 128), BF),
        pltpu.VMEM((2, HEADS * 32, TOKENS), BF),
        pltpu.VMEM((2, HEADS * 32, 128), BF),
        pltpu.VMEM((32, 128), F32),
    )


def first_sweep(coef, got, start, table, heads, first_eps, out, *work):
    _, core, _ = place()
    for at in range(2 * HEADS):
        source = 2 * at
        both = got[source, 0:80, :].astype(F32) + got[source + 1, 0:80, :].astype(F32)
        heads[at, 0:80, :] = both.astype(BF)
        heads[at, 80:128, :] = jnp.zeros((48, 128), BF)
    x = start[pl.ds(pl.multiple_of(core * 32, 32), 32), :].astype(BF).astype(F32)
    x = jnp.concatenate([x, jnp.zeros_like(x)], axis=1)
    everything = got[:, 80:96, :].astype(F32).reshape(PEERS * 16, 128)
    work[1][...] = normalized(unpack(everything), table).astype(BF)
    eps = attend((0, 1), heads, table, x, work)
    first_eps[...] = eps[0]
    both = (coef[2] * eps[0] + coef[3] * eps[1]).astype(BF)
    for to in range(Z):
        out[to] = both


def packed_start(start, core):
    x = start[pl.ds(pl.multiple_of(core * 32, 32), 32), :]
    return jnp.concatenate([x[:16], x[16:]], axis=1)


def below(got, z):
    total = jnp.zeros((16, 128), F32)
    for at in range(Z):
        total = total + jnp.where(at < z, got[at].astype(F32), 0.0)
    return total


def first_prefix(coef, got, start, first_eps, latents, out):
    z, core, _ = place()
    x = packed_start(start, core)
    even = x + coef[4] * x + below(got, z)
    odd = even + coef[0] * x + coef[2] * first_eps[...]
    latents[0] = even
    latents[1] = odd
    for to in range(PEERS):
        out[to, 0:16, :] = even.astype(BF)
        out[to, 16:32, :] = odd.astype(BF)


def second_sweep(coef, got, latents, table, heads, term, out, *work):
    terms = []
    for step in range(2):
        everything = got[:, 16 * step : 16 * step + 16, :].astype(F32).reshape(PEERS * 16, 128)
        work[1][...] = normalized(unpack(everything), table).astype(BF)
        latent = latents[step]
        x = unpack(latent.astype(BF).astype(F32))
        eps = attend((step,), heads, table, x, work)[0]
        terms.append(coef[step] * latent + coef[2 + step] * eps)
    term[...] = terms[0]
    both = terms[0] + terms[1]
    for to in range(Z):
        out[to] = both


def second_prefix(got, start, latents, term, out):
    z, core, _ = place()
    even = packed_start(start, core) + below(got, z)
    fresh = (even, even + term[...])
    for step in range(2):
        change = fresh[step] - latents[step]
        squared = change * change
        squared = squared[:8] + squared[8:]
        for to in range(PEERS // 2):
            out[step * 16 + to, 0:16, :] = fresh[step]
            out[step * 16 + to, 16:24, :] = squared


def finish(got, window, errors):
    _, _, seq = place()
    for half in range(2):
        packed = got[half * 16 + seq, 0:16, :]
        window[0, half * 32 : half * 32 + 16, :] = packed[:, :C]
        window[0, half * 32 + 16 : half * 32 + 32, :] = packed[:, C:]
    total = got[0, 16:24, :]
    for at in range(1, PEERS):
        total = total + got[at, 16:24, :]
    total = jnp.sum(total, axis=(0, 1), keepdims=True)
    errors[...] = jnp.sqrt(total / (TOKENS * C) + 1e-06)


def alpha_bar(steps_in):
    angle = (steps_in.astype(jnp.float32) / 1000.0 + 0.008) / 1.008 * (math.pi / 2)
    return jnp.cos(angle) ** 2


def coefficients(timesteps):
    z = lax.axis_index("z")
    abar = alpha_bar(timesteps)
    keep = jnp.sqrt(abar[1:] / abar[:-1])
    noise = jnp.sqrt(1.0 - abar[1:]) - keep * jnp.sqrt(1.0 - abar[:-1])
    before = jnp.sum(jnp.where(jnp.arange(STEPS) < 2 * z, keep - 1.0, 0.0))
    pair = lax.dynamic_slice_in_dim(jnp.stack([keep - 1.0, noise]), 2 * z, 2, axis=1)
    return jnp.concatenate([pair.reshape(4), before[None], jnp.zeros((3,), F32)])


def body(start, timesteps, modulation, w_in, w_qkv, w_o, w_out):
    coef = coefficients(timesteps)
    sent = call(send_weights, shape((Z, 96, 128), BF), (w_qkv, w_o, w_out))
    own = lax.all_to_all(sent, "z", 0, 0, tiled=True)
    peer = lax.ppermute(own, "core", [(0, 1), (1, 0)])
    sent, table = call(
        make_tables,
        (shape((PEERS, 96, 128), BF), shape((5, 128, 128), BF)),
        (own, peer, w_in, w_out, modulation, start),
        scratch=(pltpu.VMEM((80, D), BF), pltpu.VMEM((D, 128), BF), pltpu.VMEM((D, 128), BF)),
    )
    got = lax.all_to_all(sent, FLAT, 0, 0, tiled=True)
    heads, first_eps, sent = call(
        first_sweep,
        (shape((2 * HEADS, 128, 128), BF), shape((16, 128), F32), shape((Z, 16, 128), BF)),
        (coef, got, start, table),
        scratch=work_space(),
        smem=(0,),
    )
    got = lax.all_to_all(sent, "z", 0, 0, tiled=True)
    latents, sent = call(
        first_prefix, (shape((2, 16, 128), F32), shape((PEERS, 32, 128), BF)), (coef, got, start, first_eps), smem=(0,)
    )
    got = lax.all_to_all(sent, FLAT, 0, 0, tiled=True)
    term, sent = call(
        second_sweep, (shape((16, 128), F32), shape((Z, 16, 128), F32)), (coef, got, latents, table, heads), work_space(), (0,)
    )
    got = lax.all_to_all(sent, "z", 0, 0, tiled=True)
    sent = call(second_prefix, shape((PEERS, 24, 128), F32), (got, start, latents, term))
    got = lax.all_to_all(sent, FLAT, 0, 0, tiled=True)
    window, errors = call(finish, (shape((1, 64, C), F32), shape((1, 1), F32)), (got,))
    return window, errors.reshape(1)


def solution(mesh):
    fine = Mesh(mesh.devices.reshape(Z, 2, 4, 4), ("z", "core", "y", "x"))
    step, seq = ("z", "core"), ("y", "x")
    return jax.shard_map(
        body,
        mesh=fine,
        in_specs=(P(seq, None), P(), P(step, None), P(), P(step, None), P(step, None), P()),
        out_specs=(P(step, seq, None), P(step)),
        check_vma=False,
    )
```

```python
import math

import jax
import jax.numpy as jnp
from jax import lax
from jax.experimental import pallas as pl
from jax.experimental.pallas import tpu as pltpu
from jax.sharding import Mesh
from jax.sharding import PartitionSpec as P

D = 1536
HEADS = 8
HEAD_DIM = 128
C = 64
INNER = 1024
STEPS = 32
TOKENS = 1024
Z = 16
PEERS = 32
ROWS = 48
FLAT = ("core", "y", "x")
BF = jnp.bfloat16
F32 = jnp.float32
NT = (((1,), (1,)), ((), ()))
BEST = lax.Precision.HIGHEST
SCALE = 1.0 / (math.sqrt(HEAD_DIM) * math.log(2.0))


def place():
    return lax.axis_index("z"), lax.axis_index("core"), lax.axis_index("y") * 4 + lax.axis_index("x")


def lanes(shape):
    return lax.broadcasted_iota(jnp.int32, shape, len(shape) - 1)


def rows(shape):
    return lax.broadcasted_iota(jnp.int32, shape, 0)


def dot(a, b):
    return jnp.dot(a, b, preferred_element_type=F32)


def unpack(packed):
    low = lanes(packed.shape) < C
    return jnp.concatenate([jnp.where(low, packed, 0.0), jnp.where(low, pltpu.roll(packed, C, 1), 0.0)], axis=0)


def pack_high(values):
    half = values.shape[0] // 2
    low = lanes((half, 2 * C)) < C
    return jnp.where(low, pltpu.roll(values[:half], C, 1), values[half:])


def split_of(values, count):
    pieces = []
    for _ in range(count):
        piece = values.astype(BF)
        pieces.append(piece)
        values = values - piece.astype(F32)
    return pieces


def call(kernel, outs, args, scratch=(), smem=()):
    return pl.pallas_call(
        kernel,
        out_shape=outs,
        in_specs=[pl.BlockSpec(memory_space=pltpu.SMEM if at in smem else pltpu.VMEM) for at in range(len(args))],
        out_specs=jax.tree.map(lambda _: pl.BlockSpec(memory_space=pltpu.VMEM), outs),
        scratch_shapes=scratch,
        compiler_params=pltpu.CompilerParams(vmem_limit_bytes=40 * 1024 * 1024),
    )(*args)


def shape(dims, kind):
    return jax.ShapeDtypeStruct(dims, kind)


def send_weights(w_qkv, w_o, w_out, out):
    _, _, seq = place()
    odd = lax.rem(seq, 2) == 1

    def columns(base):
        start = pl.multiple_of(base + (seq // 2) * HEAD_DIM, HEAD_DIM)
        block = w_qkv[:, pl.ds(start, HEAD_DIM)].astype(F32)
        return jnp.where(odd, block[:, C:], block[:, :C])

    head = lax.dot_general(w_o[...], w_out[...], NT, preferred_element_type=F32)
    head = jnp.concatenate([head, jnp.zeros((ROWS - head.shape[0], C), F32)], axis=0)
    first = jnp.concatenate([columns(0), columns(INNER)], axis=1).astype(BF)
    second = jnp.concatenate([columns(2 * INNER), head], axis=1).astype(BF)
    for to in range(Z):
        out[to, 0:ROWS, :] = first
        out[to, ROWS : 2 * ROWS, :] = second


def make_tables(w_in, w_out, modulation, left, table):
    w = w_in[...].astype(F32)
    centred = w - jnp.mean(w, axis=1, keepdims=True)
    shift = modulation[:, 0:D].astype(F32)
    gain = modulation[:, D : 2 * D].astype(F32)
    left[0:C, :] = (centred * (1.0 + gain)).astype(BF)
    left[C : C + 16, :] = jnp.where(rows((16, D)) == 0, shift, 0.0).astype(BF)
    gram = lax.dot_general(centred, centred, NT, precision=BEST, preferred_element_type=F32) / D
    direct = lax.dot_general(w_in[...], w_out[...], NT, preferred_element_type=F32)
    pad = jnp.zeros((C, C), F32)
    gram = jnp.concatenate([gram, pad], axis=1)
    direct = jnp.concatenate([pad, direct], axis=1)
    for at, piece in enumerate(split_of(gram, 3) + split_of(direct, 2)):
        table[at, 0:C, :] = piece
        table[at, C : 2 * C, :] = jnp.zeros((C, 2 * C), BF)


def make_heads(both, left, start, out, qk, vw):
    _, core, seq = place()
    for z in range(Z):
        for parity in range(2):
            at = pl.ds((z * 2 + parity) * ROWS, ROWS)
            qk[at, :] = both[parity, z, 0:ROWS, :]
            vw[at, :] = both[parity, z, ROWS : 2 * ROWS, :]
    first = dot(left[...], qk[...])
    value = dot(left[...], vw[...])[:, :C]
    query, key = first[:, :C], first[:, C:]
    head = both[:, seq, ROWS : ROWS + 32, C:].astype(F32).reshape(C, C)
    a = lax.dot_general(query, key, NT, precision=BEST, preferred_element_type=F32) * SCALE
    b = jnp.dot(value, head, precision=BEST, preferred_element_type=F32)
    bias = lax.dot_general(key[C : C + 8], query, NT, precision=BEST, preferred_element_type=F32) * SCALE
    bias = jnp.concatenate([bias, jnp.zeros((8, 128 - bias.shape[1]), F32)], axis=1)[0:1]
    main = jnp.concatenate([a[:, :C], b], axis=1)
    main = jnp.where(rows(main.shape) == C + 1, bias, main).astype(BF)
    x = packed_start(start, core).astype(BF)
    for to in range(PEERS // 2):
        out[to, 0:80, :] = main
        out[to, 80:96, :] = x


def normalized(x, table):
    exact = x.astype(BF)
    y = dot(exact, table[0]) + dot(exact, table[1]) + dot(exact, table[2])
    spread = jnp.sum(x * y, axis=1, keepdims=True)
    return jnp.where(lanes(x.shape) == C, 1.0, x * lax.rsqrt(spread + 1e-06))


def attend(steps, heads, table, x, work):
    query_ref, key_ref, weight_ref, mixed_ref, direct_ref = work
    count = x.shape[0]
    span = HEADS * count
    mine = normalized(x, table)
    short = mine.astype(BF)
    lane = lanes((count, 128))
    exact = x.astype(BF)
    direct_ref[...] = dot(exact, table[3]) + dot(exact, table[4])
    results = []
    for step in steps:
        for head in range(HEADS):
            both = heads[step * HEADS + head]
            grown = dot(short, both)
            constant = jnp.sum(mine * both[C : C + 16].astype(F32)[1:2], axis=1, keepdims=True)
            grown = jnp.where(lane < C, grown, jnp.where(lane == C, constant, 0.0)).astype(BF)
            query_ref[step, head * count : (head + 1) * count, :] = grown
        scores = lax.dot_general(query_ref[step], key_ref[...], NT, preferred_element_type=F32)
        weight_ref[step] = jnp.exp2(scores - jnp.max(scores, axis=1, keepdims=True)).astype(BF)
        mixed = dot(weight_ref[step], key_ref[...])
        mixed_ref[step] = (mixed / mixed[:, C : C + 1]).astype(BF)
        eps = jnp.zeros((count, 128), F32)
        for head in range(HEADS):
            eps = eps + dot(mixed_ref[step, head * count : (head + 1) * count, :], heads[step * HEADS + head])
        results.append(pack_high(eps + direct_ref[...]))
    return results


def work_space():
    return (
        pltpu.VMEM((2, HEADS * 32, 128), BF),
        pltpu.VMEM((TOKENS, 128), BF),
        pltpu.VMEM((2, HEADS * 32, TOKENS), BF),
        pltpu.VMEM((2, HEADS * 32, 128), BF),
        pltpu.VMEM((32, 128), F32),
    )


def first_sweep(coef, got, start, table, heads, first_eps, out, *work):
    _, core, _ = place()
    for at in range(2 * HEADS):
        step, source = at // HEADS, 2 * (at % HEADS)
        both = got[step, source, 0:80, :].astype(F32) + got[step, source + 1, 0:80, :].astype(F32)
        heads[at, 0:80, :] = both.astype(BF)
        heads[at, 80:128, :] = jnp.zeros((48, 128), BF)
    x = start[pl.ds(pl.multiple_of(core * 32, 32), 32), :].astype(BF).astype(F32)
    x = jnp.concatenate([x, jnp.zeros_like(x)], axis=1)
    everything = got[:, :, 80:96, :].astype(F32).reshape(PEERS * 16, 128)
    work[1][...] = normalized(unpack(everything), table).astype(BF)
    eps = attend((0, 1), heads, table, x, work)
    first_eps[...] = eps[0]
    both = (coef[2] * eps[0] + coef[3] * eps[1]).astype(BF)
    for to in range(Z):
        out[to] = both


def packed_start(start, core):
    x = start[pl.ds(pl.multiple_of(core * 32, 32), 32), :]
    return jnp.concatenate([x[:16], x[16:]], axis=1)


def below(got, z):
    total = jnp.zeros((16, 128), F32)
    for at in range(Z):
        total = total + jnp.where(at < z, got[at].astype(F32), 0.0)
    return total


def first_prefix(coef, got, start, first_eps, latents, out):
    z, core, _ = place()
    x = packed_start(start, core)
    even = x + coef[4] * x + below(got, z)
    odd = even + coef[0] * x + coef[2] * first_eps[...]
    latents[0] = even
    latents[1] = odd
    for to in range(PEERS):
        out[to, 0:16, :] = even.astype(BF)
        out[to, 16:32, :] = odd.astype(BF)


def second_sweep(coef, got, latents, table, heads, term, out, *work):
    terms = []
    for step in range(2):
        everything = got[:, 16 * step : 16 * step + 16, :].astype(F32).reshape(PEERS * 16, 128)
        work[1][...] = normalized(unpack(everything), table).astype(BF)
        latent = latents[step]
        x = unpack(latent.astype(BF).astype(F32))
        eps = attend((step,), heads, table, x, work)[0]
        terms.append(coef[step] * latent + coef[2 + step] * eps)
    term[...] = terms[0]
    both = terms[0] + terms[1]
    for to in range(Z):
        out[to] = both


def second_prefix(got, start, latents, term, fresh, out):
    z, core, _ = place()
    even = packed_start(start, core) + below(got, z)
    fresh[0] = even
    fresh[1] = even + term[...]
    for step in range(2):
        change = fresh[step] - latents[step]
        squared = change * change
        squared = squared[:8] + squared[8:]
        for to in range(PEERS // 2):
            out[step * 16 + to] = squared


def finish(got, halves, window, errors):
    _, core, _ = place()
    for half in range(2):
        packed = halves[half, core]
        window[0, half * 32 : half * 32 + 16, :] = packed[:, :C]
        window[0, half * 32 + 16 : half * 32 + 32, :] = packed[:, C:]
    total = got[0]
    for at in range(1, PEERS):
        total = total + got[at]
    total = jnp.sum(total, axis=(0, 1), keepdims=True)
    errors[...] = jnp.sqrt(total / (TOKENS * C) + 1e-06)


def alpha_bar(steps_in):
    angle = (steps_in.astype(jnp.float32) / 1000.0 + 0.008) / 1.008 * (math.pi / 2)
    return jnp.cos(angle) ** 2


def coefficients(timesteps):
    z = lax.axis_index("z")
    abar = alpha_bar(timesteps)
    keep = jnp.sqrt(abar[1:] / abar[:-1])
    noise = jnp.sqrt(1.0 - abar[1:]) - keep * jnp.sqrt(1.0 - abar[:-1])
    before = jnp.sum(jnp.where(jnp.arange(STEPS) < 2 * z, keep - 1.0, 0.0))
    pair = lax.dynamic_slice_in_dim(jnp.stack([keep - 1.0, noise]), 2 * z, 2, axis=1)
    return jnp.concatenate([pair.reshape(4), before[None], jnp.zeros((3,), F32)])


def body(start, timesteps, modulation, w_in, w_qkv, w_o, w_out):
    coef = coefficients(timesteps)
    sent = call(send_weights, shape((Z, 96, 128), BF), (w_qkv, w_o, w_out.T))
    got = lax.all_to_all(sent, "z", 0, 0, tiled=True)
    left, table = call(make_tables, (shape((80, D), BF), shape((5, 128, 128), BF)), (w_in, w_out.T, modulation))
    sent = call(
        make_heads,
        shape((PEERS // 2, 96, 128), BF),
        (lax.all_gather(got, "core"), left, start),
        scratch=(pltpu.VMEM((D, 128), BF), pltpu.VMEM((D, 128), BF)),
    )
    got = lax.all_gather(lax.all_to_all(sent, ("y", "x"), 0, 0, tiled=True), "core")
    heads, first_eps, sent = call(
        first_sweep,
        (shape((2 * HEADS, 128, 128), BF), shape((16, 128), F32), shape((Z, 16, 128), BF)),
        (coef, got, start, table),
        scratch=work_space(),
        smem=(0,),
    )
    got = lax.all_to_all(sent, "z", 0, 0, tiled=True)
    latents, sent = call(
        first_prefix, (shape((2, 16, 128), F32), shape((PEERS, 32, 128), BF)), (coef, got, start, first_eps), smem=(0,)
    )
    got = lax.all_to_all(sent, FLAT, 0, 0, tiled=True)
    term, sent = call(
        second_sweep, (shape((16, 128), F32), shape((Z, 16, 128), F32)), (coef, got, latents, table, heads), work_space(), (0,)
    )
    got = lax.all_to_all(sent, "z", 0, 0, tiled=True)
    fresh, sent = call(
        second_prefix, (shape((2, 16, 128), F32), shape((PEERS, 8, 128), F32)), (got, start, latents, term)
    )
    got = lax.all_to_all(sent, FLAT, 0, 0, tiled=True)
    halves = lax.all_gather(fresh, "core")
    window, errors = call(finish, (shape((1, 64, C), F32), shape((1, 1), F32)), (got, halves))
    return window, errors.reshape(1)


def solution(mesh):
    fine = Mesh(mesh.devices.reshape(Z, 2, 4, 4), ("z", "core", "y", "x"))
    step, seq = ("z", "core"), ("y", "x")
    return jax.shard_map(
        body,
        mesh=fine,
        in_specs=(P(seq, None), P(), P(step, None), P(), P(step, None), P(step, None), P()),
        out_specs=(P(step, seq, None), P(step)),
        check_vma=False,
    )
```

```python
import math

import jax
import jax.numpy as jnp
from jax import lax
from jax.experimental import pallas as pl
from jax.experimental.pallas import tpu as pltpu
from jax.sharding import Mesh
from jax.sharding import PartitionSpec as P

D = 1536
HEADS = 8
HEAD_DIM = 128
C = 64
INNER = 1024
STEPS = 32
TOKENS = 1024
Z = 16
PEERS = 32
ROWS = 48
FLAT = ("core", "y", "x")
BF = jnp.bfloat16
F32 = jnp.float32
NT = (((1,), (1,)), ((), ()))
BEST = lax.Precision.HIGHEST
SCALE = 1.0 / (math.sqrt(HEAD_DIM) * math.log(2.0))


def place():
    return lax.axis_index("z"), lax.axis_index("core"), lax.axis_index("y") * 4 + lax.axis_index("x")


def lanes(shape):
    return lax.broadcasted_iota(jnp.int32, shape, len(shape) - 1)


def rows(shape):
    return lax.broadcasted_iota(jnp.int32, shape, 0)


def dot(a, b):
    return jnp.dot(a, b, preferred_element_type=F32)


def unpack(packed):
    low = lanes(packed.shape) < C
    return jnp.concatenate([jnp.where(low, packed, 0.0), jnp.where(low, pltpu.roll(packed, C, 1), 0.0)], axis=0)


def pack_high(values):
    half = values.shape[0] // 2
    low = lanes((half, 2 * C)) < C
    return jnp.where(low, pltpu.roll(values[:half], C, 1), values[half:])


def split_of(values, count):
    pieces = []
    for _ in range(count):
        piece = values.astype(BF)
        pieces.append(piece)
        values = values - piece.astype(F32)
    return pieces


def call(kernel, outs, args, scratch=(), smem=(), anywhere=(), flops=0):
    spaces = [pltpu.SMEM if at in smem else pl.ANY if at in anywhere else pltpu.VMEM for at in range(len(args))]
    return pl.pallas_call(
        kernel,
        out_shape=outs,
        in_specs=[pl.BlockSpec(memory_space=space) for space in spaces],
        out_specs=jax.tree.map(lambda _: pl.BlockSpec(memory_space=pltpu.VMEM), outs),
        scratch_shapes=scratch,
        compiler_params=pltpu.CompilerParams(vmem_limit_bytes=40 * 1024 * 1024),
        cost_estimate=pl.CostEstimate(flops=flops, bytes_accessed=0, transcendentals=0) if flops else None,
    )(*args)


def shape(dims, kind):
    return jax.ShapeDtypeStruct(dims, kind)


def send_weights(w_qkv, w_o, w_out, out, blocks, left, right, arrived):
    _, _, seq = place()
    copies = [pltpu.make_async_copy(w_o, left, arrived.at[3]), pltpu.make_async_copy(w_out, right, arrived.at[4])]
    for at in range(3):
        start = pl.multiple_of(at * INNER + (seq // 2) * HEAD_DIM, HEAD_DIM)
        copies.append(pltpu.make_async_copy(w_qkv.at[:, pl.ds(start, HEAD_DIM)], blocks.at[at], arrived.at[at]))
    for copy in copies:
        copy.start()
    for copy in copies:
        copy.wait()
    odd = lax.rem(seq, 2) == 1

    def columns(at):
        block = blocks[at].astype(F32)
        return jnp.where(odd, block[:, C:], block[:, :C])

    head = lax.dot_general(left[...], right[...], NT, preferred_element_type=F32)
    head = jnp.concatenate([head, jnp.zeros((ROWS - head.shape[0], C), F32)], axis=0)
    first = jnp.concatenate([columns(0), columns(1)], axis=1).astype(BF)
    second = jnp.concatenate([columns(2), head], axis=1).astype(BF)
    for to in range(Z):
        out[to, 0:ROWS, :] = first
        out[to, ROWS : 2 * ROWS, :] = second


def coefficients(timesteps):
    z, _, _ = place()
    lane = lanes((8, 128))
    moments = jnp.zeros((8, 128), F32)
    for at in range(STEPS + 1):
        moments = jnp.where(lane == at, timesteps[at].astype(F32), moments)
    angle = (moments / 1000.0 + 0.008) / 1.008 * (math.pi / 2)
    abar = jnp.cos(angle) ** 2
    after = pltpu.roll(abar, 127, 1)
    keep = jnp.sqrt(after / abar)
    noise = jnp.sqrt(1.0 - after) - keep * jnp.sqrt(1.0 - abar)
    less = keep - 1.0
    row = rows((8, 128))
    chosen = jnp.where(
        row < 2,
        jnp.where(lane == 2 * z + row, less, 0.0),
        jnp.where(row < 4, jnp.where(lane == 2 * z + row - 2, noise, 0.0), jnp.where(lane < 2 * z, less, 0.0)),
    )
    return jnp.broadcast_to(jnp.sum(chosen, axis=1, keepdims=True), (8, 128))


def make_tables(timesteps, w_in, w_out, modulation, left, table, coef):
    coef[...] = coefficients(timesteps)
    w = w_in[...].astype(F32)
    centred = w - jnp.mean(w, axis=1, keepdims=True)
    shift = modulation[:, 0:D].astype(F32)
    gain = modulation[:, D : 2 * D].astype(F32)
    left[0:C, :] = (centred * (1.0 + gain)).astype(BF)
    left[C : C + 16, :] = jnp.where(rows((16, D)) == 0, shift, 0.0).astype(BF)
    gram = lax.dot_general(centred, centred, NT, precision=BEST, preferred_element_type=F32) / D
    direct = lax.dot_general(w_in[...], w_out[...], NT, preferred_element_type=F32)
    pad = jnp.zeros((C, C), F32)
    gram = jnp.concatenate([gram, pad], axis=1)
    direct = jnp.concatenate([pad, direct], axis=1)
    for at, piece in enumerate(split_of(gram, 3) + split_of(direct, 2)):
        table[at, 0:C, :] = piece
        table[at, C : 2 * C, :] = jnp.zeros((C, 2 * C), BF)


def make_heads(both, left, start, out, qk, vw):
    _, core, seq = place()
    for z in range(Z):
        for parity in range(2):
            at = pl.ds((z * 2 + parity) * ROWS, ROWS)
            qk[at, :] = both[parity, z, 0:ROWS, :]
            vw[at, :] = both[parity, z, ROWS : 2 * ROWS, :]
    first = dot(left[...], qk[...])
    value = dot(left[...], vw[...])[:, :C]
    query, key = first[:, :C], first[:, C:]
    head = both[:, seq, ROWS : ROWS + 32, C:].astype(F32).reshape(C, C)
    a = lax.dot_general(query, key, NT, precision=BEST, preferred_element_type=F32) * SCALE
    b = jnp.dot(value, head, precision=BEST, preferred_element_type=F32)
    bias = lax.dot_general(key[C : C + 8], query, NT, precision=BEST, preferred_element_type=F32) * SCALE
    bias = jnp.concatenate([bias, jnp.zeros((8, 128 - bias.shape[1]), F32)], axis=1)[0:1]
    main = jnp.concatenate([a[:, :C], b], axis=1)
    main = jnp.where(rows(main.shape) == C + 1, bias, main).astype(BF)
    x = packed_start(start, core).astype(BF)
    for to in range(PEERS // 2):
        out[to, 0:80, :] = main
        out[to, 80:96, :] = x


def normalized(x, table):
    exact = x.astype(BF)
    y = dot(exact, table[0]) + dot(exact, table[1]) + dot(exact, table[2])
    spread = jnp.sum(x * y, axis=1, keepdims=True)
    return jnp.where(lanes(x.shape) == C, 1.0, x * lax.rsqrt(spread + 1e-06))


def ask(steps, heads, table, x, query, direct):
    count = x.shape[0]
    mine = normalized(x, table)
    short = mine.astype(BF)
    lane = lanes((count, 128))
    exact = x.astype(BF)
    for step in steps:
        direct[step] = dot(exact, table[3]) + dot(exact, table[4])
        for head in range(HEADS):
            both = heads[step * HEADS + head]
            grown = dot(short, both)
            constant = jnp.sum(mine * both[C : C + 16].astype(F32)[1:2], axis=1, keepdims=True)
            grown = jnp.where(lane < C, grown, jnp.where(lane == C, constant, 0.0)).astype(BF)
            query[step, head * count : (head + 1) * count, :] = grown


def attend(step, heads, query, direct, key, weight, mix):
    count = direct.shape[1]
    scores = lax.dot_general(query[step], key[...], NT, preferred_element_type=F32)
    weight[step] = jnp.exp2(scores - jnp.max(scores, axis=1, keepdims=True)).astype(BF)
    mixed = dot(weight[step], key[...])
    mix[step] = (mixed / mixed[:, C : C + 1]).astype(BF)
    eps = jnp.zeros((count, 128), F32)
    for head in range(HEADS):
        eps = eps + dot(mix[step, head * count : (head + 1) * count, :], heads[step * HEADS + head])
    return pack_high(eps + direct[step])


def work_space():
    return (
        pltpu.VMEM((TOKENS, 128), BF),
        pltpu.VMEM((2, HEADS * 32, TOKENS), BF),
        pltpu.VMEM((2, HEADS * 32, 128), BF),
    )


def first_sweep(coef, got, start, table, heads, first_eps, out, query, direct, key, weight, mix):
    _, core, _ = place()
    for at in range(2 * HEADS):
        step, source = at // HEADS, 2 * (at % HEADS)
        both = got[step, source, 0:80, :].astype(F32) + got[step, source + 1, 0:80, :].astype(F32)
        heads[at, 0:80, :] = both.astype(BF)
        heads[at, 80:128, :] = jnp.zeros((48, 128), BF)
    x = start[pl.ds(pl.multiple_of(core * 32, 32), 32), :].astype(BF).astype(F32)
    x = jnp.concatenate([x, jnp.zeros_like(x)], axis=1)
    everything = got[:, :, 80:96, :].astype(F32).reshape(PEERS * 16, 128)
    key[...] = normalized(unpack(everything), table).astype(BF)
    ask((0, 1), heads, table, x, query, direct)
    eps = [attend(step, heads, query, direct, key, weight, mix) for step in range(2)]
    first_eps[...] = eps[0]
    both = (coef[2:3] * eps[0] + coef[3:4] * eps[1]).astype(BF)
    for to in range(Z):
        out[to] = both


def packed_start(start, core):
    x = start[pl.ds(pl.multiple_of(core * 32, 32), 32), :]
    return jnp.concatenate([x[:16], x[16:]], axis=1)


def below(got, z):
    total = jnp.zeros((16, 128), F32)
    for at in range(Z):
        total = total + jnp.where(at < z, got[at].astype(F32), 0.0)
    return total


def first_prefix(coef, got, start, first_eps, latents, out):
    z, core, _ = place()
    x = packed_start(start, core)
    even = x + coef[4:5] * x + below(got, z)
    odd = even + coef[0:1] * x + coef[2:3] * first_eps[...]
    latents[0] = even
    latents[1] = odd
    for to in range(PEERS):
        out[to, 0:16, :] = even.astype(BF)
        out[to, 16:32, :] = odd.astype(BF)


def second_queries(latents, table, heads, query, direct):
    for step in range(2):
        ask((step,), heads, table, unpack(latents[step].astype(BF).astype(F32)), query, direct)


def second_sweep(coef, got, latents, table, heads, query, direct, term, out, key, weight, mix):
    terms = []
    for step in range(2):
        everything = got[:, 16 * step : 16 * step + 16, :].astype(F32).reshape(PEERS * 16, 128)
        key[...] = normalized(unpack(everything), table).astype(BF)
        eps = attend(step, heads, query, direct, key, weight, mix)
        terms.append(coef[step : step + 1] * latents[step] + coef[2 + step : 3 + step] * eps)
    term[...] = terms[0]
    both = (terms[0] + terms[1]).astype(BF)
    for to in range(Z):
        out[to] = both


def second_prefix(got, start, latents, term, fresh, out):
    z, core, _ = place()
    even = packed_start(start, core) + below(got, z)
    fresh[0] = even
    fresh[1] = even + term[...]
    for step in range(2):
        change = fresh[step] - latents[step]
        squared = change * change
        squared = squared[:8] + squared[8:]
        for to in range(PEERS // 2):
            out[step * 16 + to] = squared


def finish(got, halves, window, errors):
    _, core, _ = place()
    for half in range(2):
        packed = halves[half, core]
        window[0, half * 32 : half * 32 + 16, :] = packed[:, :C]
        window[0, half * 32 + 16 : half * 32 + 32, :] = packed[:, C:]
    total = got[0]
    for at in range(1, PEERS):
        total = total + got[at]
    total = jnp.sum(total, axis=(0, 1), keepdims=True)
    errors[...] = jnp.sqrt(total / (TOKENS * C) + 1e-06)


def body(start, timesteps, modulation, w_in, w_qkv, w_o, w_out):
    sent = call(
        send_weights,
        shape((Z, 96, 128), BF),
        (w_qkv, w_o, w_out.T),
        scratch=(
            pltpu.VMEM((3, ROWS, HEAD_DIM), BF),
            pltpu.VMEM((32, D), BF),
            pltpu.VMEM((C, D), BF),
            pltpu.SemaphoreType.DMA((5,)),
        ),
        anywhere=(0, 1, 2),
    )
    got = lax.all_to_all(sent, "z", 0, 0, tiled=True)
    left, table, coef = call(
        make_tables,
        (shape((80, D), BF), shape((5, 128, 128), BF), shape((8, 128), F32)),
        (timesteps, w_in, w_out.T, modulation),
        smem=(0,),
        flops=10**9,
    )
    sent = call(
        make_heads,
        shape((PEERS // 2, 96, 128), BF),
        (lax.all_gather(got, "core"), left, start),
        scratch=(pltpu.VMEM((D, 128), BF), pltpu.VMEM((D, 128), BF)),
    )
    got = lax.all_gather(lax.all_to_all(sent, ("y", "x"), 0, 0, tiled=True), "core")
    heads, first_eps, sent = call(
        first_sweep,
        (shape((2 * HEADS, 128, 128), BF), shape((16, 128), F32), shape((Z, 16, 128), BF)),
        (coef, got, start, table),
        scratch=(pltpu.VMEM((2, HEADS * 32, 128), BF), pltpu.VMEM((2, 32, 128), F32), *work_space()),
    )
    got = lax.all_to_all(sent, "z", 0, 0, tiled=True)
    latents, sent = call(
        first_prefix, (shape((2, 16, 128), F32), shape((PEERS, 32, 128), BF)), (coef, got, start, first_eps)
    )
    got = lax.all_to_all(sent, FLAT, 0, 0, tiled=True)
    query, direct = call(
        second_queries,
        (shape((2, HEADS * 32, 128), BF), shape((2, 32, 128), F32)),
        (latents, table, heads),
        flops=10**9,
    )
    term, sent = call(
        second_sweep,
        (shape((16, 128), F32), shape((Z, 16, 128), BF)),
        (coef, got, latents, table, heads, query, direct),
        scratch=work_space(),
    )
    got = lax.all_to_all(sent, "z", 0, 0, tiled=True)
    fresh, sent = call(
        second_prefix, (shape((2, 16, 128), F32), shape((PEERS, 8, 128), F32)), (got, start, latents, term)
    )
    got = lax.all_to_all(sent, FLAT, 0, 0, tiled=True)
    halves = lax.all_gather(fresh, "core")
    window, errors = call(finish, (shape((1, 64, C), F32), shape((1, 1), F32)), (got, halves))
    return window, errors.reshape(1)


def solution(mesh):
    fine = Mesh(mesh.devices.reshape(Z, 2, 4, 4), ("z", "core", "y", "x"))
    step, seq = ("z", "core"), ("y", "x")
    return jax.shard_map(
        body,
        mesh=fine,
        in_specs=(P(seq, None), P(), P(step, None), P(), P(step, None), P(step, None), P()),
        out_specs=(P(step, seq, None), P(step)),
        check_vma=False,
    )
```

```python
import math

import jax
import jax.numpy as jnp
from jax import lax
from jax.experimental import pallas as pl
from jax.experimental.pallas import tpu as pltpu
from jax.sharding import Mesh
from jax.sharding import PartitionSpec as P

D = 1536
HEADS = 8
HEAD_DIM = 128
C = 64
INNER = 1024
STEPS = 32
TOKENS = 1024
Z = 16
PEERS = 32
ROWS = 48
FLAT = ("core", "y", "x")
BF = jnp.bfloat16
F32 = jnp.float32
NT = (((1,), (1,)), ((), ()))
BEST = lax.Precision.HIGHEST
SCALE = 1.0 / (math.sqrt(HEAD_DIM) * math.log(2.0))


def place():
    return lax.axis_index("z"), lax.axis_index("core"), lax.axis_index("y") * 4 + lax.axis_index("x")


def lanes(shape):
    return lax.broadcasted_iota(jnp.int32, shape, len(shape) - 1)


def rows(shape):
    return lax.broadcasted_iota(jnp.int32, shape, 0)


def dot(a, b):
    return jnp.dot(a, b, preferred_element_type=F32)


def unpack(packed, after=0.0):
    lane = lanes(packed.shape)
    low = lane < C
    rest = jnp.where(lane == C, after, 0.0)
    return jnp.concatenate([jnp.where(low, packed, rest), jnp.where(low, pltpu.roll(packed, C, 1), rest)], axis=0)


def pack(values):
    half = values.shape[0] // 2
    return jnp.where(lanes((half, 2 * C)) < C, values[:half], pltpu.roll(values[half:], C, 1))


def pack_high(values):
    half = values.shape[0] // 2
    low = lanes((half, 2 * C)) < C
    return jnp.where(low, pltpu.roll(values[:half], C, 1), values[half:])


def split_of(values, count):
    pieces = []
    for _ in range(count):
        piece = values.astype(BF)
        pieces.append(piece)
        values = values - piece.astype(F32)
    return pieces


def call(kernel, outs, args, scratch=(), smem=(), far=(), flops=0):
    spaces = [pltpu.SMEM if at in smem else pltpu.HBM if at in far else pltpu.VMEM for at in range(len(args))]
    return pl.pallas_call(
        kernel,
        out_shape=outs,
        in_specs=[pl.BlockSpec(memory_space=space) for space in spaces],
        out_specs=jax.tree.map(lambda _: pl.BlockSpec(memory_space=pltpu.VMEM), outs),
        scratch_shapes=scratch,
        compiler_params=pltpu.CompilerParams(vmem_limit_bytes=40 * 1024 * 1024),
        cost_estimate=pl.CostEstimate(flops=flops, bytes_accessed=0, transcendentals=0) if flops else None,
    )(*args)


def shape(dims, kind):
    return jax.ShapeDtypeStruct(dims, kind)


def send_weights(w_qkv, w_o, w_out, out, blocks, left, right, arrived):
    _, _, seq = place()
    copies = [pltpu.make_async_copy(w_o, left, arrived.at[3]), pltpu.make_async_copy(w_out, right, arrived.at[4])]
    for at in range(3):
        start = pl.multiple_of(at * INNER + (seq // 2) * HEAD_DIM, HEAD_DIM)
        copies.append(pltpu.make_async_copy(w_qkv.at[:, pl.ds(start, HEAD_DIM)], blocks.at[at], arrived.at[at]))
    for copy in copies:
        copy.start()
    for copy in copies:
        copy.wait()
    odd = lax.rem(seq, 2) == 1

    def columns(at):
        block = blocks[at].astype(F32)
        return jnp.where(odd, block[:, C:], block[:, :C])

    head = lax.dot_general(left[...], right[...], NT, preferred_element_type=F32)
    head = jnp.concatenate([head, jnp.zeros((ROWS - head.shape[0], C), F32)], axis=0)
    first = jnp.concatenate([columns(0), columns(1)], axis=1).astype(BF)
    second = jnp.concatenate([columns(2), head], axis=1).astype(BF)
    for to in range(Z):
        out[to, 0:ROWS, :] = first
        out[to, ROWS : 2 * ROWS, :] = second


def coefficients(timesteps):
    z, _, _ = place()
    lane = lanes((8, 128))
    moments = jnp.zeros((8, 128), F32)
    for at in range(STEPS + 1):
        moments = jnp.where(lane == at, timesteps[at].astype(F32), moments)
    angle = (moments / 1000.0 + 0.008) / 1.008 * (math.pi / 2)
    abar = jnp.cos(angle) ** 2
    after = pltpu.roll(abar, 127, 1)
    keep = jnp.sqrt(after / abar)
    noise = jnp.sqrt(1.0 - after) - keep * jnp.sqrt(1.0 - abar)
    less = keep - 1.0
    row = rows((8, 128))
    chosen = jnp.where(
        row < 2,
        jnp.where(lane == 2 * z + row, less, 0.0),
        jnp.where(row < 4, jnp.where(lane == 2 * z + row - 2, noise, 0.0), jnp.where(lane < 2 * z, less, 0.0)),
    )
    return jnp.broadcast_to(jnp.sum(chosen, axis=1, keepdims=True), (8, 128))


def make_tables(timesteps, w_in, w_out, modulation, left, table, coef):
    coef[...] = coefficients(timesteps)
    w = w_in[...].astype(F32)
    centred = w - jnp.mean(w, axis=1, keepdims=True)
    shift = modulation[:, 0:D].astype(F32)
    gain = modulation[:, D : 2 * D].astype(F32)
    left[0:C, :] = (centred * (1.0 + gain)).astype(BF)
    left[C : C + 16, :] = jnp.where(rows((16, D)) == 0, shift, 0.0).astype(BF)
    gram = lax.dot_general(centred, centred, NT, precision=BEST, preferred_element_type=F32) / D
    direct = lax.dot_general(w_in[...], w_out[...], NT, preferred_element_type=F32)
    pad = jnp.zeros((C, C), F32)
    gram = jnp.concatenate([gram, pad], axis=1)
    direct = jnp.concatenate([pad, direct], axis=1)
    for at, piece in enumerate(split_of(gram, 3) + split_of(direct, 2)):
        table[at, 0:C, :] = piece
        table[at, C : 2 * C, :] = jnp.zeros((C, 2 * C), BF)


def make_heads(both, left, start, table, out, qk, vw):
    _, core, seq = place()
    for z in range(Z):
        for parity in range(2):
            at = pl.ds((z * 2 + parity) * ROWS, ROWS)
            qk[at, :] = both[parity, z, 0:ROWS, :]
            vw[at, :] = both[parity, z, ROWS : 2 * ROWS, :]
    first = dot(left[...], qk[...])
    value = dot(left[...], vw[...])[:, :C]
    query, key = first[:, :C], first[:, C:]
    head = both[:, seq, ROWS : ROWS + 32, C:].astype(F32).reshape(C, C)
    a = lax.dot_general(query, key, NT, precision=BEST, preferred_element_type=F32) * SCALE
    b = jnp.dot(value, head, precision=BEST, preferred_element_type=F32)
    bias = lax.dot_general(key[C : C + 8], query, NT, precision=BEST, preferred_element_type=F32) * SCALE
    bias = jnp.concatenate([bias, jnp.zeros((8, 128 - bias.shape[1]), F32)], axis=1)[0:1]
    main = jnp.concatenate([a[:, :C], b], axis=1)
    main = jnp.where(rows(main.shape) == C + 1, bias, main).astype(BF)
    x = pack(normalized(unpack(packed_start(start, core).astype(BF).astype(F32)), table)).astype(BF)
    for to in range(PEERS // 2):
        out[to, 0:80, :] = main
        out[to, 80:96, :] = x


def normalized(x, table):
    exact = x.astype(BF)
    y = dot(exact, table[0]) + dot(exact, table[1]) + dot(exact, table[2])
    spread = jnp.sum(x * y, axis=1, keepdims=True)
    return jnp.where(lanes(x.shape) == C, 1.0, x * lax.rsqrt(spread + 1e-06))


def ask(steps, heads, table, x, query, direct):
    count = x.shape[0]
    mine = normalized(x, table)
    short = mine.astype(BF)
    lane = lanes((count, 128))
    exact = x.astype(BF)
    for step in steps:
        direct[step] = dot(exact, table[3]) + dot(exact, table[4])
        for head in range(HEADS):
            both = heads[step * HEADS + head]
            grown = dot(short, both)
            constant = jnp.sum(mine * both[C : C + 16].astype(F32)[1:2], axis=1, keepdims=True)
            grown = jnp.where(lane < C, grown, jnp.where(lane == C, constant, 0.0)).astype(BF)
            query[step, head * count : (head + 1) * count, :] = grown


def attend(step, heads, query, direct, key, weight, mix):
    count = direct.shape[1]
    scores = lax.dot_general(query[step], key[...], NT, preferred_element_type=F32)
    weight[step] = jnp.exp2(scores - jnp.max(scores, axis=1, keepdims=True)).astype(BF)
    mixed = dot(weight[step], key[...])
    mix[step] = (mixed / mixed[:, C : C + 1]).astype(BF)
    eps = jnp.zeros((count, 128), F32)
    for head in range(HEADS):
        eps = eps + dot(mix[step, head * count : (head + 1) * count, :], heads[step * HEADS + head])
    return pack_high(eps + direct[step])


def work_space():
    return (
        pltpu.VMEM((TOKENS, 128), BF),
        pltpu.VMEM((2, HEADS * 32, TOKENS), BF),
        pltpu.VMEM((2, HEADS * 32, 128), BF),
    )


def first_sweep(coef, got, start, table, heads, first_eps, out, query, direct, key, weight, mix):
    _, core, _ = place()
    for at in range(2 * HEADS):
        step, source = at // HEADS, 2 * (at % HEADS)
        both = got[step, source, 0:80, :].astype(F32) + got[step, source + 1, 0:80, :].astype(F32)
        heads[at, 0:80, :] = both.astype(BF)
        heads[at, 80:128, :] = jnp.zeros((48, 128), BF)
    x = start[pl.ds(pl.multiple_of(core * 32, 32), 32), :].astype(BF).astype(F32)
    x = jnp.concatenate([x, jnp.zeros_like(x)], axis=1)
    everything = got[:, :, 80:96, :].astype(F32).reshape(PEERS * 16, 128)
    key[...] = unpack(everything, 1.0).astype(BF)
    ask((0, 1), heads, table, x, query, direct)
    eps = [attend(step, heads, query, direct, key, weight, mix) for step in range(2)]
    first_eps[...] = eps[0]
    both = (coef[2:3] * eps[0] + coef[3:4] * eps[1]).astype(BF)
    for to in range(Z):
        out[to] = both


def packed_start(start, core):
    x = start[pl.ds(pl.multiple_of(core * 32, 32), 32), :]
    return jnp.concatenate([x[:16], x[16:]], axis=1)


def below(got, z):
    total = jnp.zeros((16, 128), F32)
    for at in range(Z):
        total = total + jnp.where(at < z, got[at].astype(F32), 0.0)
    return total


def first_prefix(coef, got, start, first_eps, table, latents, out):
    z, core, _ = place()
    x = packed_start(start, core)
    even = x + coef[4:5] * x + below(got, z)
    odd = even + coef[0:1] * x + coef[2:3] * first_eps[...]
    latents[0] = even
    latents[1] = odd
    sent = [pack(normalized(unpack(x.astype(BF).astype(F32)), table)).astype(BF) for x in (even, odd)]
    for to in range(PEERS):
        out[to, 0:16, :] = sent[0]
        out[to, 16:32, :] = sent[1]


def second_queries(latents, table, heads, query, direct):
    for step in range(2):
        ask((step,), heads, table, unpack(latents[step].astype(BF).astype(F32)), query, direct)


def second_sweep(coef, got, latents, table, heads, query, direct, term, out, key, weight, mix):
    terms = []
    for step in range(2):
        everything = got[:, 16 * step : 16 * step + 16, :].astype(F32).reshape(PEERS * 16, 128)
        key[...] = unpack(everything, 1.0).astype(BF)
        eps = attend(step, heads, query, direct, key, weight, mix)
        terms.append(coef[step : step + 1] * latents[step] + coef[2 + step : 3 + step] * eps)
    term[...] = terms[0]
    both = (terms[0] + terms[1]).astype(BF)
    for to in range(Z):
        out[to] = both


def second_prefix(got, start, latents, term, fresh, out):
    z, core, _ = place()
    even = packed_start(start, core) + below(got, z)
    fresh[0] = even
    fresh[1] = even + term[...]
    for step in range(2):
        change = fresh[step] - latents[step]
        squared = change * change
        squared = squared[:8] + squared[8:]
        for to in range(PEERS // 2):
            out[step * 16 + to] = squared


def finish(got, halves, window, errors):
    _, core, _ = place()
    for half in range(2):
        packed = halves[half, core]
        window[0, half * 32 : half * 32 + 16, :] = packed[:, :C]
        window[0, half * 32 + 16 : half * 32 + 32, :] = packed[:, C:]
    total = got[0]
    for at in range(1, PEERS):
        total = total + got[at]
    total = jnp.sum(total, axis=(0, 1), keepdims=True)
    errors[...] = jnp.sqrt(total / (TOKENS * C) + 1e-06)


def body(start, timesteps, modulation, w_in, w_qkv, w_o, w_out):
    sent = call(
        send_weights,
        shape((Z, 96, 128), BF),
        (w_qkv, w_o, w_out.T),
        scratch=(
            pltpu.VMEM((3, ROWS, HEAD_DIM), BF),
            pltpu.VMEM((32, D), BF),
            pltpu.VMEM((C, D), BF),
            pltpu.SemaphoreType.DMA((5,)),
        ),
        far=(0, 1, 2),
    )
    got = lax.all_to_all(sent, "z", 0, 0, tiled=True)
    left, table, coef = call(
        make_tables,
        (shape((80, D), BF), shape((5, 128, 128), BF), shape((8, 128), F32)),
        (timesteps, w_in, w_out.T, modulation),
        smem=(0,),
        flops=10**9,
    )
    sent = call(
        make_heads,
        shape((PEERS // 2, 96, 128), BF),
        (lax.all_gather(got, "core"), left, start, table),
        scratch=(pltpu.VMEM((D, 128), BF), pltpu.VMEM((D, 128), BF)),
    )
    got = lax.all_gather(lax.all_to_all(sent, ("y", "x"), 0, 0, tiled=True), "core")
    heads, first_eps, sent = call(
        first_sweep,
        (shape((2 * HEADS, 128, 128), BF), shape((16, 128), F32), shape((Z, 16, 128), BF)),
        (coef, got, start, table),
        scratch=(pltpu.VMEM((2, HEADS * 32, 128), BF), pltpu.VMEM((2, 32, 128), F32), *work_space()),
    )
    got = lax.all_to_all(sent, "z", 0, 0, tiled=True)
    latents, sent = call(
        first_prefix, (shape((2, 16, 128), F32), shape((PEERS, 32, 128), BF)), (coef, got, start, first_eps, table)
    )
    got = lax.all_to_all(sent, FLAT, 0, 0, tiled=True)
    query, direct = call(
        second_queries,
        (shape((2, HEADS * 32, 128), BF), shape((2, 32, 128), F32)),
        (latents, table, heads),
        flops=10**9,
    )
    term, sent = call(
        second_sweep,
        (shape((16, 128), F32), shape((Z, 16, 128), BF)),
        (coef, got, latents, table, heads, query, direct),
        scratch=work_space(),
    )
    got = lax.all_to_all(sent, "z", 0, 0, tiled=True)
    fresh, sent = call(
        second_prefix, (shape((2, 16, 128), F32), shape((PEERS, 8, 128), F32)), (got, start, latents, term)
    )
    got = lax.all_to_all(sent, FLAT, 0, 0, tiled=True)
    halves = lax.all_gather(fresh, "core")
    window, errors = call(finish, (shape((1, 64, C), F32), shape((1, 1), F32)), (got, halves))
    return window, errors.reshape(1)


def solution(mesh):
    fine = Mesh(mesh.devices.reshape(Z, 2, 4, 4), ("z", "core", "y", "x"))
    step, seq = ("z", "core"), ("y", "x")
    return jax.shard_map(
        body,
        mesh=fine,
        in_specs=(P(seq, None), P(), P(step, None), P(), P(step, None), P(step, None), P()),
        out_specs=(P(step, seq, None), P(step)),
        check_vma=False,
    )
```

```python
import math

import jax
import jax.numpy as jnp
from jax import lax
from jax.experimental import pallas as pl
from jax.experimental.pallas import tpu as pltpu
from jax.sharding import Mesh
from jax.sharding import PartitionSpec as P

D = 1536
HEADS = 8
HEAD_DIM = 128
C = 64
INNER = 1024
STEPS = 32
TOKENS = 1024
Z = 16
PEERS = 32
ROWS = 48
FLAT = ("core", "y", "x")
BF = jnp.bfloat16
F32 = jnp.float32
NT = (((1,), (1,)), ((), ()))
BEST = lax.Precision.HIGHEST
SCALE = 1.0 / (math.sqrt(HEAD_DIM) * math.log(2.0))


def place():
    return lax.axis_index("z"), lax.axis_index("core"), lax.axis_index("y") * 4 + lax.axis_index("x")


def lanes(shape):
    return lax.broadcasted_iota(jnp.int32, shape, len(shape) - 1)


def rows(shape):
    return lax.broadcasted_iota(jnp.int32, shape, 0)


def dot(a, b):
    return jnp.dot(a, b, preferred_element_type=F32)


def unpack(packed, after=0.0):
    lane = lanes(packed.shape)
    low = lane < C
    rest = jnp.where(lane == C, after, 0.0)
    return jnp.concatenate([jnp.where(low, packed, rest), jnp.where(low, pltpu.roll(packed, C, 1), rest)], axis=0)


def pack(values):
    half = values.shape[0] // 2
    return jnp.where(lanes((half, 2 * C)) < C, values[:half], pltpu.roll(values[half:], C, 1))


def pack_high(values):
    half = values.shape[0] // 2
    low = lanes((half, 2 * C)) < C
    return jnp.where(low, pltpu.roll(values[:half], C, 1), values[half:])


def split_of(values, count):
    pieces = []
    for _ in range(count):
        piece = values.astype(BF)
        pieces.append(piece)
        values = values - piece.astype(F32)
    return pieces


def call(kernel, outs, args, scratch=(), smem=(), far=(), flops=0, grant=40):
    spaces = [pltpu.SMEM if at in smem else pl.ANY if at in far else pltpu.VMEM for at in range(len(args))]
    return pl.pallas_call(
        kernel,
        out_shape=outs,
        in_specs=[pl.BlockSpec(memory_space=space) for space in spaces],
        out_specs=jax.tree.map(lambda _: pl.BlockSpec(memory_space=pltpu.VMEM), outs),
        scratch_shapes=scratch,
        compiler_params=pltpu.CompilerParams(vmem_limit_bytes=grant * 1024 * 1024),
        cost_estimate=pl.CostEstimate(flops=flops, bytes_accessed=0, transcendentals=0) if flops else None,
    )(*args)


def shape(dims, kind):
    return jax.ShapeDtypeStruct(dims, kind)


def send_weights(w_qkv, w_o, w_out, out, blocks, left, right, arrived):
    _, _, seq = place()
    copies = [pltpu.make_async_copy(w_o, left, arrived.at[3]), pltpu.make_async_copy(w_out, right, arrived.at[4])]
    for at in range(3):
        start = pl.multiple_of(at * INNER + (seq // 2) * HEAD_DIM, HEAD_DIM)
        copies.append(pltpu.make_async_copy(w_qkv.at[:, pl.ds(start, HEAD_DIM)], blocks.at[at], arrived.at[at]))
    for copy in copies:
        copy.start()
    for copy in copies:
        copy.wait()
    odd = lax.rem(seq, 2) == 1

    def columns(at):
        block = blocks[at].astype(F32)
        return jnp.where(odd, block[:, C:], block[:, :C])

    first = jnp.concatenate([columns(0), columns(1)], axis=1).astype(BF)
    at, to = rows((HEAD_DIM, C)), lanes((HEAD_DIM, C))
    wanted = (to // 16) * 32 + to % 16 + jnp.where(odd, 16, 0)
    value = dot(blocks[2], jnp.where(at == wanted, 1.0, 0.0).astype(BF))
    head = lax.dot_general(left[...], right[...], NT, preferred_element_type=F32)
    head = jnp.where(odd, head[16:], head[:16])
    second = jnp.concatenate([value[0:16], value[16:32]], axis=1).astype(BF)
    third = jnp.concatenate([value[32:48], head], axis=1).astype(BF)
    for to in range(Z):
        out[to, 0:48, :] = first
        out[to, 48:64, :] = second
        out[to, 64:80, :] = third


def coefficients(timesteps):
    z, _, _ = place()
    lane = lanes((8, 128))
    moments = jnp.zeros((8, 128), F32)
    for at in range(STEPS + 1):
        moments = jnp.where(lane == at, timesteps[at].astype(F32), moments)
    angle = (moments / 1000.0 + 0.008) / 1.008 * (math.pi / 2)
    abar = jnp.cos(angle) ** 2
    after = pltpu.roll(abar, 127, 1)
    keep = jnp.sqrt(after / abar)
    noise = jnp.sqrt(1.0 - after) - keep * jnp.sqrt(1.0 - abar)
    less = keep - 1.0
    row = rows((8, 128))
    chosen = jnp.where(
        row < 2,
        jnp.where(lane == 2 * z + row, less, 0.0),
        jnp.where(row < 4, jnp.where(lane == 2 * z + row - 2, noise, 0.0), jnp.where(lane < 2 * z, less, 0.0)),
    )
    return jnp.broadcast_to(jnp.sum(chosen, axis=1, keepdims=True), (8, 128))


def make_tables(timesteps, w_in, w_out, modulation, left, table, coef):
    coef[...] = coefficients(timesteps)
    w = w_in[...].astype(F32)
    centred = w - jnp.mean(w, axis=1, keepdims=True)
    shift = modulation[:, 0:D].astype(F32)
    gain = modulation[:, D : 2 * D].astype(F32)
    left[0:C, :] = (centred * (1.0 + gain)).astype(BF)
    left[C : C + 16, :] = jnp.where(rows((16, D)) == 0, shift, 0.0).astype(BF)
    gram = lax.dot_general(centred, centred, NT, precision=BEST, preferred_element_type=F32) / D
    direct = lax.dot_general(w_in[...], w_out[...], NT, preferred_element_type=F32)
    pad = jnp.zeros((C, C), F32)
    gram = jnp.concatenate([gram, pad], axis=1)
    direct = jnp.concatenate([pad, direct], axis=1)
    for at, piece in enumerate(split_of(gram, 3) + split_of(direct, 2)):
        table[at, 0:C, :] = piece
        table[at, C : 2 * C, :] = jnp.zeros((C, 2 * C), BF)


def make_heads(both, left, start, table, out, qk, vw):
    _, core, seq = place()
    for z in range(Z):
        for parity in range(2):
            at = (z * 2 + parity) * ROWS
            qk[at : at + 48, :] = both[parity, z, 0:48, :]
            values = both[parity, z, 48:64, :]
            vw[at : at + 16, :] = values
            vw[at + 16 : at + 32, :] = pltpu.roll(values.astype(F32), C, 1).astype(BF)
            vw[at + 32 : at + 48, :] = both[parity, z, 64:80, :]
    first = dot(left[...], qk[...])
    value = dot(left[...], vw[...])[:, :C]
    query, key = first[:, :C], first[:, C:]
    even = seq - lax.rem(seq, 2)
    head = [both[group % 2, even + group // 2, 64:80, C:].astype(F32) for group in range(4)]
    head = jnp.concatenate(head, axis=0)
    a = lax.dot_general(query, key, NT, precision=BEST, preferred_element_type=F32) * SCALE
    b = jnp.dot(value, head, precision=BEST, preferred_element_type=F32)
    bias = lax.dot_general(key[C : C + 8], query, NT, precision=BEST, preferred_element_type=F32) * SCALE
    bias = jnp.concatenate([bias, jnp.zeros((8, 128 - bias.shape[1]), F32)], axis=1)[0:1]
    main = jnp.concatenate([a[:, :C], b], axis=1)
    main = jnp.where(rows(main.shape) == C + 1, bias, main).astype(BF)
    x = pack(normalized(unpack(packed_start(start, core).astype(BF).astype(F32)), table)).astype(BF)
    for to in range(PEERS // 2):
        out[to, 0:80, :] = main
        out[to, 80:96, :] = x


def normalized(x, table):
    exact = x.astype(BF)
    y = dot(exact, table[0]) + dot(exact, table[1]) + dot(exact, table[2])
    spread = jnp.sum(x * y, axis=1, keepdims=True)
    return jnp.where(lanes(x.shape) == C, 1.0, x * lax.rsqrt(spread + 1e-06))


def ask(steps, heads, table, x, query, direct):
    count = x.shape[0]
    mine = normalized(x, table)
    short = mine.astype(BF)
    lane = lanes((count, 128))
    exact = x.astype(BF)
    for step in steps:
        direct[step] = dot(exact, table[3]) + dot(exact, table[4])
        for head in range(HEADS):
            both = heads[step * HEADS + head]
            grown = dot(short, both)
            constant = jnp.sum(mine * both[C : C + 16].astype(F32)[1:2], axis=1, keepdims=True)
            grown = jnp.where(lane < C, grown, jnp.where(lane == C, constant, 0.0)).astype(BF)
            query[step, head * count : (head + 1) * count, :] = grown


def attend(step, heads, query, direct, key, weight, mix):
    count = direct.shape[1]
    scores = lax.dot_general(query[step], key[...], NT, preferred_element_type=F32)
    weight[step] = jnp.exp2(scores - jnp.max(scores, axis=1, keepdims=True)).astype(BF)
    mixed = dot(weight[step], key[...])
    mix[step] = (mixed / mixed[:, C : C + 1]).astype(BF)
    eps = jnp.zeros((count, 128), F32)
    for head in range(HEADS):
        eps = eps + dot(mix[step, head * count : (head + 1) * count, :], heads[step * HEADS + head])
    return pack_high(eps + direct[step])


def work_space():
    return (
        pltpu.VMEM((2, TOKENS, 128), BF),
        pltpu.VMEM((2, HEADS * 32, TOKENS), BF),
        pltpu.VMEM((2, HEADS * 32, 128), BF),
    )


def first_sweep(coef, got, start, table, heads, first_eps, out, query, direct, key, weight, mix):
    _, core, _ = place()
    for at in range(2 * HEADS):
        step, source = at // HEADS, 2 * (at % HEADS)
        both = got[step, source, 0:80, :].astype(F32) + got[step, source + 1, 0:80, :].astype(F32)
        heads[at, 0:80, :] = both.astype(BF)
        heads[at, 80:128, :] = jnp.zeros((48, 128), BF)
    x = start[pl.ds(pl.multiple_of(core * 32, 32), 32), :].astype(BF).astype(F32)
    x = jnp.concatenate([x, jnp.zeros_like(x)], axis=1)
    everything = got[:, :, 80:96, :].astype(F32).reshape(PEERS * 16, 128)
    key[0] = unpack(everything, 1.0).astype(BF)
    ask((0, 1), heads, table, x, query, direct)
    eps = [attend(step, heads, query, direct, key.at[0], weight, mix) for step in range(2)]
    first_eps[...] = eps[0]
    both = (coef[2:3] * eps[0] + coef[3:4] * eps[1]).astype(BF)
    for to in range(Z):
        out[to] = both


def packed_start(start, core):
    x = start[pl.ds(pl.multiple_of(core * 32, 32), 32), :]
    return jnp.concatenate([x[:16], x[16:]], axis=1)


def below(got, z):
    total = jnp.zeros((16, 128), F32)
    for at in range(Z):
        total = total + jnp.where(at < z, got[at].astype(F32), 0.0)
    return total


def first_prefix(coef, got, start, first_eps, table, latents, out):
    z, core, _ = place()
    x = packed_start(start, core)
    even = x + coef[4:5] * x + below(got, z)
    odd = even + coef[0:1] * x + coef[2:3] * first_eps[...]
    latents[0] = even
    latents[1] = odd
    sent = [pack(normalized(unpack(x.astype(BF).astype(F32)), table)).astype(BF) for x in (even, odd)]
    for to in range(PEERS):
        out[to, 0:16, :] = sent[0]
        out[to, 16:32, :] = sent[1]


def second_queries(latents, table, heads, query, direct):
    for step in range(2):
        ask((step,), heads, table, unpack(latents[step].astype(BF).astype(F32)), query, direct)


def second_sweep(coef, got, latents, table, heads, query, direct, term, out, key, weight, mix):
    terms = []
    for step in range(2):
        everything = got[:, 16 * step : 16 * step + 16, :].astype(F32).reshape(PEERS * 16, 128)
        key[step] = unpack(everything, 1.0).astype(BF)
        eps = attend(step, heads, query, direct, key.at[step], weight, mix)
        terms.append(coef[step : step + 1] * latents[step] + coef[2 + step : 3 + step] * eps)
    term[...] = terms[0]
    both = (terms[0] + terms[1]).astype(BF)
    for to in range(Z):
        out[to] = both


def second_prefix(got, start, latents, term, fresh, out):
    z, core, _ = place()
    even = packed_start(start, core) + below(got, z)
    fresh[0] = even
    fresh[1] = even + term[...]
    for step in range(2):
        change = fresh[step] - latents[step]
        squared = change * change
        squared = squared[:8] + squared[8:]
        for to in range(PEERS // 2):
            out[step * 16 + to] = squared


def finish(got, halves, window, errors):
    _, core, _ = place()
    for half in range(2):
        packed = halves[half, core]
        window[0, half * 32 : half * 32 + 16, :] = packed[:, :C]
        window[0, half * 32 + 16 : half * 32 + 32, :] = packed[:, C:]
    total = got[0]
    for at in range(1, PEERS):
        total = total + got[at]
    total = jnp.sum(total, axis=(0, 1), keepdims=True)
    errors[...] = jnp.sqrt(total / (TOKENS * C) + 1e-06)


def body(start, timesteps, modulation, w_in, w_qkv, w_o, w_out):
    sent = call(
        send_weights,
        shape((Z, 80, 128), BF),
        (w_qkv, w_o, w_out.T),
        scratch=(
            pltpu.VMEM((3, ROWS, HEAD_DIM), BF),
            pltpu.VMEM((32, D), BF),
            pltpu.VMEM((C, D), BF),
            pltpu.SemaphoreType.DMA((5,)),
        ),
        far=(0, 1, 2),
        grant=62,
    )
    got = lax.all_to_all(sent, "z", 0, 0, tiled=True)
    left, table, coef = call(
        make_tables,
        (shape((80, D), BF), shape((5, 128, 128), BF), shape((8, 128), F32)),
        (timesteps, w_in, w_out.T, modulation),
        smem=(0,),
        flops=10**9,
    )
    sent = call(
        make_heads,
        shape((PEERS // 2, 96, 128), BF),
        (lax.all_gather(got, "core"), left, start, table),
        scratch=(pltpu.VMEM((D, 128), BF), pltpu.VMEM((D, 128), BF)),
    )
    got = lax.all_gather(lax.all_to_all(sent, ("y", "x"), 0, 0, tiled=True), "core")
    heads, first_eps, sent = call(
        first_sweep,
        (shape((2 * HEADS, 128, 128), BF), shape((16, 128), F32), shape((Z, 16, 128), BF)),
        (coef, got, start, table),
        scratch=(pltpu.VMEM((2, HEADS * 32, 128), BF), pltpu.VMEM((2, 32, 128), F32), *work_space()),
    )
    got = lax.all_to_all(sent, "z", 0, 0, tiled=True)
    latents, sent = call(
        first_prefix, (shape((2, 16, 128), F32), shape((PEERS, 32, 128), BF)), (coef, got, start, first_eps, table)
    )
    got = lax.all_to_all(sent, FLAT, 0, 0, tiled=True)
    query, direct = call(
        second_queries,
        (shape((2, HEADS * 32, 128), BF), shape((2, 32, 128), F32)),
        (latents, table, heads),
        flops=10**9,
    )
    term, sent = call(
        second_sweep,
        (shape((16, 128), F32), shape((Z, 16, 128), BF)),
        (coef, got, latents, table, heads, query, direct),
        scratch=work_space(),
    )
    got = lax.all_to_all(sent, "z", 0, 0, tiled=True)
    fresh, sent = call(
        second_prefix, (shape((2, 16, 128), F32), shape((PEERS, 8, 128), F32)), (got, start, latents, term)
    )
    got = lax.all_to_all(sent, FLAT, 0, 0, tiled=True)
    halves = lax.all_gather(fresh, "core")
    window, errors = call(finish, (shape((1, 64, C), F32), shape((1, 1), F32)), (got, halves))
    return window, errors.reshape(1)


def solution(mesh):
    fine = Mesh(mesh.devices.reshape(Z, 2, 4, 4), ("z", "core", "y", "x"))
    step, seq = ("z", "core"), ("y", "x")
    return jax.shard_map(
        body,
        mesh=fine,
        in_specs=(P(seq, None), P(), P(step, None), P(), P(step, None), P(step, None), P()),
        out_specs=(P(step, seq, None), P(step)),
        check_vma=False,
    )
```

```python
import math

import jax
import jax.numpy as jnp
from jax import lax
from jax.experimental import pallas as pl
from jax.experimental.pallas import tpu as pltpu
from jax.sharding import Mesh
from jax.sharding import PartitionSpec as P

D = 1536
HEADS = 8
HEAD_DIM = 128
C = 64
INNER = 1024
STEPS = 32
TOKENS = 1024
Z = 16
PEERS = 32
ROWS = 48
FLAT = ("core", "y", "x")
FIRST_Z = 8
FIRST_SEQ = 10
Z_ORDER = [(at + FIRST_Z) % Z for at in range(Z)]
SEQ_ORDER = [(at + FIRST_SEQ) % 16 for at in range(16)]
FLAT_ORDER = SEQ_ORDER + [16 + at for at in SEQ_ORDER]
BF = jnp.bfloat16
F32 = jnp.float32
NT = (((1,), (1,)), ((), ()))
BEST = lax.Precision.HIGHEST
SCALE = 1.0 / (math.sqrt(HEAD_DIM) * math.log(2.0))


def place():
    return lax.axis_index("z"), lax.axis_index("core"), lax.axis_index("y") * 4 + lax.axis_index("x")


def lanes(shape):
    return lax.broadcasted_iota(jnp.int32, shape, len(shape) - 1)


def rows(shape):
    return lax.broadcasted_iota(jnp.int32, shape, 0)


def dot(a, b):
    return jnp.dot(a, b, preferred_element_type=F32)


def unpack(packed, after=0.0):
    lane = lanes(packed.shape)
    low = lane < C
    rest = jnp.where(lane == C, after, 0.0)
    return jnp.concatenate([jnp.where(low, packed, rest), jnp.where(low, pltpu.roll(packed, C, 1), rest)], axis=0)


def pack(values):
    half = values.shape[0] // 2
    return jnp.where(lanes((half, 2 * C)) < C, values[:half], pltpu.roll(values[half:], C, 1))


def pack_high(values):
    half = values.shape[0] // 2
    low = lanes((half, 2 * C)) < C
    return jnp.where(low, pltpu.roll(values[:half], C, 1), values[half:])


def split_of(values, count):
    pieces = []
    for _ in range(count):
        piece = values.astype(BF)
        pieces.append(piece)
        values = values - piece.astype(F32)
    return pieces


def call(kernel, outs, args, scratch=(), smem=(), far=(), flops=0, grant=40):
    spaces = [pltpu.SMEM if at in smem else pl.ANY if at in far else pltpu.VMEM for at in range(len(args))]
    return pl.pallas_call(
        kernel,
        out_shape=outs,
        in_specs=[pl.BlockSpec(memory_space=space) for space in spaces],
        out_specs=jax.tree.map(lambda _: pl.BlockSpec(memory_space=pltpu.VMEM), outs),
        scratch_shapes=scratch,
        compiler_params=pltpu.CompilerParams(vmem_limit_bytes=grant * 1024 * 1024),
        cost_estimate=pl.CostEstimate(flops=flops, bytes_accessed=0, transcendentals=0) if flops else None,
    )(*args)


def exchange(values, axis):
    order = {"z": Z_ORDER, ("y", "x"): SEQ_ORDER, FLAT: FLAT_ORDER}[axis]
    return lax.all_to_all(values, axis, 0, 0, axis_index_groups=[order], tiled=True)


def shape(dims, kind):
    return jax.ShapeDtypeStruct(dims, kind)


def send_weights(w_qkv, w_o, w_out, out, blocks, left, right, arrived):
    _, _, seq = place()
    copies = [pltpu.make_async_copy(w_o, left, arrived.at[3]), pltpu.make_async_copy(w_out, right, arrived.at[4])]
    for at in range(3):
        start = pl.multiple_of(at * INNER + (seq // 2) * HEAD_DIM, HEAD_DIM)
        copies.append(pltpu.make_async_copy(w_qkv.at[:, pl.ds(start, HEAD_DIM)], blocks.at[at], arrived.at[at]))
    for copy in copies:
        copy.start()
    for copy in copies:
        copy.wait()
    odd = lax.rem(seq, 2) == 1

    def columns(at):
        block = blocks[at].astype(F32)
        return jnp.where(odd, block[:, C:], block[:, :C])

    first = jnp.concatenate([columns(0), columns(1)], axis=1).astype(BF)
    at, to = rows((HEAD_DIM, C)), lanes((HEAD_DIM, C))
    wanted = (to // 16) * 32 + to % 16 + jnp.where(odd, 16, 0)
    value = dot(blocks[2], jnp.where(at == wanted, 1.0, 0.0).astype(BF))
    head = lax.dot_general(left[...], right[...], NT, preferred_element_type=F32)
    head = jnp.where(odd, head[16:], head[:16])
    second = jnp.concatenate([value[0:16], value[16:32]], axis=1).astype(BF)
    third = jnp.concatenate([value[32:48], head], axis=1).astype(BF)
    for to in range(Z):
        out[to, 0:48, :] = first
        out[to, 48:64, :] = second
        out[to, 64:80, :] = third


def coefficients(timesteps):
    z, _, _ = place()
    lane = lanes((8, 128))
    moments = jnp.zeros((8, 128), F32)
    for at in range(STEPS + 1):
        moments = jnp.where(lane == at, timesteps[at].astype(F32), moments)
    angle = (moments / 1000.0 + 0.008) / 1.008 * (math.pi / 2)
    abar = jnp.cos(angle) ** 2
    after = pltpu.roll(abar, 127, 1)
    keep = jnp.sqrt(after / abar)
    noise = jnp.sqrt(1.0 - after) - keep * jnp.sqrt(1.0 - abar)
    less = keep - 1.0
    row = rows((8, 128))
    chosen = jnp.where(
        row < 2,
        jnp.where(lane == 2 * z + row, less, 0.0),
        jnp.where(row < 4, jnp.where(lane == 2 * z + row - 2, noise, 0.0), jnp.where(lane < 2 * z, less, 0.0)),
    )
    return jnp.broadcast_to(jnp.sum(chosen, axis=1, keepdims=True), (8, 128))


def make_tables(timesteps, w_in, w_out, modulation, left, table, coef):
    coef[...] = coefficients(timesteps)
    w = w_in[...].astype(F32)
    centred = w - jnp.mean(w, axis=1, keepdims=True)
    shift = modulation[:, 0:D].astype(F32)
    gain = modulation[:, D : 2 * D].astype(F32)
    left[0:C, :] = (centred * (1.0 + gain)).astype(BF)
    left[C : C + 16, :] = jnp.where(rows((16, D)) == 0, shift, 0.0).astype(BF)
    gram = lax.dot_general(centred, centred, NT, precision=BEST, preferred_element_type=F32) / D
    direct = lax.dot_general(w_in[...], w_out[...], NT, preferred_element_type=F32)
    pad = jnp.zeros((C, C), F32)
    gram = jnp.concatenate([gram, pad], axis=1)
    direct = jnp.concatenate([pad, direct], axis=1)
    for at, piece in enumerate(split_of(gram, 3) + split_of(direct, 2)):
        table[at, 0:C, :] = piece
        table[at, C : 2 * C, :] = jnp.zeros((C, 2 * C), BF)


def make_heads(both, left, start, table, out, qk, vw):
    _, core, seq = place()
    for rank, z in enumerate(Z_ORDER):
        for parity in range(2):
            at = (z * 2 + parity) * ROWS
            qk[at : at + 48, :] = both[parity, rank, 0:48, :]
            values = both[parity, rank, 48:64, :]
            vw[at : at + 16, :] = values
            vw[at + 16 : at + 32, :] = pltpu.roll(values.astype(F32), C, 1).astype(BF)
            vw[at + 32 : at + 48, :] = both[parity, rank, 64:80, :]
    first = dot(left[...], qk[...])
    value = dot(left[...], vw[...])[:, :C]
    query, key = first[:, :C], first[:, C:]
    rank = lax.rem(seq - lax.rem(seq, 2) + Z - FIRST_Z, Z)
    head = [both[group % 2, rank + group // 2, 64:80, C:].astype(F32) for group in range(4)]
    head = jnp.concatenate(head, axis=0)
    a = lax.dot_general(query, key, NT, precision=BEST, preferred_element_type=F32) * SCALE
    b = jnp.dot(value, head, precision=BEST, preferred_element_type=F32)
    bias = lax.dot_general(key[C : C + 8], query, NT, precision=BEST, preferred_element_type=F32) * SCALE
    bias = jnp.concatenate([bias, jnp.zeros((8, 128 - bias.shape[1]), F32)], axis=1)[0:1]
    main = jnp.concatenate([a[:, :C], b], axis=1)
    main = jnp.where(rows(main.shape) == C + 1, bias, main).astype(BF)
    x = pack(normalized(unpack(packed_start(start, core).astype(BF).astype(F32)), table)).astype(BF)
    for to in range(PEERS // 2):
        out[to, 0:80, :] = main
        out[to, 80:96, :] = x


def normalized(x, table):
    exact = x.astype(BF)
    y = dot(exact, table[0]) + dot(exact, table[1]) + dot(exact, table[2])
    spread = jnp.sum(x * y, axis=1, keepdims=True)
    return jnp.where(lanes(x.shape) == C, 1.0, x * lax.rsqrt(spread + 1e-06))


def ask(steps, heads, table, x, query, direct):
    count = x.shape[0]
    mine = normalized(x, table)
    short = mine.astype(BF)
    lane = lanes((count, 128))
    exact = x.astype(BF)
    for step in steps:
        direct[step] = dot(exact, table[3]) + dot(exact, table[4])
        for head in range(HEADS):
            both = heads[step * HEADS + head]
            grown = dot(short, both)
            constant = jnp.sum(mine * both[C : C + 16].astype(F32)[1:2], axis=1, keepdims=True)
            grown = jnp.where(lane < C, grown, jnp.where(lane == C, constant, 0.0)).astype(BF)
            query[step, head * count : (head + 1) * count, :] = grown


def attend(step, heads, query, direct, key, weight, mix):
    count = direct.shape[1]
    scores = lax.dot_general(query[step], key[...], NT, preferred_element_type=F32)
    weight[step] = jnp.exp2(scores - jnp.max(scores, axis=1, keepdims=True)).astype(BF)
    mixed = dot(weight[step], key[...])
    mix[step] = (mixed / mixed[:, C : C + 1]).astype(BF)
    eps = jnp.zeros((count, 128), F32)
    for head in range(HEADS):
        eps = eps + dot(mix[step, head * count : (head + 1) * count, :], heads[step * HEADS + head])
    return pack_high(eps + direct[step])


def work_space():
    return (
        pltpu.VMEM((2, TOKENS, 128), BF),
        pltpu.VMEM((2, HEADS * 32, TOKENS), BF),
        pltpu.VMEM((2, HEADS * 32, 128), BF),
    )


def first_sweep(coef, got, start, table, heads, first_eps, out, query, direct, key, weight, mix):
    _, core, _ = place()
    for at in range(2 * HEADS):
        step, first = at // HEADS, SEQ_ORDER.index(2 * (at % HEADS))
        second = SEQ_ORDER.index(2 * (at % HEADS) + 1)
        both = got[step, first, 0:80, :].astype(F32) + got[step, second, 0:80, :].astype(F32)
        heads[at, 0:80, :] = both.astype(BF)
        heads[at, 80:128, :] = jnp.zeros((48, 128), BF)
    x = start[pl.ds(pl.multiple_of(core * 32, 32), 32), :].astype(BF).astype(F32)
    x = jnp.concatenate([x, jnp.zeros_like(x)], axis=1)
    everything = got[:, :, 80:96, :].astype(F32).reshape(PEERS * 16, 128)
    key[0] = unpack(everything, 1.0).astype(BF)
    ask((0, 1), heads, table, x, query, direct)
    eps = [attend(step, heads, query, direct, key.at[0], weight, mix) for step in range(2)]
    first_eps[...] = eps[0]
    both = (coef[2:3] * eps[0] + coef[3:4] * eps[1]).astype(BF)
    for to in range(Z):
        out[to] = both


def packed_start(start, core):
    x = start[pl.ds(pl.multiple_of(core * 32, 32), 32), :]
    return jnp.concatenate([x[:16], x[16:]], axis=1)


def below(got, z):
    total = jnp.zeros((16, 128), F32)
    for rank, at in enumerate(Z_ORDER):
        total = total + jnp.where(at < z, got[rank].astype(F32), 0.0)
    return total


def first_prefix(coef, got, start, first_eps, table, latents, out):
    z, core, _ = place()
    x = packed_start(start, core)
    even = x + coef[4:5] * x + below(got, z)
    odd = even + coef[0:1] * x + coef[2:3] * first_eps[...]
    latents[0] = even
    latents[1] = odd
    sent = [pack(normalized(unpack(x.astype(BF).astype(F32)), table)).astype(BF) for x in (even, odd)]
    for to in range(PEERS):
        out[to, 0:16, :] = sent[0]
        out[to, 16:32, :] = sent[1]


def second_queries(latents, table, heads, query, direct):
    for step in range(2):
        ask((step,), heads, table, unpack(latents[step].astype(BF).astype(F32)), query, direct)


def second_sweep(coef, got, latents, table, heads, query, direct, term, out, key, weight, mix):
    terms = []
    for step in range(2):
        everything = got[:, 16 * step : 16 * step + 16, :].astype(F32).reshape(PEERS * 16, 128)
        key[step] = unpack(everything, 1.0).astype(BF)
        eps = attend(step, heads, query, direct, key.at[step], weight, mix)
        terms.append(coef[step : step + 1] * latents[step] + coef[2 + step : 3 + step] * eps)
    term[...] = terms[0]
    both = (terms[0] + terms[1]).astype(BF)
    for to in range(Z):
        out[to] = both


def second_prefix(got, start, latents, term, fresh, out):
    z, core, _ = place()
    even = packed_start(start, core) + below(got, z)
    fresh[0] = even
    fresh[1] = even + term[...]
    for step in range(2):
        change = fresh[step] - latents[step]
        squared = change * change
        squared = squared[:8] + squared[8:]
        for to in range(PEERS // 2):
            out[step * 16 + to] = squared


def finish(got, halves, window, errors):
    _, core, _ = place()
    for half in range(2):
        packed = halves[half, core]
        window[0, half * 32 : half * 32 + 16, :] = packed[:, :C]
        window[0, half * 32 + 16 : half * 32 + 32, :] = packed[:, C:]
    total = got[0]
    for at in range(1, PEERS):
        total = total + got[at]
    total = jnp.sum(total, axis=(0, 1), keepdims=True)
    errors[...] = jnp.sqrt(total / (TOKENS * C) + 1e-06)


def body(start, timesteps, modulation, w_in, w_qkv, w_o, w_out):
    sent = call(
        send_weights,
        shape((Z, 80, 128), BF),
        (w_qkv, w_o, w_out.T),
        scratch=(
            pltpu.VMEM((3, ROWS, HEAD_DIM), BF),
            pltpu.VMEM((32, D), BF),
            pltpu.VMEM((C, D), BF),
            pltpu.SemaphoreType.DMA((5,)),
        ),
        far=(0, 1, 2),
        grant=62,
    )
    got = exchange(sent, "z")
    left, table, coef = call(
        make_tables,
        (shape((80, D), BF), shape((5, 128, 128), BF), shape((8, 128), F32)),
        (timesteps, w_in, w_out.T, modulation),
        smem=(0,),
        flops=10**9,
    )
    sent = call(
        make_heads,
        shape((PEERS // 2, 96, 128), BF),
        (lax.all_gather(got, "core"), left, start, table),
        scratch=(pltpu.VMEM((D, 128), BF), pltpu.VMEM((D, 128), BF)),
    )
    got = lax.all_gather(exchange(sent, ("y", "x")), "core")
    heads, first_eps, sent = call(
        first_sweep,
        (shape((2 * HEADS, 128, 128), BF), shape((16, 128), F32), shape((Z, 16, 128), BF)),
        (coef, got, start, table),
        scratch=(pltpu.VMEM((2, HEADS * 32, 128), BF), pltpu.VMEM((2, 32, 128), F32), *work_space()),
    )
    got = exchange(sent, "z")
    latents, sent = call(
        first_prefix, (shape((2, 16, 128), F32), shape((PEERS, 32, 128), BF)), (coef, got, start, first_eps, table)
    )
    got = exchange(sent, FLAT)
    query, direct = call(
        second_queries,
        (shape((2, HEADS * 32, 128), BF), shape((2, 32, 128), F32)),
        (latents, table, heads),
        flops=10**9,
    )
    term, sent = call(
        second_sweep,
        (shape((16, 128), F32), shape((Z, 16, 128), BF)),
        (coef, got, latents, table, heads, query, direct),
        scratch=work_space(),
    )
    got = exchange(sent, "z")
    fresh, sent = call(
        second_prefix, (shape((2, 16, 128), F32), shape((PEERS, 8, 128), F32)), (got, start, latents, term)
    )
    got = exchange(sent, FLAT)
    halves = lax.all_gather(fresh, "core")
    window, errors = call(finish, (shape((1, 64, C), F32), shape((1, 1), F32)), (got, halves))
    return window, errors.reshape(1)


def solution(mesh):
    fine = Mesh(mesh.devices.reshape(Z, 2, 4, 4), ("z", "core", "y", "x"))
    step, seq = ("z", "core"), ("y", "x")
    return jax.shard_map(
        body,
        mesh=fine,
        in_specs=(P(seq, None), P(), P(step, None), P(), P(step, None), P(step, None), P()),
        out_specs=(P(step, seq, None), P(step)),
        check_vma=False,
    )
```

```python
import math

import jax
import jax.numpy as jnp
from jax import lax
from jax.experimental import pallas as pl
from jax.experimental.pallas import tpu as pltpu
from jax.sharding import Mesh
from jax.sharding import PartitionSpec as P

D = 1536
HEADS = 8
HEAD_DIM = 128
C = 64
INNER = 1024
STEPS = 32
TOKENS = 1024
Z = 16
PEERS = 32
ROWS = 48
FLAT = ("core", "y", "x")
FIRST_Z = 8
FIRST_SEQ = 10
Z_ORDER = [(at + FIRST_Z) % Z for at in range(Z)]
SEQ_ORDER = [(at + FIRST_SEQ) % 16 for at in range(16)]
FLAT_ORDER = SEQ_ORDER + [16 + at for at in SEQ_ORDER]
BF = jnp.bfloat16
F32 = jnp.float32
NT = (((1,), (1,)), ((), ()))
BEST = lax.Precision.HIGHEST
SCALE = 1.0 / (math.sqrt(HEAD_DIM) * math.log(2.0))


def place():
    return lax.axis_index("z"), lax.axis_index("core"), lax.axis_index("y") * 4 + lax.axis_index("x")


def lanes(shape):
    return lax.broadcasted_iota(jnp.int32, shape, len(shape) - 1)


def rows(shape):
    return lax.broadcasted_iota(jnp.int32, shape, 0)


def dot(a, b):
    return jnp.dot(a, b, preferred_element_type=F32)


def unpack(packed, after=0.0):
    lane = lanes(packed.shape)
    low = lane < C
    rest = jnp.where(lane == C, after, 0.0)
    return jnp.concatenate([jnp.where(low, packed, rest), jnp.where(low, pltpu.roll(packed, C, 1), rest)], axis=0)


def pack(values):
    half = values.shape[0] // 2
    return jnp.where(lanes((half, 2 * C)) < C, values[:half], pltpu.roll(values[half:], C, 1))


def pack_high(values):
    half = values.shape[0] // 2
    low = lanes((half, 2 * C)) < C
    return jnp.where(low, pltpu.roll(values[:half], C, 1), values[half:])


def split_of(values, count):
    pieces = []
    for _ in range(count):
        piece = values.astype(BF)
        pieces.append(piece)
        values = values - piece.astype(F32)
    return pieces


def call(kernel, outs, args, scratch=(), smem=(), far=(), flops=0, grant=40, out_far=False):
    spaces = [pltpu.SMEM if at in smem else pl.ANY if at in far else pltpu.VMEM for at in range(len(args))]
    return pl.pallas_call(
        kernel,
        out_shape=outs,
        in_specs=[pl.BlockSpec(memory_space=space) for space in spaces],
        out_specs=jax.tree.map(lambda _: pl.BlockSpec(memory_space=pl.ANY if out_far else pltpu.VMEM), outs),
        scratch_shapes=scratch,
        compiler_params=pltpu.CompilerParams(vmem_limit_bytes=grant * 1024 * 1024),
        cost_estimate=pl.CostEstimate(flops=flops, bytes_accessed=0, transcendentals=0) if flops else None,
    )(*args)


def exchange(values, axis):
    order = {"z": Z_ORDER, ("y", "x"): SEQ_ORDER, FLAT: FLAT_ORDER}[axis]
    return lax.all_to_all(values, axis, 0, 0, axis_index_groups=[order], tiled=True)


def shape(dims, kind):
    return jax.ShapeDtypeStruct(dims, kind)


def send_weights(w_qkv, w_o, w_out, out, blocks, left, right, early, late, arrived, gone):
    _, _, seq = place()
    odd = lax.rem(seq, 2) == 1
    copies = []
    for at in range(3):
        start = pl.multiple_of(at * INNER + (seq // 2) * HEAD_DIM, HEAD_DIM)
        copies.append(pltpu.make_async_copy(w_qkv.at[:, pl.ds(start, HEAD_DIM)], blocks.at[at], arrived.at[at]))
    copies.append(pltpu.make_async_copy(w_o, left, arrived.at[3]))
    copies.append(pltpu.make_async_copy(w_out, right, arrived.at[4]))
    for copy in copies:
        copy.start()

    def columns(at):
        block = blocks[at].astype(F32)
        return jnp.where(odd, block[:, C:], block[:, :C])

    copies[0].wait()
    copies[1].wait()
    first = jnp.concatenate([columns(0), columns(1)], axis=1).astype(BF)
    for to in range(Z):
        early[to] = first
    first_out = pltpu.make_async_copy(early, out.at[:, 0:48, :], gone.at[0])
    first_out.start()
    at, to = rows((HEAD_DIM, C)), lanes((HEAD_DIM, C))
    wanted = (to // 16) * 32 + to % 16 + jnp.where(odd, 16, 0)
    chosen = jnp.where(at == wanted, 1.0, 0.0).astype(BF)
    copies[2].wait()
    value = dot(blocks[2], chosen)
    copies[3].wait()
    copies[4].wait()
    head = lax.dot_general(left[...], right[...], NT, preferred_element_type=F32)
    head = jnp.where(odd, head[16:], head[:16])
    second = jnp.concatenate([value[0:16], value[16:32]], axis=1).astype(BF)
    third = jnp.concatenate([value[32:48], head], axis=1).astype(BF)
    for to in range(Z):
        late[to, 0:16, :] = second
        late[to, 16:32, :] = third
    second_out = pltpu.make_async_copy(late, out.at[:, 48:80, :], gone.at[1])
    second_out.start()
    first_out.wait()
    second_out.wait()


def coefficients(timesteps):
    z, _, _ = place()
    lane = lanes((8, 128))
    moments = jnp.zeros((8, 128), F32)
    for at in range(STEPS + 1):
        moments = jnp.where(lane == at, timesteps[at].astype(F32), moments)
    angle = (moments / 1000.0 + 0.008) / 1.008 * (math.pi / 2)
    abar = jnp.cos(angle) ** 2
    after = pltpu.roll(abar, 127, 1)
    keep = jnp.sqrt(after / abar)
    noise = jnp.sqrt(1.0 - after) - keep * jnp.sqrt(1.0 - abar)
    less = keep - 1.0
    row = rows((8, 128))
    chosen = jnp.where(
        row < 2,
        jnp.where(lane == 2 * z + row, less, 0.0),
        jnp.where(row < 4, jnp.where(lane == 2 * z + row - 2, noise, 0.0), jnp.where(lane < 2 * z, less, 0.0)),
    )
    return jnp.broadcast_to(jnp.sum(chosen, axis=1, keepdims=True), (8, 128))


def make_tables(timesteps, w_in, w_out, modulation, start, left, table, coef, mine, direct, own):
    coef[...] = coefficients(timesteps)
    w = w_in[...].astype(F32)
    centred = w - jnp.mean(w, axis=1, keepdims=True)
    shift = modulation[:, 0:D].astype(F32)
    gain = modulation[:, D : 2 * D].astype(F32)
    left[0:C, :] = (centred * (1.0 + gain)).astype(BF)
    left[C : C + 16, :] = jnp.where(rows((16, D)) == 0, shift, 0.0).astype(BF)
    gram = lax.dot_general(centred, centred, NT, precision=BEST, preferred_element_type=F32) / D
    embed = lax.dot_general(w_in[...], w_out[...], NT, preferred_element_type=F32)
    pad = jnp.zeros((C, C), F32)
    gram = jnp.concatenate([gram, pad], axis=1)
    embed = jnp.concatenate([pad, embed], axis=1)
    for at, piece in enumerate(split_of(gram, 3) + split_of(embed, 2)):
        table[at, 0:C, :] = piece
        table[at, C : 2 * C, :] = jnp.zeros((C, 2 * C), BF)
    _, core, _ = place()
    x = unpack(packed_start(start, core).astype(BF).astype(F32))
    mine[...] = normalized(x, table)
    own[...] = pack(mine[...]).astype(BF)
    direct[...] = direct_of(x, table)


def make_heads(both, left, own, out, qk, vw):
    _, _, seq = place()
    for rank, z in enumerate(Z_ORDER):
        for parity in range(2):
            at = (z * 2 + parity) * ROWS
            qk[at : at + 48, :] = both[parity, rank, 0:48, :]
            values = both[parity, rank, 48:64, :]
            vw[at : at + 16, :] = values
            vw[at + 16 : at + 32, :] = pltpu.roll(values.astype(F32), C, 1).astype(BF)
            vw[at + 32 : at + 48, :] = both[parity, rank, 64:80, :]
    first = dot(left[...], qk[...])
    value = dot(left[...], vw[...])[:, :C]
    query, key = first[:, :C], first[:, C:]
    rank = lax.rem(seq - lax.rem(seq, 2) + Z - FIRST_Z, Z)
    head = [both[group % 2, rank + group // 2, 64:80, C:].astype(F32) for group in range(4)]
    head = jnp.concatenate(head, axis=0)
    a = lax.dot_general(query, key, NT, precision=BEST, preferred_element_type=F32) * SCALE
    b = jnp.dot(value, head, precision=BEST, preferred_element_type=F32)
    bias = lax.dot_general(key[C : C + 8], query, NT, precision=BEST, preferred_element_type=F32) * SCALE
    bias = jnp.concatenate([bias, jnp.zeros((8, 128 - bias.shape[1]), F32)], axis=1)[0:1]
    main = jnp.concatenate([a[:, :C], b], axis=1)
    main = jnp.where(rows(main.shape) == C + 1, bias, main).astype(BF)
    x = own[...]
    for to in range(PEERS // 2):
        out[to, 0:80, :] = main
        out[to, 80:96, :] = x


def normalized(x, table):
    exact = x.astype(BF)
    y = dot(exact, table[0]) + dot(exact, table[1]) + dot(exact, table[2])
    spread = jnp.sum(x * y, axis=1, keepdims=True)
    return jnp.where(lanes(x.shape) == C, 1.0, x * lax.rsqrt(spread + 1e-06))


def direct_of(x, table):
    exact = x.astype(BF)
    return pack_high(dot(exact, table[3]) + dot(exact, table[4]))


def ask(step, heads, mine, query):
    short = mine.astype(BF)
    lane = lanes(mine.shape)
    for head in range(HEADS):
        both = heads[step * HEADS + head]
        grown = dot(short, both)
        constant = jnp.sum(mine * both[C : C + 16].astype(F32)[1:2], axis=1, keepdims=True)
        grown = jnp.where(lane < C, grown, jnp.where(lane == C, constant, 0.0)).astype(BF)
        query[step, head * 32 : (head + 1) * 32, :] = grown


def attend(heads, query, direct, keys, weight, mix):
    both = range(2)
    scores = [lax.dot_general(query[step], keys[step][...], NT, preferred_element_type=F32) for step in both]
    tops = [jnp.max(score, axis=1, keepdims=True) for score in scores]
    for step in both:
        weight[step] = jnp.exp2(scores[step] - tops[step]).astype(BF)
    mixed = [dot(weight[step], keys[step][...]) for step in both]
    for step in both:
        shares = (mixed[step] / mixed[step][:, C : C + 1]).astype(BF)
        for head in range(HEADS):
            mix[step, :, head * 128 : (head + 1) * 128] = shares[head * 32 : (head + 1) * 32]
    eps = []
    for step in both:
        blocks = heads[step * HEADS : (step + 1) * HEADS].reshape(HEADS * 128, 128)
        eps.append(pack_high(dot(mix[step], blocks)) + direct[step])
    return eps


def work_space():
    return (
        pltpu.VMEM((2, TOKENS, 128), BF),
        pltpu.VMEM((2, HEADS * 32, TOKENS), BF),
        pltpu.VMEM((2, 32, HEADS * 128), BF),
    )


def first_sweep(coef, got, mine, direct, heads, first_eps, out, query, key, weight, mix):
    for at in range(2 * HEADS):
        step, first = at // HEADS, SEQ_ORDER.index(2 * (at % HEADS))
        second = SEQ_ORDER.index(2 * (at % HEADS) + 1)
        both = got[step, first, 0:80, :].astype(F32) + got[step, second, 0:80, :].astype(F32)
        heads[at, 0:80, :] = both.astype(BF)
        heads[at, 80:128, :] = jnp.zeros((48, 128), BF)
    everything = got[:, :, 80:96, :].astype(F32).reshape(PEERS * 16, 128)
    key[0] = unpack(everything, 1.0).astype(BF)
    for step in range(2):
        ask(step, heads, mine[...], query)
    eps = attend(heads, query, (direct[...], direct[...]), (key.at[0], key.at[0]), weight, mix)
    first_eps[...] = eps[0]
    both = (coef[2:3] * eps[0] + coef[3:4] * eps[1]).astype(BF)
    for to in range(Z):
        out[to] = both


def packed_start(start, core):
    x = start[pl.ds(pl.multiple_of(core * 32, 32), 32), :]
    return jnp.concatenate([x[:16], x[16:]], axis=1)


def below(got, z):
    total = jnp.zeros((16, 128), F32)
    for rank, at in enumerate(Z_ORDER):
        total = total + jnp.where(at < z, got[rank].astype(F32), 0.0)
    return total


def first_prefix(coef, got, start, first_eps, table, latents, out):
    z, core, _ = place()
    x = packed_start(start, core)
    even = x + coef[4:5] * x + below(got, z)
    odd = even + coef[0:1] * x + coef[2:3] * first_eps[...]
    latents[0] = even
    latents[1] = odd
    sent = [pack(normalized(unpack(x.astype(BF).astype(F32)), table)).astype(BF) for x in (even, odd)]
    for to in range(PEERS):
        out[to, 0:16, :] = sent[0]
        out[to, 16:32, :] = sent[1]


def second_queries(latents, table, heads, query, direct):
    for step in range(2):
        x = unpack(latents[step].astype(BF).astype(F32))
        direct[step] = direct_of(x, table)
        ask(step, heads, normalized(x, table), query)


def second_sweep(coef, got, latents, heads, query, direct, term, out, key, weight, mix):
    for step in range(2):
        everything = got[:, 16 * step : 16 * step + 16, :].astype(F32).reshape(PEERS * 16, 128)
        key[step] = unpack(everything, 1.0).astype(BF)
    eps = attend(heads, query, direct, (key.at[0], key.at[1]), weight, mix)
    terms = [coef[step : step + 1] * latents[step] + coef[2 + step : 3 + step] * eps[step] for step in range(2)]
    term[...] = terms[0]
    both = (terms[0] + terms[1]).astype(BF)
    for to in range(Z):
        out[to] = both


def second_prefix(got, start, latents, term, fresh, out):
    z, core, _ = place()
    even = packed_start(start, core) + below(got, z)
    fresh[0] = even
    fresh[1] = even + term[...]
    for step in range(2):
        change = fresh[step] - latents[step]
        squared = change * change
        squared = squared[:8] + squared[8:]
        for to in range(PEERS // 2):
            out[step * 16 + to] = squared


def finish(got, halves, window, errors):
    _, core, _ = place()
    for half in range(2):
        packed = halves[half, core]
        window[0, half * 32 : half * 32 + 16, :] = packed[:, :C]
        window[0, half * 32 + 16 : half * 32 + 32, :] = packed[:, C:]
    total = got[0]
    for at in range(1, PEERS):
        total = total + got[at]
    total = jnp.sum(total, axis=(0, 1), keepdims=True)
    errors[...] = jnp.sqrt(total / (TOKENS * C) + 1e-06)


def body(start, timesteps, modulation, w_in, w_qkv, w_o, w_out):
    sent = call(
        send_weights,
        shape((Z, 80, 128), BF),
        (w_qkv, w_o, w_out.T),
        scratch=(
            pltpu.VMEM((3, ROWS, HEAD_DIM), BF),
            pltpu.VMEM((32, D), BF),
            pltpu.VMEM((C, D), BF),
            pltpu.VMEM((Z, 48, 128), BF),
            pltpu.VMEM((Z, 32, 128), BF),
            pltpu.SemaphoreType.DMA((5,)),
            pltpu.SemaphoreType.DMA((2,)),
        ),
        far=(0, 1, 2),
        grant=62,
        out_far=True,
    )
    got = exchange(sent, "z")
    left, table, coef, mine, direct, own = call(
        make_tables,
        (
            shape((80, D), BF),
            shape((5, 128, 128), BF),
            shape((8, 128), F32),
            shape((32, 128), F32),
            shape((16, 128), F32),
            shape((16, 128), BF),
        ),
        (timesteps, w_in, w_out.T, modulation, start),
        smem=(0,),
        flops=10**9,
    )
    sent = call(
        make_heads,
        shape((PEERS // 2, 96, 128), BF),
        (lax.all_gather(got, "core"), left, own),
        scratch=(pltpu.VMEM((D, 128), BF), pltpu.VMEM((D, 128), BF)),
    )
    got = lax.all_gather(exchange(sent, ("y", "x")), "core")
    heads, first_eps, sent = call(
        first_sweep,
        (shape((2 * HEADS, 128, 128), BF), shape((16, 128), F32), shape((Z, 16, 128), BF)),
        (coef, got, mine, direct),
        scratch=(pltpu.VMEM((2, HEADS * 32, 128), BF), *work_space()),
    )
    got = exchange(sent, "z")
    latents, sent = call(
        first_prefix, (shape((2, 16, 128), F32), shape((PEERS, 32, 128), BF)), (coef, got, start, first_eps, table)
    )
    got = exchange(sent, FLAT)
    query, direct = call(
        second_queries,
        (shape((2, HEADS * 32, 128), BF), shape((2, 16, 128), F32)),
        (latents, table, heads),
        flops=10**9,
    )
    term, sent = call(
        second_sweep,
        (shape((16, 128), F32), shape((Z, 16, 128), BF)),
        (coef, got, latents, heads, query, direct),
        scratch=work_space(),
    )
    got = exchange(sent, "z")
    fresh, sent = call(
        second_prefix, (shape((2, 16, 128), F32), shape((PEERS, 8, 128), F32)), (got, start, latents, term)
    )
    got = exchange(sent, FLAT)
    halves = lax.all_gather(fresh, "core")
    window, errors = call(finish, (shape((1, 64, C), F32), shape((1, 1), F32)), (got, halves))
    return window, errors.reshape(1)


def solution(mesh):
    fine = Mesh(mesh.devices.reshape(Z, 2, 4, 4), ("z", "core", "y", "x"))
    step, seq = ("z", "core"), ("y", "x")
    return jax.shard_map(
        body,
        mesh=fine,
        in_specs=(P(seq, None), P(), P(step, None), P(), P(step, None), P(step, None), P()),
        out_specs=(P(step, seq, None), P(step)),
        check_vma=False,
    )
```

```python
import math

import jax
import jax.numpy as jnp
from jax import lax
from jax.experimental import pallas as pl
from jax.experimental.pallas import tpu as pltpu
from jax.sharding import Mesh
from jax.sharding import PartitionSpec as P

D = 1536
HEADS = 8
HEAD_DIM = 128
C = 64
INNER = 1024
STEPS = 32
TOKENS = 1024
Z = 16
PEERS = 32
ROWS = 48
FLAT = ("core", "y", "x")
FIRST_Z = 8
FIRST_SEQ = 10
Z_ORDER = [(at + FIRST_Z) % Z for at in range(Z)]
SEQ_ORDER = [(at + FIRST_SEQ) % 16 for at in range(16)]
FLAT_ORDER = SEQ_ORDER + [16 + at for at in SEQ_ORDER]
BF = jnp.bfloat16
F32 = jnp.float32
NT = (((1,), (1,)), ((), ()))
BEST = lax.Precision.HIGHEST
SCALE = 1.0 / (math.sqrt(HEAD_DIM) * math.log(2.0))


def place():
    return lax.axis_index("z"), lax.axis_index("core"), lax.axis_index("y") * 4 + lax.axis_index("x")


def lanes(shape):
    return lax.broadcasted_iota(jnp.int32, shape, len(shape) - 1)


def rows(shape):
    return lax.broadcasted_iota(jnp.int32, shape, 0)


def dot(a, b):
    return jnp.dot(a, b, preferred_element_type=F32)


def unpack(packed, after=0.0):
    lane = lanes(packed.shape)
    low = lane < C
    rest = jnp.where(lane == C, after, 0.0)
    return jnp.concatenate([jnp.where(low, packed, rest), jnp.where(low, pltpu.roll(packed, C, 1), rest)], axis=0)


def pack(values):
    half = values.shape[0] // 2
    return jnp.where(lanes((half, 2 * C)) < C, values[:half], pltpu.roll(values[half:], C, 1))


def pack_high(values):
    half = values.shape[0] // 2
    low = lanes((half, 2 * C)) < C
    return jnp.where(low, pltpu.roll(values[:half], C, 1), values[half:])


def split_of(values, count):
    pieces = []
    for _ in range(count):
        piece = values.astype(BF)
        pieces.append(piece)
        values = values - piece.astype(F32)
    return pieces


def call(kernel, outs, args, scratch=(), smem=(), far=(), flops=0, grant=40, out_far=False):
    spaces = [pltpu.SMEM if at in smem else pl.ANY if at in far else pltpu.VMEM for at in range(len(args))]
    return pl.pallas_call(
        kernel,
        out_shape=outs,
        in_specs=[pl.BlockSpec(memory_space=space) for space in spaces],
        out_specs=jax.tree.map(lambda _: pl.BlockSpec(memory_space=pl.ANY if out_far else pltpu.VMEM), outs),
        scratch_shapes=scratch,
        compiler_params=pltpu.CompilerParams(vmem_limit_bytes=grant * 1024 * 1024),
        cost_estimate=pl.CostEstimate(flops=flops, bytes_accessed=0, transcendentals=0) if flops else None,
    )(*args)


def exchange(values, axis):
    order = {"z": Z_ORDER, ("y", "x"): SEQ_ORDER, FLAT: FLAT_ORDER}[axis]
    return lax.all_to_all(values, axis, 0, 0, axis_index_groups=[order], tiled=True)


def shape(dims, kind):
    return jax.ShapeDtypeStruct(dims, kind)


def send_weights(w_qkv, w_o, w_out, out, blocks, left, right, early, late, arrived, gone):
    _, _, seq = place()
    odd = lax.rem(seq, 2) == 1
    copies = []
    for at in range(3):
        start = pl.multiple_of(at * INNER + (seq // 2) * HEAD_DIM, HEAD_DIM)
        copies.append(pltpu.make_async_copy(w_qkv.at[:, pl.ds(start, HEAD_DIM)], blocks.at[at], arrived.at[at]))
    copies.append(pltpu.make_async_copy(w_o, left, arrived.at[3]))
    copies.append(pltpu.make_async_copy(w_out, right, arrived.at[4]))
    for copy in copies:
        copy.start()

    def columns(at):
        block = blocks[at].astype(F32)
        return jnp.where(odd, block[:, C:], block[:, :C])

    copies[0].wait()
    copies[1].wait()
    first = jnp.concatenate([columns(0), columns(1)], axis=1).astype(BF)
    for to in range(Z):
        early[to] = first
    first_out = pltpu.make_async_copy(early, out.at[:, 0:48, :], gone.at[0])
    first_out.start()
    at, to = rows((HEAD_DIM, C)), lanes((HEAD_DIM, C))
    wanted = (to // 16) * 32 + to % 16 + jnp.where(odd, 16, 0)
    chosen = jnp.where(at == wanted, 1.0, 0.0).astype(BF)
    copies[2].wait()
    value = dot(blocks[2], chosen)
    copies[3].wait()
    copies[4].wait()
    head = lax.dot_general(left[...], right[...], NT, preferred_element_type=F32)
    head = jnp.where(odd, head[16:], head[:16])
    second = jnp.concatenate([value[0:16], value[16:32]], axis=1).astype(BF)
    third = jnp.concatenate([value[32:48], head], axis=1).astype(BF)
    for to in range(Z):
        late[to, 0:16, :] = second
        late[to, 16:32, :] = third
    second_out = pltpu.make_async_copy(late, out.at[:, 48:80, :], gone.at[1])
    second_out.start()
    first_out.wait()
    second_out.wait()


def coefficients(timesteps):
    z, _, _ = place()
    lane = lanes((8, 128))
    moments = jnp.zeros((8, 128), F32)
    for at in range(STEPS + 1):
        moments = jnp.where(lane == at, timesteps[at].astype(F32), moments)
    angle = (moments / 1000.0 + 0.008) / 1.008 * (math.pi / 2)
    abar = jnp.cos(angle) ** 2
    after = pltpu.roll(abar, 127, 1)
    keep = jnp.sqrt(after / abar)
    noise = jnp.sqrt(1.0 - after) - keep * jnp.sqrt(1.0 - abar)
    less = keep - 1.0
    row = rows((8, 128))
    chosen = jnp.where(
        row < 2,
        jnp.where(lane == 2 * z + row, less, 0.0),
        jnp.where(row < 4, jnp.where(lane == 2 * z + row - 2, noise, 0.0), jnp.where(lane < 2 * z, less, 0.0)),
    )
    return jnp.broadcast_to(jnp.sum(chosen, axis=1, keepdims=True), (8, 128))


def make_tables(timesteps, w_in, w_out, modulation, start, left, table, coef, mine, direct, own):
    coef[...] = coefficients(timesteps)
    w = w_in[...].astype(F32)
    centred = w - jnp.mean(w, axis=1, keepdims=True)
    shift = modulation[:, 0:D].astype(F32)
    gain = modulation[:, D : 2 * D].astype(F32)
    left[0:C, :] = (centred * (1.0 + gain)).astype(BF)
    left[C : C + 16, :] = jnp.where(rows((16, D)) == 0, shift, 0.0).astype(BF)
    gram = lax.dot_general(centred, centred, NT, precision=BEST, preferred_element_type=F32) / D
    embed = lax.dot_general(w_in[...], w_out[...], NT, preferred_element_type=F32)
    pad = jnp.zeros((C, C), F32)
    gram = jnp.concatenate([gram, pad], axis=1)
    embed = jnp.concatenate([pad, embed], axis=1)
    for at, piece in enumerate(split_of(gram, 3) + split_of(embed, 2)):
        table[at, 0:C, :] = piece
        table[at, C : 2 * C, :] = jnp.zeros((C, 2 * C), BF)
    _, core, _ = place()
    x = unpack(packed_start(start, core).astype(BF).astype(F32))
    mine[...] = normalized(x, table)
    own[...] = pack(mine[...]).astype(BF)
    direct[...] = direct_of(x, table)


def make_heads(both, left, own, out, qk, vw):
    _, _, seq = place()
    for rank, z in enumerate(Z_ORDER):
        for parity in range(2):
            at = (z * 2 + parity) * ROWS
            qk[at : at + 48, :] = both[parity, rank, 0:48, :]
            values = both[parity, rank, 48:64, :]
            vw[at : at + 16, :] = values
            vw[at + 16 : at + 32, :] = pltpu.roll(values.astype(F32), C, 1).astype(BF)
            vw[at + 32 : at + 48, :] = both[parity, rank, 64:80, :]
    first = dot(left[...], qk[...])
    value = dot(left[...], vw[...])[:, :C]
    query, key = first[:, :C], first[:, C:]
    ranks = [sum(jnp.where(seq // 2 == z // 2, Z_ORDER.index(z), 0) for z in range(late, Z, 2)) for late in range(2)]
    head = [both[group % 2, ranks[group // 2], 64:80, C:].astype(F32) for group in range(4)]
    head = jnp.concatenate(head, axis=0)
    a = lax.dot_general(query, key, NT, precision=BEST, preferred_element_type=F32) * SCALE
    b = jnp.dot(value, head, precision=BEST, preferred_element_type=F32)
    bias = lax.dot_general(key[C : C + 8], query, NT, precision=BEST, preferred_element_type=F32) * SCALE
    bias = jnp.concatenate([bias, jnp.zeros((8, 128 - bias.shape[1]), F32)], axis=1)[0:1]
    main = jnp.concatenate([a[:, :C], b], axis=1)
    main = jnp.where(rows(main.shape) == C + 1, bias, main).astype(BF)
    x = own[...]
    for to in range(PEERS // 2):
        out[to, 0:80, :] = main
        out[to, 80:96, :] = x


def normalized(x, table):
    exact = x.astype(BF)
    y = dot(exact, table[0]) + dot(exact, table[1]) + dot(exact, table[2])
    spread = jnp.sum(x * y, axis=1, keepdims=True)
    return jnp.where(lanes(x.shape) == C, 1.0, x * lax.rsqrt(spread + 1e-06))


def direct_of(x, table):
    exact = x.astype(BF)
    return pack_high(dot(exact, table[3]) + dot(exact, table[4]))


def ask(step, heads, mine, query):
    short = mine.astype(BF)
    lane = lanes(mine.shape)
    for head in range(HEADS):
        both = heads[step * HEADS + head]
        grown = dot(short, both)
        constant = jnp.sum(mine * both[C : C + 16].astype(F32)[1:2], axis=1, keepdims=True)
        grown = jnp.where(lane < C, grown, jnp.where(lane == C, constant, 0.0)).astype(BF)
        query[step, head * 32 : (head + 1) * 32, :] = grown


def attend(heads, query, direct, keys, weight, mix):
    both = range(2)
    scores = [lax.dot_general(query[step], keys[step][...], NT, preferred_element_type=F32) for step in both]
    tops = [jnp.max(score, axis=1, keepdims=True) for score in scores]
    for step in both:
        weight[step] = jnp.exp2(scores[step] - tops[step]).astype(BF)
    mixed = [dot(weight[step], keys[step][...]) for step in both]
    for step in both:
        shares = (mixed[step] / mixed[step][:, C : C + 1]).astype(BF)
        for head in range(HEADS):
            mix[step, :, head * 128 : (head + 1) * 128] = shares[head * 32 : (head + 1) * 32]
    eps = []
    for step in both:
        blocks = heads[step * HEADS : (step + 1) * HEADS].reshape(HEADS * 128, 128)
        eps.append(pack_high(dot(mix[step], blocks)) + direct[step])
    return eps


def work_space():
    return (
        pltpu.VMEM((2, TOKENS, 128), BF),
        pltpu.VMEM((2, HEADS * 32, TOKENS), BF),
        pltpu.VMEM((2, 32, HEADS * 128), BF),
    )


def first_sweep(coef, got, mine, direct, heads, first_eps, out, query, key, weight, mix):
    for at in range(2 * HEADS):
        step, first = at // HEADS, SEQ_ORDER.index(2 * (at % HEADS))
        second = SEQ_ORDER.index(2 * (at % HEADS) + 1)
        both = got[step, first, 0:80, :].astype(F32) + got[step, second, 0:80, :].astype(F32)
        heads[at, 0:80, :] = both.astype(BF)
        heads[at, 80:128, :] = jnp.zeros((48, 128), BF)
    everything = got[:, :, 80:96, :].astype(F32).reshape(PEERS * 16, 128)
    key[0] = unpack(everything, 1.0).astype(BF)
    for step in range(2):
        ask(step, heads, mine[...], query)
    eps = attend(heads, query, (direct[...], direct[...]), (key.at[0], key.at[0]), weight, mix)
    first_eps[...] = eps[0]
    both = (coef[2:3] * eps[0] + coef[3:4] * eps[1]).astype(BF)
    for to in range(Z):
        out[to] = both


def packed_start(start, core):
    x = start[pl.ds(pl.multiple_of(core * 32, 32), 32), :]
    return jnp.concatenate([x[:16], x[16:]], axis=1)


def below(got, z):
    total = jnp.zeros((16, 128), F32)
    for rank, at in enumerate(Z_ORDER):
        total = total + jnp.where(at < z, got[rank].astype(F32), 0.0)
    return total


def first_prefix(coef, got, start, first_eps, table, latents, mine, out):
    z, core, _ = place()
    x = packed_start(start, core)
    even = x + coef[4:5] * x + below(got, z)
    odd = even + coef[0:1] * x + coef[2:3] * first_eps[...]
    latents[0] = even
    latents[1] = odd
    sent = []
    for step, x in enumerate((even, odd)):
        mine[step] = normalized(unpack(x.astype(BF).astype(F32)), table)
        sent.append(pack(mine[step]).astype(BF))
    for to in range(PEERS):
        out[to, 0:16, :] = sent[0]
        out[to, 16:32, :] = sent[1]


def second_sweep(coef, got, latents, mine, table, heads, term, out, query, key, weight, mix):
    direct = []
    for step in range(2):
        everything = got[:, 16 * step : 16 * step + 16, :].astype(F32).reshape(PEERS * 16, 128)
        key[step] = unpack(everything, 1.0).astype(BF)
        direct.append(direct_of(unpack(latents[step].astype(BF).astype(F32)), table))
        ask(step, heads, mine[step], query)
    eps = attend(heads, query, direct, (key.at[0], key.at[1]), weight, mix)
    terms = [coef[step : step + 1] * latents[step] + coef[2 + step : 3 + step] * eps[step] for step in range(2)]
    term[...] = terms[0]
    both = (terms[0] + terms[1]).astype(BF)
    for to in range(Z):
        out[to] = both


def second_prefix(got, start, latents, term, out):
    z, core, _ = place()
    even = packed_start(start, core) + below(got, z)
    fresh = (even, even + term[...])
    for step in range(2):
        change = fresh[step] - latents[step]
        squared = change * change
        out[step, 0:16, :] = fresh[step]
        out[step, 16:24, :] = squared[:8] + squared[8:]


def send_errors(halves, out):
    _, core, _ = place()
    squared = halves[0, core, 16:24, :] + halves[1, core, 16:24, :]
    for to in range(PEERS // 2):
        out[to] = squared


def finish(got, halves, window, errors):
    _, core, _ = place()
    for half in range(2):
        packed = halves[half, core, 0:16, :]
        window[0, half * 32 : half * 32 + 16, :] = packed[:, :C]
        window[0, half * 32 + 16 : half * 32 + 32, :] = packed[:, C:]
    total = got[0]
    for at in range(1, PEERS // 2):
        total = total + got[at]
    total = jnp.sum(total, axis=(0, 1), keepdims=True)
    errors[...] = jnp.sqrt(total / (TOKENS * C) + 1e-06)


def body(start, timesteps, modulation, w_in, w_qkv, w_o, w_out):
    sent = call(
        send_weights,
        shape((Z, 80, 128), BF),
        (w_qkv, w_o, w_out.T),
        scratch=(
            pltpu.VMEM((3, ROWS, HEAD_DIM), BF),
            pltpu.VMEM((32, D), BF),
            pltpu.VMEM((C, D), BF),
            pltpu.VMEM((Z, 48, 128), BF),
            pltpu.VMEM((Z, 32, 128), BF),
            pltpu.SemaphoreType.DMA((5,)),
            pltpu.SemaphoreType.DMA((2,)),
        ),
        far=(0, 1, 2),
        grant=62,
        out_far=True,
    )
    got = exchange(sent, "z")
    left, table, coef, mine, direct, own = call(
        make_tables,
        (
            shape((80, D), BF),
            shape((5, 128, 128), BF),
            shape((8, 128), F32),
            shape((32, 128), F32),
            shape((16, 128), F32),
            shape((16, 128), BF),
        ),
        (timesteps, w_in, w_out.T, modulation, start),
        smem=(0,),
        flops=10**9,
    )
    sent = call(
        make_heads,
        shape((PEERS // 2, 96, 128), BF),
        (lax.all_gather(got, "core"), left, own),
        scratch=(pltpu.VMEM((D, 128), BF), pltpu.VMEM((D, 128), BF)),
    )
    got = lax.all_gather(exchange(sent, ("y", "x")), "core")
    heads, first_eps, sent = call(
        first_sweep,
        (shape((2 * HEADS, 128, 128), BF), shape((16, 128), F32), shape((Z, 16, 128), BF)),
        (coef, got, mine, direct),
        scratch=(pltpu.VMEM((2, HEADS * 32, 128), BF), *work_space()),
    )
    got = exchange(sent, "z")
    latents, mine, sent = call(
        first_prefix,
        (shape((2, 16, 128), F32), shape((2, 32, 128), F32), shape((PEERS, 32, 128), BF)),
        (coef, got, start, first_eps, table),
    )
    got = exchange(sent, FLAT)
    term, sent = call(
        second_sweep,
        (shape((16, 128), F32), shape((Z, 16, 128), BF)),
        (coef, got, latents, mine, table, heads),
        scratch=(pltpu.VMEM((2, HEADS * 32, 128), BF), *work_space()),
    )
    got = exchange(sent, "z")
    fresh = call(second_prefix, shape((2, 24, 128), F32), (got, start, latents, term))
    halves = lax.all_gather(fresh, "core")
    sent = call(send_errors, shape((PEERS // 2, 8, 128), F32), (halves,))
    got = exchange(sent, ("y", "x"))
    window, errors = call(finish, (shape((1, 64, C), F32), shape((1, 1), F32)), (got, halves))
    return window, errors.reshape(1)


def solution(mesh):
    fine = Mesh(mesh.devices.reshape(Z, 2, 4, 4), ("z", "core", "y", "x"))
    step, seq = ("z", "core"), ("y", "x")
    return jax.shard_map(
        body,
        mesh=fine,
        in_specs=(P(seq, None), P(), P(step, None), P(), P(step, None), P(step, None), P()),
        out_specs=(P(step, seq, None), P(step)),
        check_vma=False,
    )
```

```python
import math

import jax
import jax.numpy as jnp
from jax import lax
from jax.experimental import pallas as pl
from jax.experimental.pallas import tpu as pltpu
from jax.sharding import Mesh
from jax.sharding import PartitionSpec as P

D = 1536
HEADS = 8
HEAD_DIM = 128
C = 64
INNER = 1024
STEPS = 32
TOKENS = 1024
Z = 16
PEERS = 32
ROWS = 48
FLAT = ("core", "y", "x")
FIRST_Z = 8
FIRST_SEQ = 10
Z_ORDER = [(at + FIRST_Z) % Z for at in range(Z)]
SEQ_ORDER = [(at + FIRST_SEQ) % 16 for at in range(16)]
FLAT_ORDER = SEQ_ORDER + [16 + at for at in SEQ_ORDER]
BF = jnp.bfloat16
F32 = jnp.float32
NT = (((1,), (1,)), ((), ()))
BEST = lax.Precision.HIGHEST
SCALE = 1.0 / (math.sqrt(HEAD_DIM) * math.log(2.0))


def place():
    return lax.axis_index("z"), lax.axis_index("core"), lax.axis_index("y") * 4 + lax.axis_index("x")


def lanes(shape):
    return lax.broadcasted_iota(jnp.int32, shape, len(shape) - 1)


def rows(shape):
    return lax.broadcasted_iota(jnp.int32, shape, 0)


def dot(a, b):
    return jnp.dot(a, b, preferred_element_type=F32)


def unpack(packed, after=0.0):
    lane = lanes(packed.shape)
    low = lane < C
    rest = jnp.where(lane == C, after, 0.0)
    return jnp.concatenate([jnp.where(low, packed, rest), jnp.where(low, pltpu.roll(packed, C, 1), rest)], axis=0)


def pack(values):
    half = values.shape[0] // 2
    return jnp.where(lanes((half, 2 * C)) < C, values[:half], pltpu.roll(values[half:], C, 1))


def pack_high(values):
    half = values.shape[0] // 2
    low = lanes((half, 2 * C)) < C
    return jnp.where(low, pltpu.roll(values[:half], C, 1), values[half:])


def split_of(values, count):
    pieces = []
    for _ in range(count):
        piece = values.astype(BF)
        pieces.append(piece)
        values = values - piece.astype(F32)
    return pieces


def call(kernel, outs, args, scratch=(), smem=(), far=(), flops=0, grant=40, out_far=False):
    spaces = [pltpu.SMEM if at in smem else pl.ANY if at in far else pltpu.VMEM for at in range(len(args))]
    return pl.pallas_call(
        kernel,
        out_shape=outs,
        in_specs=[pl.BlockSpec(memory_space=space) for space in spaces],
        out_specs=jax.tree.map(lambda _: pl.BlockSpec(memory_space=pl.ANY if out_far else pltpu.VMEM), outs),
        scratch_shapes=scratch,
        compiler_params=pltpu.CompilerParams(vmem_limit_bytes=grant * 1024 * 1024),
        cost_estimate=pl.CostEstimate(flops=flops, bytes_accessed=0, transcendentals=0) if flops else None,
    )(*args)


def exchange(values, axis):
    order = {"z": Z_ORDER, ("y", "x"): SEQ_ORDER, FLAT: FLAT_ORDER}[axis]
    return lax.all_to_all(values, axis, 0, 0, axis_index_groups=[order], tiled=True)


def shape(dims, kind):
    return jax.ShapeDtypeStruct(dims, kind)


def send_weights(w_qkv, w_o, w_out, out, blocks, left, right, early, late, arrived, gone):
    _, _, seq = place()
    odd = lax.rem(seq, 2) == 1
    copies = []
    for at in range(3):
        start = pl.multiple_of(at * INNER + (seq // 2) * HEAD_DIM, HEAD_DIM)
        copies.append(pltpu.make_async_copy(w_qkv.at[:, pl.ds(start, HEAD_DIM)], blocks.at[at], arrived.at[at]))
    part = pl.multiple_of(lax.rem(seq, 2) * 16, 16)
    copies.append(pltpu.make_async_copy(w_o.at[pl.ds(part, 16), :], left, arrived.at[3]))
    copies.append(pltpu.make_async_copy(w_out, right, arrived.at[4]))
    for copy in copies:
        copy.start()

    def columns(at):
        block = blocks[at].astype(F32)
        return jnp.where(odd, block[:, C:], block[:, :C])

    copies[0].wait()
    copies[1].wait()
    first = jnp.concatenate([columns(0), columns(1)], axis=1).astype(BF)
    for to in range(Z):
        early[to] = first
    first_out = pltpu.make_async_copy(early, out.at[:, 0:48, :], gone.at[0])
    first_out.start()
    at, to = rows((HEAD_DIM, C)), lanes((HEAD_DIM, C))
    wanted = (to // 16) * 32 + to % 16 + jnp.where(odd, 16, 0)
    chosen = jnp.where(at == wanted, 1.0, 0.0).astype(BF)
    copies[2].wait()
    value = dot(blocks[2], chosen)
    copies[3].wait()
    copies[4].wait()
    head = lax.dot_general(left[...], right[...], NT, preferred_element_type=F32)
    second = jnp.concatenate([value[0:16], value[16:32]], axis=1).astype(BF)
    third = jnp.concatenate([value[32:48], head], axis=1).astype(BF)
    for to in range(Z):
        late[to, 0:16, :] = second
        late[to, 16:32, :] = third
    second_out = pltpu.make_async_copy(late, out.at[:, 48:80, :], gone.at[1])
    second_out.start()
    first_out.wait()
    second_out.wait()


def coefficients(timesteps):
    z, _, _ = place()
    lane = lanes((8, 128))
    moments = jnp.zeros((8, 128), F32)
    for at in range(STEPS + 1):
        moments = jnp.where(lane == at, timesteps[at].astype(F32), moments)
    angle = (moments / 1000.0 + 0.008) / 1.008 * (math.pi / 2)
    abar = jnp.cos(angle) ** 2
    after = pltpu.roll(abar, 127, 1)
    keep = jnp.sqrt(after / abar)
    noise = jnp.sqrt(1.0 - after) - keep * jnp.sqrt(1.0 - abar)
    less = keep - 1.0
    row = rows((8, 128))
    chosen = jnp.where(
        row < 2,
        jnp.where(lane == 2 * z + row, less, 0.0),
        jnp.where(row < 4, jnp.where(lane == 2 * z + row - 2, noise, 0.0), jnp.where(lane < 2 * z, less, 0.0)),
    )
    return jnp.broadcast_to(jnp.sum(chosen, axis=1, keepdims=True), (8, 128))


def make_tables(timesteps, w_in, w_out, modulation, start, left, table, coef, mine, direct, own):
    coef[...] = coefficients(timesteps)
    w = w_in[...].astype(F32)
    centred = w - jnp.mean(w, axis=1, keepdims=True)
    shift = modulation[:, 0:D].astype(F32)
    gain = modulation[:, D : 2 * D].astype(F32)
    left[0:C, :] = (centred * (1.0 + gain)).astype(BF)
    left[C : C + 16, :] = jnp.where(rows((16, D)) == 0, shift, 0.0).astype(BF)
    gram = lax.dot_general(centred, centred, NT, precision=BEST, preferred_element_type=F32) / D
    embed = lax.dot_general(w_in[...], w_out[...], NT, preferred_element_type=F32)
    pad = jnp.zeros((C, C), F32)
    gram = jnp.concatenate([gram, pad], axis=1)
    embed = jnp.concatenate([pad, embed], axis=1)
    for at, piece in enumerate(split_of(gram, 3) + split_of(embed, 2)):
        table[at, 0:C, :] = piece
        table[at, C : 2 * C, :] = jnp.zeros((C, 2 * C), BF)
    _, core, _ = place()
    x = unpack(packed_start(start, core).astype(BF).astype(F32))
    mine[...] = normalized(x, table)
    own[...] = pack(mine[...]).astype(BF)
    direct[...] = direct_of(x, table)


def make_heads(both, left, own, out, qk, vw):
    _, _, seq = place()
    for rank, z in enumerate(Z_ORDER):
        for parity in range(2):
            at = (z * 2 + parity) * ROWS
            qk[at : at + 48, :] = both[parity, rank, 0:48, :]
            values = both[parity, rank, 48:64, :]
            vw[at : at + 16, :] = values
            vw[at + 16 : at + 32, :] = pltpu.roll(values.astype(F32), C, 1).astype(BF)
            vw[at + 32 : at + 48, :] = both[parity, rank, 64:80, :]
    first = dot(left[...], qk[...])
    value = dot(left[...], vw[...])[:, :C]
    query, key = first[:, :C], first[:, C:]
    ranks = [sum(jnp.where(seq // 2 == z // 2, Z_ORDER.index(z), 0) for z in range(late, Z, 2)) for late in range(2)]
    head = [both[group % 2, ranks[group // 2], 64:80, C:].astype(F32) for group in range(4)]
    head = jnp.concatenate(head, axis=0)
    a = lax.dot_general(query, key, NT, precision=BEST, preferred_element_type=F32) * SCALE
    b = jnp.dot(value, head, precision=BEST, preferred_element_type=F32)
    bias = lax.dot_general(key[C : C + 8], query, NT, precision=BEST, preferred_element_type=F32) * SCALE
    bias = jnp.concatenate([bias, jnp.zeros((8, 128 - bias.shape[1]), F32)], axis=1)[0:1]
    main = jnp.concatenate([a[:, :C], b], axis=1)
    main = jnp.where(rows(main.shape) == C + 1, bias, main).astype(BF)
    x = own[...]
    for to in range(PEERS // 2):
        out[to, 0:80, :] = main
        out[to, 80:96, :] = x


def normalized(x, table):
    exact = x.astype(BF)
    y = dot(exact, table[0]) + dot(exact, table[1]) + dot(exact, table[2])
    spread = jnp.maximum(jnp.sum(x * y, axis=1, keepdims=True), 0.0)
    return jnp.where(lanes(x.shape) == C, 1.0, x * lax.rsqrt(spread + 1e-06))


def direct_of(x, table):
    exact = x.astype(BF)
    return pack_high(dot(exact, table[3]) + dot(exact, table[4]))


def ask(step, heads, mine, query):
    short = mine.astype(BF)
    lane = lanes(mine.shape)
    for head in range(HEADS):
        both = heads[step * HEADS + head]
        grown = dot(short, both)
        constant = jnp.sum(mine * both[C : C + 16].astype(F32)[1:2], axis=1, keepdims=True)
        grown = jnp.where(lane < C, grown, jnp.where(lane == C, constant, 0.0)).astype(BF)
        query[step, head * 32 : (head + 1) * 32, :] = grown


def attend(heads, query, direct, keys, weight, mix):
    both = range(2)
    scores = [lax.dot_general(query[step], keys[step][...], NT, preferred_element_type=F32) for step in both]
    tops = [jnp.max(score, axis=1, keepdims=True) for score in scores]
    for step in both:
        weight[step] = jnp.exp2(scores[step] - tops[step]).astype(BF)
    mixed = [dot(weight[step], keys[step][...]) for step in both]
    for step in both:
        shares = (mixed[step] / mixed[step][:, C : C + 1]).astype(BF)
        for head in range(HEADS):
            mix[step, :, head * 128 : (head + 1) * 128] = shares[head * 32 : (head + 1) * 32]
    eps = []
    for step in both:
        blocks = heads[step * HEADS : (step + 1) * HEADS].reshape(HEADS * 128, 128)
        eps.append(pack_high(dot(mix[step], blocks)) + direct[step])
    return eps


def work_space():
    return (
        pltpu.VMEM((2, TOKENS, 128), BF),
        pltpu.VMEM((2, HEADS * 32, TOKENS), BF),
        pltpu.VMEM((2, 32, HEADS * 128), BF),
    )


def first_sweep(coef, got, mine, direct, heads, first_eps, out, query, key, weight, mix):
    for at in range(2 * HEADS):
        step, first = at // HEADS, SEQ_ORDER.index(2 * (at % HEADS))
        second = SEQ_ORDER.index(2 * (at % HEADS) + 1)
        both = got[step, first, 0:80, :].astype(F32) + got[step, second, 0:80, :].astype(F32)
        heads[at, 0:80, :] = both.astype(BF)
        heads[at, 80:128, :] = jnp.zeros((48, 128), BF)
    everything = got[:, :, 80:96, :].astype(F32).reshape(PEERS * 16, 128)
    key[0] = unpack(everything, 1.0).astype(BF)
    for step in range(2):
        ask(step, heads, mine[...], query)
    eps = attend(heads, query, (direct[...], direct[...]), (key.at[0], key.at[0]), weight, mix)
    first_eps[...] = eps[0]
    both = (coef[2:3] * eps[0] + coef[3:4] * eps[1]).astype(BF)
    for to in range(Z):
        out[to] = both


def packed_start(start, core):
    x = start[pl.ds(pl.multiple_of(core * 32, 32), 32), :]
    return jnp.concatenate([x[:16], x[16:]], axis=1)


def below(got, z):
    total = jnp.zeros((16, 128), F32)
    for rank, at in enumerate(Z_ORDER):
        total = total + jnp.where(at < z, got[rank].astype(F32), 0.0)
    return total


def first_prefix(coef, got, start, first_eps, table, latents, mine, out):
    z, core, _ = place()
    x = packed_start(start, core)
    even = x + coef[4:5] * x + below(got, z)
    odd = even + coef[0:1] * x + coef[2:3] * first_eps[...]
    latents[0] = even
    latents[1] = odd
    sent = []
    for step, x in enumerate((even, odd)):
        mine[step] = normalized(unpack(x.astype(BF).astype(F32)), table)
        sent.append(pack(mine[step]).astype(BF))
    for to in range(PEERS):
        out[to, 0:16, :] = sent[0]
        out[to, 16:32, :] = sent[1]


def second_sweep(coef, got, latents, mine, table, heads, term, out, query, key, weight, mix):
    direct = []
    for step in range(2):
        everything = got[:, 16 * step : 16 * step + 16, :].astype(F32).reshape(PEERS * 16, 128)
        key[step] = unpack(everything, 1.0).astype(BF)
        direct.append(direct_of(unpack(latents[step].astype(BF).astype(F32)), table))
        ask(step, heads, mine[step], query)
    eps = attend(heads, query, direct, (key.at[0], key.at[1]), weight, mix)
    terms = [coef[step : step + 1] * latents[step] + coef[2 + step : 3 + step] * eps[step] for step in range(2)]
    term[...] = terms[0]
    both = (terms[0] + terms[1]).astype(BF)
    for to in range(Z):
        out[to] = both


def second_prefix(got, start, latents, term, out):
    z, core, _ = place()
    even = packed_start(start, core) + below(got, z)
    fresh = (even, even + term[...])
    for step in range(2):
        change = fresh[step] - latents[step]
        squared = change * change
        out[step, 0:16, :] = fresh[step]
        out[step, 16:24, :] = squared[:8] + squared[8:]


def send_errors(halves, out):
    _, core, _ = place()
    squared = halves[0, core, 16:24, :] + halves[1, core, 16:24, :]
    for to in range(PEERS // 2):
        out[to] = squared


def finish(got, halves, window, errors):
    _, core, _ = place()
    for half in range(2):
        packed = halves[half, core, 0:16, :]
        window[0, half * 32 : half * 32 + 16, :] = packed[:, :C]
        window[0, half * 32 + 16 : half * 32 + 32, :] = packed[:, C:]
    total = got[0]
    for at in range(1, PEERS // 2):
        total = total + got[at]
    total = jnp.sum(total, axis=(0, 1), keepdims=True)
    errors[...] = jnp.sqrt(total / (TOKENS * C) + 1e-06)


def body(start, timesteps, modulation, w_in, w_qkv, w_o, w_out):
    sent = call(
        send_weights,
        shape((Z, 80, 128), BF),
        (w_qkv, w_o, w_out.T),
        scratch=(
            pltpu.VMEM((3, ROWS, HEAD_DIM), BF),
            pltpu.VMEM((16, D), BF),
            pltpu.VMEM((C, D), BF),
            pltpu.VMEM((Z, 48, 128), BF),
            pltpu.VMEM((Z, 32, 128), BF),
            pltpu.SemaphoreType.DMA((5,)),
            pltpu.SemaphoreType.DMA((2,)),
        ),
        far=(0, 1, 2),
        grant=62,
        out_far=True,
    )
    got = exchange(sent, "z")
    left, table, coef, mine, direct, own = call(
        make_tables,
        (
            shape((80, D), BF),
            shape((5, 128, 128), BF),
            shape((8, 128), F32),
            shape((32, 128), F32),
            shape((16, 128), F32),
            shape((16, 128), BF),
        ),
        (timesteps, w_in, w_out.T, modulation, start),
        smem=(0,),
        flops=10**9,
    )
    sent = call(
        make_heads,
        shape((PEERS // 2, 96, 128), BF),
        (lax.all_gather(got, "core"), left, own),
        scratch=(pltpu.VMEM((D, 128), BF), pltpu.VMEM((D, 128), BF)),
    )
    got = lax.all_gather(exchange(sent, ("y", "x")), "core")
    heads, first_eps, sent = call(
        first_sweep,
        (shape((2 * HEADS, 128, 128), BF), shape((16, 128), F32), shape((Z, 16, 128), BF)),
        (coef, got, mine, direct),
        scratch=(pltpu.VMEM((2, HEADS * 32, 128), BF), *work_space()),
    )
    got = exchange(sent, "z")
    latents, mine, sent = call(
        first_prefix,
        (shape((2, 16, 128), F32), shape((2, 32, 128), F32), shape((PEERS, 32, 128), BF)),
        (coef, got, start, first_eps, table),
    )
    got = exchange(sent, FLAT)
    term, sent = call(
        second_sweep,
        (shape((16, 128), F32), shape((Z, 16, 128), BF)),
        (coef, got, latents, mine, table, heads),
        scratch=(pltpu.VMEM((2, HEADS * 32, 128), BF), *work_space()),
    )
    got = exchange(sent, "z")
    fresh = call(second_prefix, shape((2, 24, 128), F32), (got, start, latents, term))
    halves = lax.all_gather(fresh, "core")
    sent = call(send_errors, shape((PEERS // 2, 8, 128), F32), (halves,))
    got = exchange(sent, ("y", "x"))
    window, errors = call(finish, (shape((1, 64, C), F32), shape((1, 1), F32)), (got, halves))
    return window, errors.reshape(1)


def solution(mesh):
    fine = Mesh(mesh.devices.reshape(Z, 2, 4, 4), ("z", "core", "y", "x"))
    step, seq = ("z", "core"), ("y", "x")
    return jax.shard_map(
        body,
        mesh=fine,
        in_specs=(P(seq, None), P(), P(step, None), P(), P(step, None), P(step, None), P()),
        out_specs=(P(step, seq, None), P(step)),
        check_vma=False,
    )
```

```python
import math

import jax
import jax.numpy as jnp
from jax import lax
from jax.experimental import pallas as pl
from jax.experimental.pallas import tpu as pltpu
from jax.sharding import Mesh
from jax.sharding import PartitionSpec as P

D = 1536
HEADS = 8
HEAD_DIM = 128
C = 64
INNER = 1024
STEPS = 32
TOKENS = 1024
Z = 16
PEERS = 32
ROWS = 48
FLAT = ("core", "y", "x")
FIRST_Z = 8
FIRST_SEQ = 10
Z_ORDER = [(at + FIRST_Z) % Z for at in range(Z)]
Z_FIRST = [(at + 11) % Z for at in range(Z)]
SEQ_ORDER = [(at + FIRST_SEQ) % 16 for at in range(16)]
FLAT_ORDER = SEQ_ORDER + [16 + at for at in SEQ_ORDER]
BF = jnp.bfloat16
F32 = jnp.float32
NT = (((1,), (1,)), ((), ()))
BEST = lax.Precision.HIGHEST
SCALE = 1.0 / (math.sqrt(HEAD_DIM) * math.log(2.0))


def place():
    return lax.axis_index("z"), lax.axis_index("core"), lax.axis_index("y") * 4 + lax.axis_index("x")


def lanes(shape):
    return lax.broadcasted_iota(jnp.int32, shape, len(shape) - 1)


def rows(shape):
    return lax.broadcasted_iota(jnp.int32, shape, 0)


def dot(a, b):
    return jnp.dot(a, b, preferred_element_type=F32)


def unpack(packed, after=0.0):
    lane = lanes(packed.shape)
    low = lane < C
    rest = jnp.where(lane == C, after, 0.0)
    return jnp.concatenate([jnp.where(low, packed, rest), jnp.where(low, pltpu.roll(packed, C, 1), rest)], axis=0)


def pack(values):
    half = values.shape[0] // 2
    return jnp.where(lanes((half, 2 * C)) < C, values[:half], pltpu.roll(values[half:], C, 1))


def pack_high(values):
    half = values.shape[0] // 2
    low = lanes((half, 2 * C)) < C
    return jnp.where(low, pltpu.roll(values[:half], C, 1), values[half:])


def split_of(values, count):
    pieces = []
    for _ in range(count):
        piece = values.astype(BF)
        pieces.append(piece)
        values = values - piece.astype(F32)
    return pieces


def fine_dot(a, b, dims):
    a_high, a_low = split_of(a, 2)
    b_high, b_low = split_of(b, 2)
    parts = [lax.dot_general(x, y, dims, preferred_element_type=F32) for x, y in ((a_high, b_low), (a_low, b_high), (a_high, b_high))]
    return parts[0] + parts[1] + parts[2]


def call(kernel, outs, args, scratch=(), smem=(), far=(), flops=0, grant=40, out_far=False):
    spaces = [pltpu.SMEM if at in smem else pl.ANY if at in far else pltpu.VMEM for at in range(len(args))]
    return pl.pallas_call(
        kernel,
        out_shape=outs,
        in_specs=[pl.BlockSpec(memory_space=space) for space in spaces],
        out_specs=jax.tree.map(lambda _: pl.BlockSpec(memory_space=pl.ANY if out_far else pltpu.VMEM), outs),
        scratch_shapes=scratch,
        compiler_params=pltpu.CompilerParams(vmem_limit_bytes=grant * 1024 * 1024),
        cost_estimate=pl.CostEstimate(flops=flops, bytes_accessed=0, transcendentals=0) if flops else None,
    )(*args)


def exchange(values, axis):
    order = {"z": Z_ORDER, ("y", "x"): SEQ_ORDER, FLAT: FLAT_ORDER}[axis]
    return lax.all_to_all(values, axis, 0, 0, axis_index_groups=[order], tiled=True)


def shape(dims, kind):
    return jax.ShapeDtypeStruct(dims, kind)


def send_weights(w_qkv, w_o, w_out, out, blocks, left, right, early, late, arrived, gone):
    _, _, seq = place()
    odd = lax.rem(seq, 2) == 1
    copies = []
    for at in range(3):
        start = pl.multiple_of(at * INNER + (seq // 2) * HEAD_DIM, HEAD_DIM)
        copies.append(pltpu.make_async_copy(w_qkv.at[:, pl.ds(start, HEAD_DIM)], blocks.at[at], arrived.at[at]))
    part = pl.multiple_of(lax.rem(seq, 2) * 16, 16)
    copies.append(pltpu.make_async_copy(w_o.at[pl.ds(part, 16), :], left, arrived.at[3]))
    copies.append(pltpu.make_async_copy(w_out, right, arrived.at[4]))
    for copy in copies:
        copy.start()

    def columns(at):
        block = blocks[at].astype(F32)
        return jnp.where(odd, block[:, C:], block[:, :C])

    copies[0].wait()
    copies[1].wait()
    first = jnp.concatenate([columns(0), columns(1)], axis=1).astype(BF)
    for to in range(Z):
        early[to] = first
    first_out = pltpu.make_async_copy(early, out.at[:, 0:48, :], gone.at[0])
    first_out.start()
    at, to = rows((HEAD_DIM, C)), lanes((HEAD_DIM, C))
    wanted = (to // 16) * 32 + to % 16 + jnp.where(odd, 16, 0)
    chosen = jnp.where(at == wanted, 1.0, 0.0).astype(BF)
    copies[2].wait()
    value = dot(blocks[2], chosen)
    copies[3].wait()
    copies[4].wait()
    head = lax.dot_general(left[...], right[...], NT, preferred_element_type=F32)
    second = jnp.concatenate([value[0:16], value[16:32]], axis=1).astype(BF)
    third = jnp.concatenate([value[32:48], head], axis=1).astype(BF)
    for to in range(Z):
        late[to, 0:16, :] = second
        late[to, 16:32, :] = third
    second_out = pltpu.make_async_copy(late, out.at[:, 48:80, :], gone.at[1])
    second_out.start()
    first_out.wait()
    second_out.wait()


def coefficients(timesteps):
    z, _, _ = place()
    lane = lanes((8, 128))
    moments = jnp.zeros((8, 128), F32)
    for at in range(STEPS + 1):
        moments = jnp.where(lane == at, timesteps[at].astype(F32), moments)
    angle = (moments / 1000.0 + 0.008) / 1.008 * (math.pi / 2)
    abar = jnp.cos(angle) ** 2
    after = pltpu.roll(abar, 127, 1)
    keep = jnp.sqrt(after / abar)
    noise = jnp.sqrt(1.0 - after) - keep * jnp.sqrt(1.0 - abar)
    less = keep - 1.0
    row = rows((8, 128))
    chosen = jnp.where(
        row < 2,
        jnp.where(lane == 2 * z + row, less, 0.0),
        jnp.where(row < 4, jnp.where(lane == 2 * z + row - 2, noise, 0.0), jnp.where(lane < 2 * z, less, 0.0)),
    )
    return jnp.broadcast_to(jnp.sum(chosen, axis=1, keepdims=True), (8, 128))


def make_tables(timesteps, w_in, w_out, modulation, start, left, table, coef, mine, direct, own):
    coef[...] = coefficients(timesteps)
    w = w_in[...].astype(F32)
    centred = w - jnp.mean(w, axis=1, keepdims=True)
    shift = modulation[:, 0:D].astype(F32)
    gain = modulation[:, D : 2 * D].astype(F32)
    left[0:C, :] = (centred * (1.0 + gain)).astype(BF)
    left[C : C + 16, :] = jnp.where(rows((16, D)) == 0, shift, 0.0).astype(BF)
    gram = lax.dot_general(centred, centred, NT, precision=BEST, preferred_element_type=F32) / D
    embed = lax.dot_general(w_in[...], w_out[...], NT, preferred_element_type=F32)
    pad = jnp.zeros((C, C), F32)
    gram = jnp.concatenate([gram, pad], axis=1)
    embed = jnp.concatenate([pad, embed], axis=1)
    for at, piece in enumerate(split_of(gram, 3) + split_of(embed, 2)):
        table[at, 0:C, :] = piece
        table[at, C : 2 * C, :] = jnp.zeros((C, 2 * C), BF)
    _, core, _ = place()
    x = unpack(packed_start(start, core).astype(BF).astype(F32))
    mine[...] = normalized(x, table)
    own[...] = pack(mine[...]).astype(BF)
    direct[...] = direct_of(x, table)


def make_heads(both, left, own, out, qk, vw):
    _, _, seq = place()
    for rank, z in enumerate(Z_FIRST):
        for parity in range(2):
            at = (z * 2 + parity) * ROWS
            qk[at : at + 48, :] = both[parity, rank, 0:48, :]
            values = both[parity, rank, 48:64, :]
            vw[at : at + 16, :] = values
            vw[at + 16 : at + 32, :] = pltpu.roll(values.astype(F32), C, 1).astype(BF)
            vw[at + 32 : at + 48, :] = both[parity, rank, 64:80, :]
    first = dot(left[...], qk[...])
    value = dot(left[...], vw[...])[:, :C]
    query, key = first[:, :C], first[:, C:]
    ranks = [sum(jnp.where(seq // 2 == z // 2, Z_FIRST.index(z), 0) for z in range(late, Z, 2)) for late in range(2)]
    head = [both[group % 2, ranks[group // 2], 64:80, C:].astype(F32) for group in range(4)]
    head = jnp.concatenate(head, axis=0)
    a = fine_dot(query, key, NT) * SCALE
    b = fine_dot(value, head, (((1,), (0,)), ((), ())))
    bias = fine_dot(key[C : C + 8], query, NT) * SCALE
    bias = jnp.concatenate([bias, jnp.zeros((8, 128 - bias.shape[1]), F32)], axis=1)[0:1]
    main = jnp.concatenate([a[:, :C], b], axis=1)
    main = jnp.where(rows(main.shape) == C + 1, bias, main).astype(BF)
    x = own[...]
    for to in range(PEERS // 2):
        out[to, 0:80, :] = main
        out[to, 80:96, :] = x


def normalized(x, table):
    exact = x.astype(BF)
    y = dot(exact, table[0]) + dot(exact, table[1]) + dot(exact, table[2])
    spread = jnp.maximum(jnp.sum(x * y, axis=1, keepdims=True), 0.0)
    return jnp.where(lanes(x.shape) == C, 1.0, x * lax.rsqrt(spread + 1e-06))


def direct_of(x, table):
    exact = x.astype(BF)
    return pack_high(dot(exact, table[3]) + dot(exact, table[4]))


def ask(step, heads, mine, query):
    short = mine.astype(BF)
    lane = lanes(mine.shape)
    for head in range(HEADS):
        both = heads[step * HEADS + head]
        grown = dot(short, both)
        constant = jnp.sum(mine * both[C : C + 16].astype(F32)[1:2], axis=1, keepdims=True)
        grown = jnp.where(lane < C, grown, jnp.where(lane == C, constant, 0.0)).astype(BF)
        query[step, head * 32 : (head + 1) * 32, :] = grown


def attend(heads, query, direct, keys, weight, mix):
    both = range(2)
    scores = [lax.dot_general(query[step], keys[step][...], NT, preferred_element_type=F32) for step in both]
    tops = [jnp.max(score, axis=1, keepdims=True) for score in scores]
    for step in both:
        weight[step] = jnp.exp2(scores[step] - tops[step]).astype(BF)
    mixed = [dot(weight[step], keys[step][...]) for step in both]
    for step in both:
        shares = (mixed[step] / mixed[step][:, C : C + 1]).astype(BF)
        for head in range(HEADS):
            mix[step, :, head * 128 : (head + 1) * 128] = shares[head * 32 : (head + 1) * 32]
    eps = []
    for step in both:
        blocks = heads[step * HEADS : (step + 1) * HEADS].reshape(HEADS * 128, 128)
        eps.append(pack_high(dot(mix[step], blocks)) + direct[step])
    return eps


def work_space():
    return (
        pltpu.VMEM((2, TOKENS, 128), BF),
        pltpu.VMEM((2, HEADS * 32, TOKENS), BF),
        pltpu.VMEM((2, 32, HEADS * 128), BF),
    )


def first_sweep(coef, got, mine, direct, heads, first_eps, out, query, key, weight, mix):
    for at in range(2 * HEADS):
        step, first = at // HEADS, SEQ_ORDER.index(2 * (at % HEADS))
        second = SEQ_ORDER.index(2 * (at % HEADS) + 1)
        both = got[step, first, 0:80, :].astype(F32) + got[step, second, 0:80, :].astype(F32)
        heads[at, 0:80, :] = both.astype(BF)
        heads[at, 80:128, :] = jnp.zeros((48, 128), BF)
    everything = got[:, :, 80:96, :].astype(F32).reshape(PEERS * 16, 128)
    key[0] = unpack(everything, 1.0).astype(BF)
    for step in range(2):
        ask(step, heads, mine[...], query)
    eps = attend(heads, query, (direct[...], direct[...]), (key.at[0], key.at[0]), weight, mix)
    first_eps[...] = eps[0]
    both = (coef[2:3] * eps[0] + coef[3:4] * eps[1]).astype(BF)
    for to in range(Z):
        out[to] = both


def packed_start(start, core):
    x = start[pl.ds(pl.multiple_of(core * 32, 32), 32), :]
    return jnp.concatenate([x[:16], x[16:]], axis=1)


def below(got, z):
    total = jnp.zeros((16, 128), F32)
    for rank, at in enumerate(Z_ORDER):
        total = total + jnp.where(at < z, got[rank].astype(F32), 0.0)
    return total


def first_prefix(coef, got, start, first_eps, table, latents, mine, out):
    z, core, _ = place()
    x = packed_start(start, core)
    even = x + coef[4:5] * x + below(got, z)
    odd = even + coef[0:1] * x + coef[2:3] * first_eps[...]
    latents[0] = even
    latents[1] = odd
    sent = []
    for step, x in enumerate((even, odd)):
        mine[step] = normalized(unpack(x.astype(BF).astype(F32)), table)
        sent.append(pack(mine[step]).astype(BF))
    for to in range(PEERS):
        out[to, 0:16, :] = sent[0]
        out[to, 16:32, :] = sent[1]


def second_sweep(coef, got, latents, mine, table, heads, term, out, query, key, weight, mix):
    direct = []
    for step in range(2):
        everything = got[:, 16 * step : 16 * step + 16, :].astype(F32).reshape(PEERS * 16, 128)
        key[step] = unpack(everything, 1.0).astype(BF)
        direct.append(direct_of(unpack(latents[step].astype(BF).astype(F32)), table))
        ask(step, heads, mine[step], query)
    eps = attend(heads, query, direct, (key.at[0], key.at[1]), weight, mix)
    terms = [coef[step : step + 1] * latents[step] + coef[2 + step : 3 + step] * eps[step] for step in range(2)]
    term[...] = terms[0]
    both = (terms[0] + terms[1]).astype(BF)
    for to in range(Z):
        out[to] = both


def second_prefix(got, start, latents, term, out):
    z, core, _ = place()
    even = packed_start(start, core) + below(got, z)
    fresh = (even, even + term[...])
    for step in range(2):
        change = fresh[step] - latents[step]
        squared = change * change
        out[step, 0:16, :] = fresh[step]
        out[step, 16:24, :] = squared[:8] + squared[8:]


def send_errors(halves, out):
    _, core, _ = place()
    squared = halves[0, core, 16:24, :] + halves[1, core, 16:24, :]
    for to in range(PEERS // 2):
        out[to] = squared


def finish(got, halves, window, errors):
    _, core, _ = place()
    for half in range(2):
        packed = halves[half, core, 0:16, :]
        window[0, half * 32 : half * 32 + 16, :] = packed[:, :C]
        window[0, half * 32 + 16 : half * 32 + 32, :] = packed[:, C:]
    total = got[0]
    for at in range(1, PEERS // 2):
        total = total + got[at]
    total = jnp.sum(total, axis=(0, 1), keepdims=True)
    errors[...] = jnp.sqrt(total / (TOKENS * C) + 1e-06)


def body(start, timesteps, modulation, w_in, w_qkv, w_o, w_out):
    sent = call(
        send_weights,
        shape((Z, 80, 128), BF),
        (w_qkv, w_o, w_out.T),
        scratch=(
            pltpu.VMEM((3, ROWS, HEAD_DIM), BF),
            pltpu.VMEM((16, D), BF),
            pltpu.VMEM((C, D), BF),
            pltpu.VMEM((Z, 48, 128), BF),
            pltpu.VMEM((Z, 32, 128), BF),
            pltpu.SemaphoreType.DMA((5,)),
            pltpu.SemaphoreType.DMA((2,)),
        ),
        far=(0, 1, 2),
        grant=62,
        out_far=True,
    )
    got = lax.all_to_all(sent, "z", 0, 0, axis_index_groups=[Z_FIRST], tiled=True)
    left, table, coef, mine, direct, own = call(
        make_tables,
        (
            shape((80, D), BF),
            shape((5, 128, 128), BF),
            shape((8, 128), F32),
            shape((32, 128), F32),
            shape((16, 128), F32),
            shape((16, 128), BF),
        ),
        (timesteps, w_in, w_out.T, modulation, start),
        smem=(0,),
        flops=10**9,
    )
    sent = call(
        make_heads,
        shape((PEERS // 2, 96, 128), BF),
        (lax.all_gather(got, "core"), left, own),
        scratch=(pltpu.VMEM((D, 128), BF), pltpu.VMEM((D, 128), BF)),
    )
    got = lax.all_gather(exchange(sent, ("y", "x")), "core")
    heads, first_eps, sent = call(
        first_sweep,
        (shape((2 * HEADS, 128, 128), BF), shape((16, 128), F32), shape((Z, 16, 128), BF)),
        (coef, got, mine, direct),
        scratch=(pltpu.VMEM((2, HEADS * 32, 128), BF), *work_space()),
    )
    got = exchange(sent, "z")
    latents, mine, sent = call(
        first_prefix,
        (shape((2, 16, 128), F32), shape((2, 32, 128), F32), shape((PEERS, 32, 128), BF)),
        (coef, got, start, first_eps, table),
    )
    got = exchange(sent, FLAT)
    term, sent = call(
        second_sweep,
        (shape((16, 128), F32), shape((Z, 16, 128), BF)),
        (coef, got, latents, mine, table, heads),
        scratch=(pltpu.VMEM((2, HEADS * 32, 128), BF), *work_space()),
    )
    got = exchange(sent, "z")
    fresh = call(second_prefix, shape((2, 24, 128), F32), (got, start, latents, term))
    halves = lax.all_gather(fresh, "core")
    sent = call(send_errors, shape((PEERS // 2, 8, 128), F32), (halves,))
    got = exchange(sent, ("y", "x"))
    window, errors = call(finish, (shape((1, 64, C), F32), shape((1, 1), F32)), (got, halves))
    return window, errors.reshape(1)


def solution(mesh):
    fine = Mesh(mesh.devices.reshape(Z, 2, 4, 4), ("z", "core", "y", "x"))
    step, seq = ("z", "core"), ("y", "x")
    return jax.shard_map(
        body,
        mesh=fine,
        in_specs=(P(seq, None), P(), P(step, None), P(), P(step, None), P(step, None), P()),
        out_specs=(P(step, seq, None), P(step)),
        check_vma=False,
    )
```

```python
import math

import jax
import jax.numpy as jnp
from jax import lax
from jax.experimental import pallas as pl
from jax.experimental.pallas import tpu as pltpu
from jax.sharding import Mesh
from jax.sharding import PartitionSpec as P

D = 1536
HEADS = 8
HEAD_DIM = 128
C = 64
INNER = 1024
STEPS = 32
TOKENS = 1024
Z = 16
PEERS = 32
ROWS = 48
FLAT = ("core", "y", "x")
FIRST_Z = 8
FIRST_SEQ = 10
Z_ORDER = [(at + FIRST_Z) % Z for at in range(Z)]
Z_FIRST = [(at + 11) % Z for at in range(Z)]
SEQ_ORDER = [(at + FIRST_SEQ) % 16 for at in range(16)]
FLAT_ORDER = SEQ_ORDER + [16 + at for at in SEQ_ORDER]
BF = jnp.bfloat16
F32 = jnp.float32
NT = (((1,), (1,)), ((), ()))
BEST = lax.Precision.HIGHEST
SCALE = 1.0 / (math.sqrt(HEAD_DIM) * math.log(2.0))


def place():
    return lax.axis_index("z"), lax.axis_index("core"), lax.axis_index("y") * 4 + lax.axis_index("x")


def lanes(shape):
    return lax.broadcasted_iota(jnp.int32, shape, len(shape) - 1)


def rows(shape):
    return lax.broadcasted_iota(jnp.int32, shape, 0)


def dot(a, b):
    return jnp.dot(a, b, preferred_element_type=F32)


def unpack(packed, after=0.0):
    lane = lanes(packed.shape)
    low = lane < C
    rest = jnp.where(lane == C, after, 0.0)
    return jnp.concatenate([jnp.where(low, packed, rest), jnp.where(low, pltpu.roll(packed, C, 1), rest)], axis=0)


def pack(values):
    half = values.shape[0] // 2
    return jnp.where(lanes((half, 2 * C)) < C, values[:half], pltpu.roll(values[half:], C, 1))


def pack_high(values):
    half = values.shape[0] // 2
    low = lanes((half, 2 * C)) < C
    return jnp.where(low, pltpu.roll(values[:half], C, 1), values[half:])


def split_of(values, count):
    pieces = []
    for _ in range(count):
        piece = values.astype(BF)
        pieces.append(piece)
        values = values - piece.astype(F32)
    return pieces


def fine_dot(a, b, dims):
    a_high, a_low = split_of(a, 2)
    b_high, b_low = split_of(b, 2)
    parts = [lax.dot_general(x, y, dims, preferred_element_type=F32) for x, y in ((a_high, b_low), (a_low, b_high), (a_high, b_high))]
    return parts[0] + parts[1] + parts[2]


def call(kernel, outs, args, scratch=(), smem=(), far=(), flops=0, grant=40, out_far=False):
    spaces = [pltpu.SMEM if at in smem else pl.ANY if at in far else pltpu.VMEM for at in range(len(args))]
    return pl.pallas_call(
        kernel,
        out_shape=outs,
        in_specs=[pl.BlockSpec(memory_space=space) for space in spaces],
        out_specs=jax.tree.map(lambda _: pl.BlockSpec(memory_space=pl.ANY if out_far else pltpu.VMEM), outs),
        scratch_shapes=scratch,
        compiler_params=pltpu.CompilerParams(vmem_limit_bytes=grant * 1024 * 1024),
        cost_estimate=pl.CostEstimate(flops=flops, bytes_accessed=0, transcendentals=0) if flops else None,
    )(*args)


def exchange(values, axis):
    order = {"z": Z_ORDER, ("y", "x"): SEQ_ORDER, FLAT: FLAT_ORDER}[axis]
    return lax.all_to_all(values, axis, 0, 0, axis_index_groups=[order], tiled=True)


def shape(dims, kind):
    return jax.ShapeDtypeStruct(dims, kind)


def send_weights(w_qkv, w_o, w_out, out, blocks, left, right, early, late, arrived, gone):
    _, _, seq = place()
    odd = lax.rem(seq, 2) == 1
    copies = []
    for at in range(3):
        start = pl.multiple_of(at * INNER + (seq // 2) * HEAD_DIM, HEAD_DIM)
        copies.append(pltpu.make_async_copy(w_qkv.at[:, pl.ds(start, HEAD_DIM)], blocks.at[at], arrived.at[at]))
    part = pl.multiple_of(lax.rem(seq, 2) * 16, 16)
    copies.append(pltpu.make_async_copy(w_o.at[pl.ds(part, 16), :], left, arrived.at[3]))
    copies.append(pltpu.make_async_copy(w_out, right, arrived.at[4]))
    for copy in copies:
        copy.start()

    def columns(at):
        block = blocks[at].astype(F32)
        return jnp.where(odd, block[:, C:], block[:, :C])

    copies[0].wait()
    copies[1].wait()
    first = jnp.concatenate([columns(0), columns(1)], axis=1).astype(BF)
    for to in range(Z):
        early[to] = first
    first_out = pltpu.make_async_copy(early, out.at[:, 0:48, :], gone.at[0])
    first_out.start()
    at, to = rows((HEAD_DIM, C)), lanes((HEAD_DIM, C))
    wanted = (to // 16) * 32 + to % 16 + jnp.where(odd, 16, 0)
    chosen = jnp.where(at == wanted, 1.0, 0.0).astype(BF)
    copies[2].wait()
    value = dot(blocks[2], chosen)
    copies[3].wait()
    copies[4].wait()
    head = lax.dot_general(left[...], right[...], NT, preferred_element_type=F32)
    second = jnp.concatenate([value[0:16], value[16:32]], axis=1).astype(BF)
    third = jnp.concatenate([value[32:48], head], axis=1).astype(BF)
    for to in range(Z):
        late[to, 0:16, :] = second
        late[to, 16:32, :] = third
    second_out = pltpu.make_async_copy(late, out.at[:, 48:80, :], gone.at[1])
    second_out.start()
    first_out.wait()
    second_out.wait()


def coefficients(timesteps):
    z, _, _ = place()
    lane = lanes((8, 128))
    moments = jnp.zeros((8, 128), F32)
    for at in range(STEPS + 1):
        moments = jnp.where(lane == at, timesteps[at].astype(F32), moments)
    angle = (moments / 1000.0 + 0.008) / 1.008 * (math.pi / 2)
    abar = jnp.cos(angle) ** 2
    after = pltpu.roll(abar, 127, 1)
    keep = jnp.sqrt(after / abar)
    noise = jnp.sqrt(1.0 - after) - keep * jnp.sqrt(1.0 - abar)
    less = keep - 1.0
    row = rows((8, 128))
    chosen = jnp.where(
        row < 2,
        jnp.where(lane == 2 * z + row, less, 0.0),
        jnp.where(row < 4, jnp.where(lane == 2 * z + row - 2, noise, 0.0), jnp.where(lane < 2 * z, less, 0.0)),
    )
    return jnp.broadcast_to(jnp.sum(chosen, axis=1, keepdims=True), (8, 128))


def make_tables(timesteps, w_in, w_out, modulation, start, left, table, coef, mine, direct, own):
    coef[...] = coefficients(timesteps)
    w = w_in[...].astype(F32)
    centred = w - jnp.mean(w, axis=1, keepdims=True)
    shift = modulation[:, 0:D].astype(F32)
    gain = modulation[:, D : 2 * D].astype(F32)
    left[0:C, :] = (centred * (1.0 + gain)).astype(BF)
    left[C : C + 16, :] = jnp.where(rows((16, D)) == 0, shift, 0.0).astype(BF)
    gram = lax.dot_general(centred, centred, NT, precision=BEST, preferred_element_type=F32) / D
    embed = lax.dot_general(w_in[...], w_out[...], NT, preferred_element_type=F32)
    pad = jnp.zeros((C, C), F32)
    gram = jnp.concatenate([gram, pad], axis=1)
    embed = jnp.concatenate([pad, embed], axis=1)
    for at, piece in enumerate(split_of(gram, 3) + split_of(embed, 2)):
        table[at, 0:C, :] = piece
        table[at, C : 2 * C, :] = jnp.zeros((C, 2 * C), BF)
    _, core, _ = place()
    x = unpack(packed_start(start, core).astype(BF).astype(F32))
    mine[...] = normalized(x, table)
    own[...] = pack(mine[...]).astype(BF)
    direct[...] = direct_of(x, table)


def make_heads(both, left, own, out, qk, vw):
    _, _, seq = place()
    for rank, z in enumerate(Z_FIRST):
        for parity in range(2):
            at = (z * 2 + parity) * ROWS
            qk[at : at + 48, :] = both[parity, rank, 0:48, :]
            values = both[parity, rank, 48:64, :]
            vw[at : at + 16, :] = values
            vw[at + 16 : at + 32, :] = pltpu.roll(values.astype(F32), C, 1).astype(BF)
            vw[at + 32 : at + 48, :] = both[parity, rank, 64:80, :]
    first = dot(left[...], qk[...])
    value = dot(left[...], vw[...])[:, :C]
    query, key = first[:, :C], first[:, C:]
    ranks = [sum(jnp.where(seq // 2 == z // 2, Z_FIRST.index(z), 0) for z in range(late, Z, 2)) for late in range(2)]
    head = [both[group % 2, ranks[group // 2], 64:80, C:].astype(F32) for group in range(4)]
    head = jnp.concatenate(head, axis=0)
    a = fine_dot(query, key, NT) * SCALE
    b = fine_dot(value, head, (((1,), (0,)), ((), ())))
    bias = fine_dot(key[C : C + 8], query, NT) * SCALE
    bias = jnp.concatenate([bias, jnp.zeros((8, 128 - bias.shape[1]), F32)], axis=1)[0:1]
    main = jnp.concatenate([a[:, :C], b], axis=1)
    main = jnp.where(rows(main.shape) == C + 1, bias, main).astype(BF)
    x = own[...]
    for to in range(PEERS // 2):
        out[to, 0:80, :] = main
        out[to, 80:96, :] = x


def normalized(x, table):
    exact = x.astype(BF)
    y = dot(exact, table[0]) + dot(exact, table[1]) + dot(exact, table[2])
    spread = jnp.maximum(jnp.sum(x * y, axis=1, keepdims=True), 0.0)
    return jnp.where(lanes(x.shape) == C, 1.0, x * lax.rsqrt(spread + 1e-06))


def direct_of(x, table):
    exact = x.astype(BF)
    return pack_high(dot(exact, table[3]) + dot(exact, table[4]))


def ask(step, heads, mine, query):
    short = mine.astype(BF)
    lane = lanes(mine.shape)
    for head in range(HEADS):
        both = heads[step * HEADS + head]
        grown = dot(short, both)
        constant = jnp.sum(mine * both[C : C + 16].astype(F32)[1:2], axis=1, keepdims=True)
        grown = jnp.where(lane < C, grown, jnp.where(lane == C, constant, 0.0)).astype(BF)
        query[step, head * 32 : (head + 1) * 32, :] = grown


def attend(heads, query, direct, keys, weight, mix):
    both = range(2)
    scores = [lax.dot_general(query[step], keys[step][...], NT, preferred_element_type=F32) for step in both]
    tops = [jnp.max(score, axis=1, keepdims=True) for score in scores]
    for step in both:
        weight[step] = jnp.exp2(scores[step] - tops[step]).astype(BF)
    mixed = [dot(weight[step], keys[step][...]) for step in both]
    for step in both:
        shares = (mixed[step] * (1.0 / mixed[step][:, C : C + 1])).astype(BF)
        for head in range(HEADS):
            mix[step, :, head * 128 : (head + 1) * 128] = shares[head * 32 : (head + 1) * 32]
    eps = []
    for step in both:
        blocks = heads[step * HEADS : (step + 1) * HEADS].reshape(HEADS * 128, 128)
        eps.append(pack_high(dot(mix[step], blocks)) + direct[step])
    return eps


def work_space():
    return (
        pltpu.VMEM((2, TOKENS, 128), BF),
        pltpu.VMEM((2, HEADS * 32, TOKENS), BF),
        pltpu.VMEM((2, 32, HEADS * 128), BF),
    )


def first_sweep(coef, got, mine, direct, heads, first_eps, out, query, key, weight, mix):
    for at in range(2 * HEADS):
        step, first = at // HEADS, SEQ_ORDER.index(2 * (at % HEADS))
        second = SEQ_ORDER.index(2 * (at % HEADS) + 1)
        both = got[step, first, 0:80, :].astype(F32) + got[step, second, 0:80, :].astype(F32)
        heads[at, 0:80, :] = both.astype(BF)
        heads[at, 80:128, :] = jnp.zeros((48, 128), BF)
    everything = got[:, :, 80:96, :].astype(F32).reshape(PEERS * 16, 128)
    key[0] = unpack(everything, 1.0).astype(BF)
    for step in range(2):
        ask(step, heads, mine[...], query)
    eps = attend(heads, query, (direct[...], direct[...]), (key.at[0], key.at[0]), weight, mix)
    first_eps[...] = eps[0]
    both = (coef[2:3] * eps[0] + coef[3:4] * eps[1]).astype(BF)
    for to in range(Z):
        out[to] = both


def packed_start(start, core):
    x = start[pl.ds(pl.multiple_of(core * 32, 32), 32), :]
    return jnp.concatenate([x[:16], x[16:]], axis=1)


def below(got, z):
    total = jnp.zeros((16, 128), F32)
    for rank, at in enumerate(Z_ORDER):
        total = total + jnp.where(at < z, got[rank].astype(F32), 0.0)
    return total


def first_prefix(coef, got, start, first_eps, table, latents, mine, out):
    z, core, _ = place()
    x = packed_start(start, core)
    even = x + coef[4:5] * x + below(got, z)
    odd = even + coef[0:1] * x + coef[2:3] * first_eps[...]
    latents[0] = even
    latents[1] = odd
    sent = []
    for step, x in enumerate((even, odd)):
        mine[step] = normalized(unpack(x.astype(BF).astype(F32)), table)
        sent.append(pack(mine[step]).astype(BF))
    for to in range(PEERS):
        out[to, 0:16, :] = sent[0]
        out[to, 16:32, :] = sent[1]


def second_sweep(coef, got, latents, mine, table, heads, term, out, query, key, weight, mix):
    direct = []
    for step in range(2):
        everything = got[:, 16 * step : 16 * step + 16, :].astype(F32).reshape(PEERS * 16, 128)
        key[step] = unpack(everything, 1.0).astype(BF)
        direct.append(direct_of(unpack(latents[step].astype(BF).astype(F32)), table))
        ask(step, heads, mine[step], query)
    eps = attend(heads, query, direct, (key.at[0], key.at[1]), weight, mix)
    terms = [coef[step : step + 1] * latents[step] + coef[2 + step : 3 + step] * eps[step] for step in range(2)]
    term[...] = terms[0]
    both = (terms[0] + terms[1]).astype(BF)
    for to in range(Z):
        out[to] = both


def second_prefix(got, start, latents, term, out):
    z, core, _ = place()
    even = packed_start(start, core) + below(got, z)
    fresh = (even, even + term[...])
    for step in range(2):
        change = fresh[step] - latents[step]
        squared = change * change
        out[step, 0:16, :] = fresh[step]
        out[step, 16:24, :] = squared[:8] + squared[8:]


def send_errors(halves, out):
    _, core, _ = place()
    squared = halves[0, core, 16:24, :] + halves[1, core, 16:24, :]
    for to in range(PEERS // 2):
        out[to] = squared


def finish(got, halves, window, errors):
    _, core, _ = place()
    for half in range(2):
        packed = halves[half, core, 0:16, :]
        window[0, half * 32 : half * 32 + 16, :] = packed[:, :C]
        window[0, half * 32 + 16 : half * 32 + 32, :] = packed[:, C:]
    total = got[0]
    for at in range(1, PEERS // 2):
        total = total + got[at]
    total = jnp.sum(total, axis=(0, 1), keepdims=True)
    errors[...] = jnp.sqrt(total / (TOKENS * C) + 1e-06)


def body(start, timesteps, modulation, w_in, w_qkv, w_o, w_out):
    sent = call(
        send_weights,
        shape((Z, 80, 128), BF),
        (w_qkv, w_o, w_out.T),
        scratch=(
            pltpu.VMEM((3, ROWS, HEAD_DIM), BF),
            pltpu.VMEM((16, D), BF),
            pltpu.VMEM((C, D), BF),
            pltpu.VMEM((Z, 48, 128), BF),
            pltpu.VMEM((Z, 32, 128), BF),
            pltpu.SemaphoreType.DMA((5,)),
            pltpu.SemaphoreType.DMA((2,)),
        ),
        far=(0, 1, 2),
        grant=62,
        out_far=True,
    )
    got = lax.all_to_all(sent, "z", 0, 0, axis_index_groups=[Z_FIRST], tiled=True)
    left, table, coef, mine, direct, own = call(
        make_tables,
        (
            shape((80, D), BF),
            shape((5, 128, 128), BF),
            shape((8, 128), F32),
            shape((32, 128), F32),
            shape((16, 128), F32),
            shape((16, 128), BF),
        ),
        (timesteps, w_in, w_out.T, modulation, start),
        smem=(0,),
        flops=10**9,
    )
    sent = call(
        make_heads,
        shape((PEERS // 2, 96, 128), BF),
        (lax.all_gather(got, "core"), left, own),
        scratch=(pltpu.VMEM((D, 128), BF), pltpu.VMEM((D, 128), BF)),
    )
    got = lax.all_gather(exchange(sent, ("y", "x")), "core")
    heads, first_eps, sent = call(
        first_sweep,
        (shape((2 * HEADS, 128, 128), BF), shape((16, 128), F32), shape((Z, 16, 128), BF)),
        (coef, got, mine, direct),
        scratch=(pltpu.VMEM((2, HEADS * 32, 128), BF), *work_space()),
    )
    got = exchange(sent, "z")
    latents, mine, sent = call(
        first_prefix,
        (shape((2, 16, 128), F32), shape((2, 32, 128), F32), shape((PEERS, 32, 128), BF)),
        (coef, got, start, first_eps, table),
    )
    got = exchange(sent, FLAT)
    term, sent = call(
        second_sweep,
        (shape((16, 128), F32), shape((Z, 16, 128), BF)),
        (coef, got, latents, mine, table, heads),
        scratch=(pltpu.VMEM((2, HEADS * 32, 128), BF), *work_space()),
    )
    got = exchange(sent, "z")
    fresh = call(second_prefix, shape((2, 24, 128), F32), (got, start, latents, term))
    halves = lax.all_gather(fresh, "core")
    sent = call(send_errors, shape((PEERS // 2, 8, 128), F32), (halves,))
    got = exchange(sent, ("y", "x"))
    window, errors = call(finish, (shape((1, 64, C), F32), shape((1, 1), F32)), (got, halves))
    return window, errors.reshape(1)


def solution(mesh):
    fine = Mesh(mesh.devices.reshape(Z, 2, 4, 4), ("z", "core", "y", "x"))
    step, seq = ("z", "core"), ("y", "x")
    return jax.shard_map(
        body,
        mesh=fine,
        in_specs=(P(seq, None), P(), P(step, None), P(), P(step, None), P(step, None), P()),
        out_specs=(P(step, seq, None), P(step)),
        check_vma=False,
    )
```

```python
import math

import jax
import jax.numpy as jnp
from jax import lax
from jax.experimental import pallas as pl
from jax.experimental.pallas import tpu as pltpu
from jax.sharding import Mesh
from jax.sharding import PartitionSpec as P

D = 1536
HEADS = 8
HEAD_DIM = 128
C = 64
INNER = 1024
STEPS = 32
TOKENS = 1024
Z = 16
PEERS = 32
ROWS = 48
FLAT = ("core", "y", "x")
FIRST_Z = 8
FIRST_SEQ = 10
Z_ORDER = [(at + FIRST_Z) % Z for at in range(Z)]
Z_FIRST = [(at + 10) % Z for at in range(Z)]
SEQ_ORDER = [(at + FIRST_SEQ) % 16 for at in range(16)]
FLAT_ORDER = SEQ_ORDER + [16 + at for at in SEQ_ORDER]
BF = jnp.bfloat16
F32 = jnp.float32
NT = (((1,), (1,)), ((), ()))
BEST = lax.Precision.HIGHEST
SCALE = 1.0 / (math.sqrt(HEAD_DIM) * math.log(2.0))


def place():
    return lax.axis_index("z"), lax.axis_index("core"), lax.axis_index("y") * 4 + lax.axis_index("x")


def lanes(shape):
    return lax.broadcasted_iota(jnp.int32, shape, len(shape) - 1)


def rows(shape):
    return lax.broadcasted_iota(jnp.int32, shape, 0)


def dot(a, b):
    return jnp.dot(a, b, preferred_element_type=F32)


def unpack(packed, after=0.0):
    lane = lanes(packed.shape)
    low = lane < C
    rest = jnp.where(lane == C, after, 0.0)
    return jnp.concatenate([jnp.where(low, packed, rest), jnp.where(low, pltpu.roll(packed, C, 1), rest)], axis=0)


def pack(values):
    half = values.shape[0] // 2
    return jnp.where(lanes((half, 2 * C)) < C, values[:half], pltpu.roll(values[half:], C, 1))


def pack_high(values):
    half = values.shape[0] // 2
    low = lanes((half, 2 * C)) < C
    return jnp.where(low, pltpu.roll(values[:half], C, 1), values[half:])


def split_of(values, count):
    pieces = []
    for _ in range(count):
        piece = values.astype(BF)
        pieces.append(piece)
        values = values - piece.astype(F32)
    return pieces


def fine_dot(a, b, dims):
    a_high, a_low = split_of(a, 2)
    b_high, b_low = split_of(b, 2)
    parts = [lax.dot_general(x, y, dims, preferred_element_type=F32) for x, y in ((a_high, b_low), (a_low, b_high), (a_high, b_high))]
    return parts[0] + parts[1] + parts[2]


def call(kernel, outs, args, scratch=(), smem=(), far=(), flops=0, grant=40, out_far=False):
    spaces = [pltpu.SMEM if at in smem else pl.ANY if at in far else pltpu.VMEM for at in range(len(args))]
    return pl.pallas_call(
        kernel,
        out_shape=outs,
        in_specs=[pl.BlockSpec(memory_space=space) for space in spaces],
        out_specs=jax.tree.map(lambda _: pl.BlockSpec(memory_space=pl.ANY if out_far else pltpu.VMEM), outs),
        scratch_shapes=scratch,
        compiler_params=pltpu.CompilerParams(vmem_limit_bytes=grant * 1024 * 1024),
        cost_estimate=pl.CostEstimate(flops=flops, bytes_accessed=0, transcendentals=0) if flops else None,
    )(*args)


def exchange(values, axis):
    order = {"z": Z_ORDER, ("y", "x"): SEQ_ORDER, FLAT: FLAT_ORDER}[axis]
    return lax.all_to_all(values, axis, 0, 0, axis_index_groups=[order], tiled=True)


def shape(dims, kind):
    return jax.ShapeDtypeStruct(dims, kind)


def send_weights(w_qkv, w_o, w_out, out, blocks, left, right, early, late, arrived, gone):
    _, _, seq = place()
    odd = lax.rem(seq, 2) == 1
    copies = []
    for at in range(3):
        start = pl.multiple_of(at * INNER + (seq // 2) * HEAD_DIM, HEAD_DIM)
        copies.append(pltpu.make_async_copy(w_qkv.at[:, pl.ds(start, HEAD_DIM)], blocks.at[at], arrived.at[at]))
    part = pl.multiple_of(lax.rem(seq, 2) * 16, 16)
    copies.append(pltpu.make_async_copy(w_o.at[pl.ds(part, 16), :], left, arrived.at[3]))
    copies.append(pltpu.make_async_copy(w_out, right, arrived.at[4]))
    for copy in copies:
        copy.start()

    def columns(at):
        block = blocks[at].astype(F32)
        return jnp.where(odd, block[:, C:], block[:, :C])

    copies[0].wait()
    copies[1].wait()
    first = jnp.concatenate([columns(0), columns(1)], axis=1).astype(BF)
    for to in range(Z):
        early[to] = first
    first_out = pltpu.make_async_copy(early, out.at[:, 0:48, :], gone.at[0])
    first_out.start()
    at, to = rows((HEAD_DIM, C)), lanes((HEAD_DIM, C))
    wanted = (to // 16) * 32 + to % 16 + jnp.where(odd, 16, 0)
    chosen = jnp.where(at == wanted, 1.0, 0.0).astype(BF)
    copies[2].wait()
    value = dot(blocks[2], chosen)
    copies[3].wait()
    copies[4].wait()
    head = lax.dot_general(left[...], right[...], NT, preferred_element_type=F32)
    second = jnp.concatenate([value[0:16], value[16:32]], axis=1).astype(BF)
    third = jnp.concatenate([value[32:48], head], axis=1).astype(BF)
    for to in range(Z):
        late[to, 0:16, :] = second
        late[to, 16:32, :] = third
    second_out = pltpu.make_async_copy(late, out.at[:, 48:80, :], gone.at[1])
    second_out.start()
    first_out.wait()
    second_out.wait()


def coefficients(timesteps):
    z, _, _ = place()
    lane = lanes((8, 128))
    moments = jnp.zeros((8, 128), F32)
    for at in range(STEPS + 1):
        moments = jnp.where(lane == at, timesteps[at].astype(F32), moments)
    angle = (moments / 1000.0 + 0.008) / 1.008 * (math.pi / 2)
    abar = jnp.cos(angle) ** 2
    after = pltpu.roll(abar, 127, 1)
    keep = jnp.sqrt(after / abar)
    noise = jnp.sqrt(1.0 - after) - keep * jnp.sqrt(1.0 - abar)
    less = keep - 1.0
    row = rows((8, 128))
    chosen = jnp.where(
        row < 2,
        jnp.where(lane == 2 * z + row, less, 0.0),
        jnp.where(row < 4, jnp.where(lane == 2 * z + row - 2, noise, 0.0), jnp.where(lane < 2 * z, less, 0.0)),
    )
    return jnp.broadcast_to(jnp.sum(chosen, axis=1, keepdims=True), (8, 128))


def make_tables(timesteps, w_in, w_out, modulation, start, left, table, coef, mine, direct, own):
    coef[...] = coefficients(timesteps)
    w = w_in[...].astype(F32)
    centred = w - jnp.mean(w, axis=1, keepdims=True)
    shift = modulation[:, 0:D].astype(F32)
    gain = modulation[:, D : 2 * D].astype(F32)
    left[0:C, :] = (centred * (1.0 + gain)).astype(BF)
    left[C : C + 16, :] = jnp.where(rows((16, D)) == 0, shift, 0.0).astype(BF)
    gram = lax.dot_general(centred, centred, NT, precision=BEST, preferred_element_type=F32) / D
    embed = lax.dot_general(w_in[...], w_out[...], NT, preferred_element_type=F32)
    pad = jnp.zeros((C, C), F32)
    gram = jnp.concatenate([gram, pad], axis=1)
    embed = jnp.concatenate([pad, embed], axis=1)
    for at, piece in enumerate(split_of(gram, 3) + split_of(embed, 2)):
        table[at, 0:C, :] = piece
        table[at, C : 2 * C, :] = jnp.zeros((C, 2 * C), BF)
    _, core, _ = place()
    x = unpack(packed_start(start, core).astype(BF).astype(F32))
    mine[...] = normalized(x, table)
    own[...] = pack(mine[...]).astype(BF)
    direct[...] = direct_of(x, table)


def make_heads(both, left, own, out, qk, vw):
    _, _, seq = place()
    for rank, z in enumerate(Z_FIRST):
        for parity in range(2):
            at = (z * 2 + parity) * ROWS
            qk[at : at + 48, :] = both[parity, rank, 0:48, :]
            values = both[parity, rank, 48:64, :]
            vw[at : at + 16, :] = values
            vw[at + 16 : at + 32, :] = pltpu.roll(values.astype(F32), C, 1).astype(BF)
            vw[at + 32 : at + 48, :] = both[parity, rank, 64:80, :]
    first = dot(left[...], qk[...])
    value = dot(left[...], vw[...])[:, :C]
    query, key = first[:, :C], first[:, C:]
    ranks = [sum(jnp.where(seq // 2 == z // 2, Z_FIRST.index(z), 0) for z in range(late, Z, 2)) for late in range(2)]
    head = [both[group % 2, ranks[group // 2], 64:80, C:].astype(F32) for group in range(4)]
    head = jnp.concatenate(head, axis=0)
    a = fine_dot(query, key, NT) * SCALE
    b = fine_dot(value, head, (((1,), (0,)), ((), ())))
    bias = fine_dot(key[C : C + 8], query, NT) * SCALE
    bias = jnp.concatenate([bias, jnp.zeros((8, 128 - bias.shape[1]), F32)], axis=1)[0:1]
    main = jnp.concatenate([a[:, :C], b], axis=1)
    main = jnp.where(rows(main.shape) == C + 1, bias, main).astype(BF)
    x = own[...]
    for to in range(PEERS // 2):
        out[to, 0:80, :] = main
        out[to, 80:96, :] = x


def normalized(x, table):
    exact = x.astype(BF)
    y = dot(exact, table[0]) + dot(exact, table[1]) + dot(exact, table[2])
    spread = jnp.maximum(jnp.sum(x * y, axis=1, keepdims=True), 0.0)
    return jnp.where(lanes(x.shape) == C, 1.0, x * lax.rsqrt(spread + 1e-06))


def direct_of(x, table):
    exact = x.astype(BF)
    return pack_high(dot(exact, table[3]) + dot(exact, table[4]))


def ask(step, heads, mine, query):
    short = mine.astype(BF)
    lane = lanes(mine.shape)
    for head in range(HEADS):
        both = heads[step * HEADS + head]
        grown = dot(short, both)
        constant = jnp.sum(mine * both[C : C + 16].astype(F32)[1:2], axis=1, keepdims=True)
        grown = jnp.where(lane < C, grown, jnp.where(lane == C, constant, 0.0)).astype(BF)
        query[step, head * 32 : (head + 1) * 32, :] = grown


def attend(heads, query, direct, keys, weight, mix):
    both = range(2)
    scores = [lax.dot_general(query[step], keys[step][...], NT, preferred_element_type=F32) for step in both]
    tops = [jnp.max(score, axis=1, keepdims=True) for score in scores]
    for step in both:
        weight[step] = jnp.exp2(scores[step] - tops[step]).astype(BF)
    mixed = [dot(weight[step], keys[step][...]) for step in both]
    for step in both:
        shares = (mixed[step] * (1.0 / mixed[step][:, C : C + 1])).astype(BF)
        for head in range(HEADS):
            mix[step, :, head * 128 : (head + 1) * 128] = shares[head * 32 : (head + 1) * 32]
    eps = []
    for step in both:
        blocks = heads[step * HEADS : (step + 1) * HEADS].reshape(HEADS * 128, 128)
        eps.append(pack_high(dot(mix[step], blocks)) + direct[step])
    return eps


def work_space():
    return (
        pltpu.VMEM((2, TOKENS, 128), BF),
        pltpu.VMEM((2, HEADS * 32, TOKENS), BF),
        pltpu.VMEM((2, 32, HEADS * 128), BF),
    )


def first_sweep(coef, got, mine, direct, heads, first_eps, out, query, key, weight, mix):
    for at in range(2 * HEADS):
        step, first = at // HEADS, SEQ_ORDER.index(2 * (at % HEADS))
        second = SEQ_ORDER.index(2 * (at % HEADS) + 1)
        both = got[step, first, 0:80, :].astype(F32) + got[step, second, 0:80, :].astype(F32)
        heads[at, 0:80, :] = both.astype(BF)
        heads[at, 80:128, :] = jnp.zeros((48, 128), BF)
    everything = got[:, :, 80:96, :].astype(F32).reshape(PEERS * 16, 128)
    key[0] = unpack(everything, 1.0).astype(BF)
    for step in range(2):
        ask(step, heads, mine[...], query)
    eps = attend(heads, query, (direct[...], direct[...]), (key.at[0], key.at[0]), weight, mix)
    first_eps[...] = eps[0]
    both = (coef[2:3] * eps[0] + coef[3:4] * eps[1]).astype(BF)
    for to in range(Z):
        out[to] = both


def packed_start(start, core):
    x = start[pl.ds(pl.multiple_of(core * 32, 32), 32), :]
    return jnp.concatenate([x[:16], x[16:]], axis=1)


def below(got, z):
    total = jnp.zeros((16, 128), F32)
    for rank, at in enumerate(Z_ORDER):
        total = total + jnp.where(at < z, got[rank].astype(F32), 0.0)
    return total


def first_prefix(coef, got, start, first_eps, table, latents, mine, out):
    z, core, _ = place()
    x = packed_start(start, core)
    even = x + coef[4:5] * x + below(got, z)
    odd = even + coef[0:1] * x + coef[2:3] * first_eps[...]
    latents[0] = even
    latents[1] = odd
    sent = []
    for step, x in enumerate((even, odd)):
        mine[step] = normalized(unpack(x.astype(BF).astype(F32)), table)
        sent.append(pack(mine[step]).astype(BF))
    for to in range(PEERS):
        out[to, 0:16, :] = sent[0]
        out[to, 16:32, :] = sent[1]


def second_sweep(coef, got, latents, mine, table, heads, term, out, query, key, weight, mix):
    direct = []
    for step in range(2):
        everything = got[:, 16 * step : 16 * step + 16, :].astype(F32).reshape(PEERS * 16, 128)
        key[step] = unpack(everything, 1.0).astype(BF)
        direct.append(direct_of(unpack(latents[step].astype(BF).astype(F32)), table))
        ask(step, heads, mine[step], query)
    eps = attend(heads, query, direct, (key.at[0], key.at[1]), weight, mix)
    terms = [coef[step : step + 1] * latents[step] + coef[2 + step : 3 + step] * eps[step] for step in range(2)]
    term[...] = terms[0]
    both = (terms[0] + terms[1]).astype(BF)
    for to in range(Z):
        out[to] = both


def second_prefix(got, start, latents, term, out):
    z, core, _ = place()
    even = packed_start(start, core) + below(got, z)
    fresh = (even, even + term[...])
    for step in range(2):
        change = fresh[step] - latents[step]
        squared = change * change
        out[step, 0:16, :] = fresh[step]
        out[step, 16:24, :] = squared[:8] + squared[8:]


def send_errors(halves, out):
    _, core, _ = place()
    squared = halves[0, core, 16:24, :] + halves[1, core, 16:24, :]
    for to in range(PEERS // 2):
        out[to] = squared


def finish(got, halves, window, errors):
    _, core, _ = place()
    for half in range(2):
        packed = halves[half, core, 0:16, :]
        window[0, half * 32 : half * 32 + 16, :] = packed[:, :C]
        window[0, half * 32 + 16 : half * 32 + 32, :] = packed[:, C:]
    total = got[0]
    for at in range(1, PEERS // 2):
        total = total + got[at]
    total = jnp.sum(total, axis=(0, 1), keepdims=True)
    errors[...] = jnp.sqrt(total / (TOKENS * C) + 1e-06)


def body(start, timesteps, modulation, w_in, w_qkv, w_o, w_out):
    sent = call(
        send_weights,
        shape((Z, 80, 128), BF),
        (w_qkv, w_o, w_out.T),
        scratch=(
            pltpu.VMEM((3, ROWS, HEAD_DIM), BF),
            pltpu.VMEM((16, D), BF),
            pltpu.VMEM((C, D), BF),
            pltpu.VMEM((Z, 48, 128), BF),
            pltpu.VMEM((Z, 32, 128), BF),
            pltpu.SemaphoreType.DMA((5,)),
            pltpu.SemaphoreType.DMA((2,)),
        ),
        far=(0, 1, 2),
        grant=62,
        out_far=True,
    )
    got = lax.all_to_all(sent, "z", 0, 0, axis_index_groups=[Z_FIRST], tiled=True)
    left, table, coef, mine, direct, own = call(
        make_tables,
        (
            shape((80, D), BF),
            shape((5, 128, 128), BF),
            shape((8, 128), F32),
            shape((32, 128), F32),
            shape((16, 128), F32),
            shape((16, 128), BF),
        ),
        (timesteps, w_in, w_out.T, modulation, start),
        smem=(0,),
        flops=10**9,
    )
    sent = call(
        make_heads,
        shape((PEERS // 2, 96, 128), BF),
        (lax.all_gather(got, "core"), left, own),
        scratch=(pltpu.VMEM((D, 128), BF), pltpu.VMEM((D, 128), BF)),
    )
    got = lax.all_gather(exchange(sent, ("y", "x")), "core")
    heads, first_eps, sent = call(
        first_sweep,
        (shape((2 * HEADS, 128, 128), BF), shape((16, 128), F32), shape((Z, 16, 128), BF)),
        (coef, got, mine, direct),
        scratch=(pltpu.VMEM((2, HEADS * 32, 128), BF), *work_space()),
    )
    got = exchange(sent, "z")
    latents, mine, sent = call(
        first_prefix,
        (shape((2, 16, 128), F32), shape((2, 32, 128), F32), shape((PEERS, 32, 128), BF)),
        (coef, got, start, first_eps, table),
    )
    got = exchange(sent, FLAT)
    term, sent = call(
        second_sweep,
        (shape((16, 128), F32), shape((Z, 16, 128), BF)),
        (coef, got, latents, mine, table, heads),
        scratch=(pltpu.VMEM((2, HEADS * 32, 128), BF), *work_space()),
    )
    got = exchange(sent, "z")
    fresh = call(second_prefix, shape((2, 24, 128), F32), (got, start, latents, term))
    halves = lax.all_gather(fresh, "core")
    sent = call(send_errors, shape((PEERS // 2, 8, 128), F32), (halves,))
    got = exchange(sent, ("y", "x"))
    window, errors = call(finish, (shape((1, 64, C), F32), shape((1, 1), F32)), (got, halves))
    return window, errors.reshape(1)


def solution(mesh):
    fine = Mesh(mesh.devices.reshape(Z, 2, 4, 4), ("z", "core", "y", "x"))
    step, seq = ("z", "core"), ("y", "x")
    return jax.shard_map(
        body,
        mesh=fine,
        in_specs=(P(seq, None), P(), P(step, None), P(), P(step, None), P(step, None), P()),
        out_specs=(P(step, seq, None), P(step)),
        check_vma=False,
    )
```
